32 devices in a mesh: cam: 4 (over x, core), clip: 8 (over z, y).
Axes of the slice: x: 2, y: 2, z: 4, core: 2. Of those that a mesh axis runs over, the one named last changes fastest.
Arguments:
- tokens: bfloat16 [16, 4, 256, 1024], P('clip', 'cam'), may hold values from -6 to 6
- w_query: bfloat16 [1024, 1024], replicated, may hold values from -0.1875 to 0.1875
- w_key: bfloat16 [1024, 1024], replicated, may hold values from -0.1875 to 0.1875
- w_value: bfloat16 [1024, 1024], replicated, may hold values from -0.1875 to 0.1875
- w_proj: bfloat16 [1024, 256], replicated, may hold values from -0.1875 to 0.1875
- prototypes: bfloat16 [256, 65536], P(None, ('cam', 'clip')), may hold values from -6 to 6
Outputs:
- codes: float32 [16, 65536], P(None, ('cam', 'clip'))
- prototype_gradient: float32 [256, 65536], P(None, ('cam', 'clip'))
- grad_proj: float32 [1024, 256], P('clip')
- grad_value: float32 [1024, 1024], P('clip', 'cam')
The draws below stay inside these ranges and needn't reach their ends.
All inputs are finite; a program needn't handle non-finite values.
Results may differ from the reference program's by a relative error of at most 0.015.
Values may be sent and summed in bfloat16 or wider, within the bound.
No kernel may reach another device: no remote copies, remote signals or barrier semaphores. Data moves between devices by JAX's collectives and lax.ppermute only.
A program may use at most 128 MiB of HBM per device.

```python
import jax
import jax.numpy as jnp
from jax import lax

D = 1024
HD = 64
BOT = 256
PROTOS = 65536
TOK = 256
ITERS = 3
H = 16
CAMS = 4
CLIPS = 16
N_CAM = 4


def draw_prototypes(key, part):
    groups = 16
    key_dirs, key_noise, key_member, key_sign, key_scale = jax.random.split(jax.random.fold_in(key, 7), 5)
    directions = jnp.clip(jax.random.normal(key_dirs, (BOT, groups), jnp.float32), -4.0, 4.0)
    noise = 0.5 * jnp.clip(jax.random.normal(key_noise, (BOT, PROTOS), jnp.float32), -4.0, 4.0)
    members = jax.random.randint(key_member, (PROTOS,), 0, groups)
    signs = 2.0 * jax.random.randint(key_sign, (PROTOS,), 0, 2).astype(jnp.float32) - 1.0
    scales = jax.random.uniform(key_scale, (PROTOS,), jnp.float32, 0.5, 1.0)
    picked = jnp.take(directions, members, axis=1)
    values = (picked * signs[None, :] + noise) * scales[None, :]
    return values.astype(jnp.bfloat16)


def level_of(stream_key, extent, shards, least, largest):
    gain = 1.0
    for axis_at, shards_of in shards:
        heights = jax.random.uniform(jax.random.fold_in(jax.random.fold_in(stream_key, 6), axis_at), (shards_of,), jnp.float32, least / len(shards), largest / len(shards))
        gain = gain * jnp.repeat(jnp.exp(heights), extent[axis_at] // shards_of).reshape((-1,) + (1,) * (len(extent) - 1 - axis_at))
    return gain


def normal_values(key, shape, spread, most, cuts=(), kind=jnp.bfloat16):
    entries = spread * jax.random.normal(key, shape, jnp.float32)
    if cuts:
        entries = entries * level_of(key, shape, cuts, -0.22, 0.18)
    return jnp.clip(entries, -most, most).astype(kind)


def setup_inputs(seed: int = 0) -> dict:
    splits = jax.random.split(jax.random.key(seed), 7)
    return {
        "tokens": normal_values(splits[0], (CLIPS, CAMS, TOK, D), 1.0, 6.0, ((0, 8), (1, 4))),
        "w_query": normal_values(splits[1], (D, D), D ** -0.5, 0.1875),
        "w_key": normal_values(splits[2], (D, D), D ** -0.5, 0.1875),
        "w_value": normal_values(splits[3], (D, D), D ** -0.5, 0.1875),
        "w_proj": normal_values(splits[4], (D, BOT), D ** -0.5, 0.1875),
        "prototypes": draw_prototypes(jax.random.fold_in(splits[6], 71), 0),
    }


SINK_EPS = 0.05
SOFTMAX_TEMP = 0.1
NORM_EPS = 1e-06

def column_averages(query_vectors, key_rows):
    total = key_rows.shape[0]

    def per_head(index):
        query_head = lax.dynamic_slice_in_dim(query_vectors, index * HD, HD, 1).astype(jnp.float32)
        key_head = lax.dynamic_slice_in_dim(key_rows, index * HD, HD, 1).astype(jnp.float32)
        scores = jnp.dot(query_head, key_head.T, precision=lax.Precision.HIGHEST) * HD ** (-0.5)
        exponent_values = jnp.exp(scores)
        probs = exponent_values / lax.optimization_barrier(jnp.sum(exponent_values, axis=1, keepdims=True))
        return lax.optimization_barrier(jnp.sum(probs, axis=0)) / total
    return lax.map(per_head, jnp.arange(H, dtype=jnp.int32))

def reference(tokens, w_query, w_key, w_value, w_proj, prototypes):
    value_heads = w_value.astype(jnp.float32).reshape(D, H, HD)

    def pool_clip(clip_rows):
        flat = clip_rows.reshape(N_CAM * TOK, D)
        query_vectors = jnp.dot(flat, w_query, preferred_element_type=jnp.float32).astype(jnp.bfloat16)
        key_rows = jnp.dot(flat, w_key, preferred_element_type=jnp.float32).astype(jnp.bfloat16)
        weights = column_averages(query_vectors, key_rows).astype(jnp.bfloat16).reshape(H, N_CAM, TOK)
        mixture = jnp.einsum('hcj,cjd->chd', weights.astype(jnp.float32), clip_rows.astype(jnp.float32), precision=lax.Precision.HIGHEST).astype(jnp.bfloat16)
        head_out = jnp.einsum('chd,dhe->che', mixture.astype(jnp.float32), value_heads, precision=lax.Precision.HIGHEST)
        return (lax.optimization_barrier(jnp.sum(head_out, axis=0)).reshape(D).astype(jnp.bfloat16), mixture)
    pooled, mixtures = lax.map(pool_clip, tokens)
    embed = jnp.dot(pooled, w_proj, preferred_element_type=jnp.float32)
    embed_norm = jnp.sqrt(lax.optimization_barrier(jnp.sum(embed * embed, axis=1, keepdims=True)) + NORM_EPS)
    unit = embed / embed_norm
    unit_b = unit.astype(jnp.bfloat16)
    proto_f = prototypes.astype(jnp.float32)
    column_norm = jnp.sqrt(lax.optimization_barrier(jnp.sum(proto_f * proto_f, axis=0, keepdims=True)) + NORM_EPS)
    unit_proto = proto_f / column_norm
    proto_b = unit_proto.astype(jnp.bfloat16)
    logit_scores = jnp.dot(unit_b, proto_b, preferred_element_type=jnp.float32)
    assign = jnp.exp(logit_scores / SINK_EPS)
    for step in range(ITERS):
        assign = assign / lax.optimization_barrier(jnp.sum(assign, axis=0, keepdims=True))
        assign = assign / lax.optimization_barrier(jnp.sum(assign, axis=1, keepdims=True))
    exponent_values = jnp.exp(logit_scores / SOFTMAX_TEMP)
    prob = exponent_values / lax.optimization_barrier(jnp.sum(exponent_values, axis=1, keepdims=True))
    grad_logits = (PROTOS * (prob - assign)).astype(jnp.bfloat16)
    codes = PROTOS * assign
    grad_unit = jnp.dot(grad_logits, proto_b.T, preferred_element_type=jnp.float32)
    grad_embed = (grad_unit - unit * lax.optimization_barrier(jnp.sum(unit * grad_unit, axis=1, keepdims=True))) / embed_norm
    grad_embed_b = grad_embed.astype(jnp.bfloat16)
    grad_proj = jnp.dot(pooled.T, grad_embed_b, preferred_element_type=jnp.float32)
    grad_pooled = jnp.dot(grad_embed_b, w_proj.T, preferred_element_type=jnp.float32).astype(jnp.bfloat16)
    grad_value = jnp.einsum('bchd,bhe->dhe', mixtures.astype(jnp.float32), grad_pooled.astype(jnp.float32).reshape(CLIPS, H, HD), precision=lax.Precision.HIGHEST).reshape(D, D)
    grad_unit_proto = jnp.dot(unit_b.T, grad_logits, preferred_element_type=jnp.float32)
    prototype_gradient = (grad_unit_proto - unit_proto * lax.optimization_barrier(jnp.sum(unit_proto * grad_unit_proto, axis=0, keepdims=True))) / column_norm
    return (codes, prototype_gradient, grad_proj, grad_value)
```

```python
import functools

import jax
import jax.numpy as jnp
from jax import lax
from jax.experimental import pallas as pl
from jax.experimental.pallas import tpu as pltpu
from jax.sharding import PartitionSpec as P

HD = 64
SINK_EPS = 0.05
SOFTMAX_TEMP = 0.1
NORM_EPS = 1e-06
LANES = 128
ALL = ("cam", "clip")
F32 = jnp.float32
BF16 = jnp.bfloat16


def pool_kernel(blocks, *refs):
    x_refs = refs[:blocks]
    wq_ref, wk_ref, wv_ref, pooled_ref, mix_ref, q_s, kt_s, w_s = refs[blocks:]
    tok = x_refs[0].shape[0]
    total = tok * blocks
    heads = mix_ref.shape[0]
    cols = heads * HD
    for c in range(blocks):
        x = x_refs[c][...]
        rows = slice(c * tok, (c + 1) * tok)
        q = jnp.dot(x, wq_ref[...], preferred_element_type=F32).astype(BF16)
        q_s[rows, :] = q * BF16(HD**-0.5)
        k = jnp.dot(x, wk_ref[...], preferred_element_type=F32).astype(BF16)
        kt_s[:, rows] = k.T
    lane = lax.broadcasted_iota(jnp.int32, (total, LANES), 1)

    @pl.loop(0, cols // LANES)
    def _(p):
        here = pl.ds(pl.multiple_of(p * LANES, LANES), LANES)
        q_pair = q_s[:, here]
        k_pair = kt_s[here, :]
        for e in range(LANES // HD):
            q_head = jnp.where(lane // HD == e, q_pair, BF16(0))
            s = jnp.dot(q_head, k_pair, preferred_element_type=F32)
            a = jnp.exp(s)
            a = a * (1.0 / jnp.sum(a, axis=1, keepdims=True))
            w = jnp.sum(a, axis=0, keepdims=True) * (1.0 / total)
            w_s[pl.ds(p * (LANES // HD) + e, 1), :] = w

    weights = w_s[...].astype(BF16)
    mixtures = []
    mix_sum = jnp.zeros(mix_ref.shape, F32)
    for c in range(blocks):
        m = jnp.dot(weights[:, c * tok : (c + 1) * tok], x_refs[c][...], preferred_element_type=F32)
        mixtures.append(m.astype(BF16).astype(F32))
        mix_sum = mix_sum + mixtures[-1]
    mix_ref[...] = mix_sum
    stacked = jnp.concatenate(mixtures, axis=0).astype(BF16)
    out = jnp.dot(stacked, wv_ref[...], preferred_element_type=F32)
    row_head = lax.broadcasted_iota(jnp.int32, out.shape, 0) % heads
    col_head = lax.broadcasted_iota(jnp.int32, out.shape, 1) // HD
    pooled_ref[...] = jnp.sum(jnp.where(row_head == col_head, out, 0.0), axis=0, keepdims=True)


def pool(blocks, wq, wk, wv):
    tok, d = blocks[0].shape
    cols = wq.shape[1]
    heads = cols // HD
    total = tok * len(blocks)
    return pl.pallas_call(
        functools.partial(pool_kernel, len(blocks)),
        out_shape=(
            jax.ShapeDtypeStruct((1, cols), F32),
            jax.ShapeDtypeStruct((heads, d), F32),
        ),
        in_specs=[pl.BlockSpec(memory_space=pltpu.VMEM)] * (len(blocks) + 3),
        out_specs=[pl.BlockSpec(memory_space=pltpu.VMEM)] * 2,
        scratch_shapes=[
            pltpu.VMEM((total, cols), BF16),
            pltpu.VMEM((cols, total), BF16),
            pltpu.VMEM((heads, total), F32),
        ],
        compiler_params=pltpu.CompilerParams(vmem_limit_bytes=52 * 2**20),
        cost_estimate=pl.CostEstimate(
            flops=2 * total * d * cols * 2 + 2 * total * total * cols,
            bytes_accessed=total * d * 2 + 3 * d * cols * 2,
            transcendentals=heads * total * total,
        ),
    )(*blocks, wq, wk, wv)


def gather_clip(tokens, n_cam):
    clips = tokens.shape[0]
    ranks = n_cam // clips
    group = lax.axis_index("cam") // ranks
    mine = lax.dynamic_index_in_dim(tokens, group, 0, keepdims=False)
    held = [mine]
    for s in range(1, clips):
        other = lax.dynamic_index_in_dim(tokens, (group + s) % clips, 0, keepdims=False)
        perm = [(i, ((i // ranks + s) % clips) * ranks + i % ranks) for i in range(n_cam)]
        held.append(lax.ppermute(other, "cam", perm))
    blocks = list(held)
    for t in range(1, ranks):
        perm = [(i, (i // ranks) * ranks + (i % ranks + t) % ranks) for i in range(n_cam)]
        blocks.extend(lax.ppermute(b, "cam", perm) for b in held)
    return blocks


def exchange(message):
    devices, length = message.shape
    padded = -(-length // LANES) * LANES
    message = jnp.pad(message, ((0, 0), (0, padded - length)))
    message = message.reshape(devices, padded // LANES, LANES)
    out = lax.all_to_all(message, ALL, split_axis=0, concat_axis=0, tiled=True)
    return out.reshape(devices, padded)[:, :length]


def tell_all(values, devices):
    return exchange(jnp.broadcast_to(values[None], (devices,) + values.shape))


def local(tokens, w_query, w_key, w_value, w_proj, prototypes):
    clips, _, tok, d = tokens.shape
    n_cam, n_clip = lax.axis_size("cam"), lax.axis_size("clip")
    devices = n_cam * n_clip
    ranks = n_cam // clips
    batch = clips * n_clip
    cols = d // ranks
    heads = cols // HD
    heads_here = heads // clips
    share = d // n_clip
    bottleneck = w_proj.shape[1]
    cam, clip = lax.axis_index("cam"), lax.axis_index("clip")
    rank = cam % ranks

    with jax.named_scope("prototypes"):
        proto_f = prototypes.astype(F32)
        column_norm = jnp.sqrt(jnp.sum(proto_f * proto_f, axis=0, keepdims=True) + NORM_EPS)
        unit_proto = proto_f / column_norm
        proto_b = unit_proto.astype(BF16)

    with jax.named_scope("pooling"):
        wq, wk, wv = (
            lax.dynamic_slice_in_dim(w, rank * cols, cols, 1) for w in (w_query, w_key, w_value)
        )
        blocks = gather_clip(tokens.reshape(clips, tok, d), n_cam)
        pooled, mix = pool(blocks, wq, wk, wv)

    with jax.named_scope("features_of_all_clips"):
        pooled_to = jnp.broadcast_to(pooled.astype(BF16), (devices, cols))
        mix_to = mix.astype(BF16).reshape(clips, heads_here, n_clip, share).transpose(0, 2, 1, 3)
        mix_to = mix_to.reshape(clips * n_clip, heads_here * share)
        mix_to = jnp.tile(mix_to, (ranks, 1))
        came = exchange(jnp.concatenate([pooled_to, mix_to], axis=1))
        came = came.reshape(clips, ranks, n_clip, cols + heads_here * share)
        pooled = came[..., :cols].transpose(2, 0, 1, 3).reshape(batch, d)
        mixed = lax.dynamic_index_in_dim(came[..., cols:], cam // clips, 1, keepdims=False)
        mixed = mixed.transpose(1, 0, 2).reshape(batch, heads_here, share)

    with jax.named_scope("logits"):
        embed = jnp.dot(pooled, w_proj, preferred_element_type=F32)
        embed_norm = jnp.sqrt(jnp.sum(embed * embed, axis=1, keepdims=True) + NORM_EPS)
        unit = embed / embed_norm
        unit_b = unit.astype(BF16)
        logits = jnp.dot(unit_b, proto_b, preferred_element_type=F32)
        exponents = jnp.exp(logits / SOFTMAX_TEMP)
        assign = jnp.exp(logits / SINK_EPS)
        prob_part = lax.dot_general(
            exponents.astype(BF16), proto_b, (((1,), (1,)), ((), ())), preferred_element_type=F32
        )
        prob_sum = jnp.sum(exponents, axis=1)

    with jax.named_scope("row_total_1"):
        assign = assign / jnp.sum(assign, axis=0, keepdims=True)
        piece = batch * bottleneck // devices
        sums = jnp.concatenate([jnp.sum(assign, axis=1), prob_sum])
        came = exchange(
            jnp.concatenate(
                [
                    prob_part.reshape(devices, piece),
                    jnp.broadcast_to(sums[None], (devices, 2 * batch)),
                ],
                axis=1,
            )
        )
        came = jnp.sum(came, axis=0)
        prob_piece, row_total, prob_total = (
            came[:piece],
            came[piece : piece + batch],
            came[piece + batch :],
        )
        assign = assign / row_total[:, None]

    with jax.named_scope("row_total_2"):
        assign = assign / jnp.sum(assign, axis=0, keepdims=True)
        came = tell_all(jnp.concatenate([prob_piece, jnp.sum(assign, axis=1)]), devices)
        prob_grad = came[:, :piece].reshape(batch, bottleneck)
        assign = assign / jnp.sum(came[:, piece:], axis=0)[:, None]

    with jax.named_scope("row_total_3"):
        assign = assign / jnp.sum(assign, axis=0, keepdims=True)
        assign_part = lax.dot_general(
            assign.astype(BF16), proto_b, (((1,), (1,)), ((), ())), preferred_element_type=F32
        )
        rest = jnp.sum(assign, axis=1)
        digits = []
        for _ in range(3):
            digits.append(lax.reduce_precision(rest, 8, 7))
            rest = rest - digits[-1]
        message = jnp.concatenate([assign_part.reshape(-1)] + digits).astype(BF16)
        came = jnp.sum(tell_all(message, devices).astype(F32), axis=0)
        assign_grad = came[: batch * bottleneck].reshape(batch, bottleneck)
        row_total = jnp.sum(came[batch * bottleneck :].reshape(3, batch), axis=0)
        assign = assign / row_total[:, None]

    protos = prototypes.shape[1] * devices
    with jax.named_scope("outputs"):
        grad_logits = (protos * (exponents / prob_total[:, None] - assign)).astype(BF16)
        codes = protos * assign
        grad_unit_proto = lax.dot_general(
            unit_b, grad_logits, (((0,), (0,)), ((), ())), preferred_element_type=F32
        )
        prototype_gradient = (
            grad_unit_proto
            - unit_proto * jnp.sum(unit_proto * grad_unit_proto, axis=0, keepdims=True)
        ) / column_norm
        grad_unit = protos * (prob_grad / prob_total[:, None] - assign_grad / row_total[:, None])
        grad_embed = (
            grad_unit - unit * jnp.sum(unit * grad_unit, axis=1, keepdims=True)
        ) / embed_norm
        grad_embed_b = grad_embed.astype(BF16)
        pooled_share = lax.dynamic_slice_in_dim(pooled, clip * share, share, 1)
        grad_proj = lax.dot_general(
            pooled_share, grad_embed_b, (((0,), (0,)), ((), ())), preferred_element_type=F32
        )
        width = heads_here * HD
        proj_rows = lax.dynamic_slice_in_dim(w_proj, cam * width, width, 0)
        grad_pooled = lax.dot_general(
            grad_embed_b, proj_rows, (((1,), (1,)), ((), ())), preferred_element_type=F32
        ).astype(BF16)
        grad_value = jnp.einsum(
            "bhd,bhe->dhe",
            mixed,
            grad_pooled.reshape(batch, heads_here, HD),
            preferred_element_type=F32,
        ).reshape(share, width)
    return (codes, prototype_gradient, grad_proj, grad_value)


def solution(mesh):
    in_specs = (P("clip", "cam", None, None), P(), P(), P(), P(), P(None, ALL))
    out_specs = (P(None, ALL), P(None, ALL), P("clip", None), P("clip", "cam"))
    return jax.shard_map(local, mesh=mesh, in_specs=in_specs, out_specs=out_specs, check_vma=False)
```

```python
import functools

import jax
import jax.numpy as jnp
from jax import lax
from jax.experimental import pallas as pl
from jax.experimental.pallas import tpu as pltpu
from jax.sharding import PartitionSpec as P

HD = 64
SINK_EPS = 0.05
SOFTMAX_TEMP = 0.1
NORM_EPS = 1e-06
LANES = 128
DIGITS = 3
CHUNKS = 2
ALL = ("cam", "clip")
F32 = jnp.float32
BF16 = jnp.bfloat16
TRANSPOSED = (((1,), (1,)), ((), ()))
OUTER = (((0,), (0,)), ((), ()))
WHOLE = pl.BlockSpec(memory_space=pltpu.VMEM)
SCALARS = pl.BlockSpec(memory_space=pltpu.SMEM)


def call(kernel, outs, ins, flops, extra=0, scratch=(), grid=None, out_specs=None, in_specs=None):
    moved = sum(a.size * a.dtype.itemsize for a in ins)
    return pl.pallas_call(
        kernel,
        out_shape=tuple(jax.ShapeDtypeStruct(*o) for o in outs),
        in_specs=in_specs or [WHOLE] * len(ins),
        out_specs=out_specs or [WHOLE] * len(outs),
        scratch_shapes=list(scratch),
        grid=grid or (),
        compiler_params=pltpu.CompilerParams(vmem_limit_bytes=52 * 2**20),
        cost_estimate=pl.CostEstimate(flops=flops, bytes_accessed=moved, transcendentals=extra),
    )(*ins)


def project(x, wq, wk, wv):
    q = jnp.dot(x, wq, preferred_element_type=F32).astype(BF16) * BF16(HD**-0.5)
    kt = jnp.dot(x, wk, preferred_element_type=F32).astype(BF16).T
    v = jnp.dot(x, wv, preferred_element_type=F32).astype(BF16)
    return q, kt, v


def project_kernel(blocks, *refs):
    wq, wk, wv = refs[blocks : blocks + 3]
    q_ref, kt_ref, v_ref = refs[blocks + 3 :]
    at = 0
    for x_ref in refs[:blocks]:
        rows = slice(at, at + x_ref.shape[0])
        at += x_ref.shape[0]
        q_ref[rows, :], kt_ref[:, rows], v_ref[rows, :] = project(
            x_ref[...], wq[...], wk[...], wv[...]
        )


def project_blocks(blocks, weights):
    d, cols = weights[0].shape
    rows = sum(b.shape[0] for b in blocks)
    return call(
        functools.partial(project_kernel, len(blocks)),
        [((rows, cols), BF16), ((cols, rows), BF16), ((rows, cols), BF16)],
        [*blocks, *weights],
        2 * rows * d * cols * 3,
    )


def pool_kernel(parts, late, *refs):
    early = [refs[3 * i : 3 * i + 3] for i in range(parts)]
    refs = refs[3 * parts :]
    x_refs, (wq, wk, wv, wp) = refs[:late], refs[late : late + 4]
    weight_ref, pooled_ref, embed_ref, q_s, kt_s, v_s, w_s = refs[late + 4 :]
    project_kernel(late, *x_refs, wq, wk, wv, q_s, kt_s, v_s)
    pieces = early + [(q_s, kt_s, v_s)]
    heads, total = w_s.shape
    cols = heads * HD
    lane = lax.broadcasted_iota(jnp.int32, (total, LANES), 1)

    @pl.loop(0, cols // LANES)
    def _(p):
        here = pl.ds(pl.multiple_of(p * LANES, LANES), LANES)
        q_pair = jnp.concatenate([q[:, here] for q, _, _ in pieces], axis=0)
        k_pair = jnp.concatenate([kt[here, :] for _, kt, _ in pieces], axis=1)
        for e in range(LANES // HD):
            q_head = jnp.where(lane // HD == e, q_pair, BF16(0))
            a = jnp.exp(jnp.dot(q_head, k_pair, preferred_element_type=F32))
            a = a * (1.0 / jnp.sum(a, axis=1, keepdims=True))
            w = jnp.sum(a, axis=0, keepdims=True) * (1.0 / total)
            w_s[pl.ds(p * (LANES // HD) + e, 1), :] = w

    weights = w_s[...].astype(BF16)
    weight_ref[...] = weights
    out, at = jnp.zeros((heads, cols), F32), 0
    for _, _, v in pieces:
        rows = slice(at, at + v.shape[0])
        at += v.shape[0]
        out = out + jnp.dot(weights[:, rows], v[...], preferred_element_type=F32)
    row_head = lax.broadcasted_iota(jnp.int32, out.shape, 0)
    col_head = lax.broadcasted_iota(jnp.int32, out.shape, 1) // HD
    pooled = jnp.sum(jnp.where(row_head == col_head, out, 0.0), axis=0, keepdims=True)
    pooled_ref[...] = pooled
    pooled_b = jnp.broadcast_to(pooled, (8, cols)).astype(BF16)
    embed = jnp.dot(pooled_b, wp[...], preferred_element_type=F32)[:1]
    for i in range(embed_ref.shape[0]):
        embed_ref[i : i + 1, :] = embed[:, i * LANES : (i + 1) * LANES]


def pool(parts, late, weights, wp):
    d, cols = weights[0].shape
    heads = cols // HD
    fresh = sum(b.shape[0] for b in late)
    total = fresh + sum(q.shape[0] for q, _, _ in parts)
    bottleneck = wp.shape[1]
    ins = [a for part in parts for a in part] + [*late, *weights, wp]
    return call(
        functools.partial(pool_kernel, len(parts), len(late)),
        [((heads, total), BF16), ((1, cols), F32), ((bottleneck // LANES, LANES), F32)],
        ins,
        2 * fresh * d * cols * 3 + 2 * total * total * cols * 4,
        heads * total * total,
        scratch=[
            pltpu.VMEM((fresh, cols), BF16),
            pltpu.VMEM((cols, fresh), BF16),
            pltpu.VMEM((fresh, cols), BF16),
            pltpu.VMEM((heads, total), F32),
        ],
    )


def mixture_kernel(cameras, w_ref, *refs):
    x_refs, out_ref = refs[:-1], refs[-1]
    mix = jnp.zeros(out_ref.shape, F32)
    for camera in cameras:
        m = jnp.zeros(out_ref.shape, F32)
        for block, at in camera:
            w = w_ref[:, at : at + x_refs[block].shape[0]]
            m = m + jnp.dot(w, x_refs[block][...], preferred_element_type=F32)
        mix = mix + m.astype(BF16).astype(F32)
    out_ref[...] = mix


def gather_clip(tokens, n_cam):
    clips, tok, _ = tokens.shape
    ranks = n_cam // clips
    group = lax.axis_index("cam") // ranks
    size = tok // CHUNKS
    held = [[] for _ in range(CHUNKS + 1)]
    for c in range(CHUNKS):
        for s in range(1, clips):
            start = ((group + s) % clips, c * size, 0)
            sent = lax.dynamic_slice(tokens, start, (1, size, tokens.shape[2]))[0]
            perm = [(i, ((i // ranks + s) % clips) * ranks + i % ranks) for i in range(n_cam)]
            held[c + 1].append((s * ranks, lax.ppermute(sent, "cam", perm)))
    held[0].append((0, lax.dynamic_index_in_dim(tokens, group, 0, keepdims=False)))
    stages = []
    for blocks in held:
        stage = list(blocks)
        for t in range(1, ranks):
            perm = [(i, (i // ranks) * ranks + (i % ranks + t) % ranks) for i in range(n_cam)]
            stage.extend((camera + t, lax.ppermute(b, "cam", perm)) for camera, b in blocks)
        stages.append(stage)
    return stages


def to_lanes(column, offset=0):
    shape = (column.shape[0], LANES)
    row = lax.broadcasted_iota(jnp.int32, shape, 0) + offset
    lane = lax.broadcasted_iota(jnp.int32, shape, 1)
    return jnp.sum(jnp.where(lane == row, column, 0.0), axis=0, keepdims=True)


def from_lanes(line, size, offset=0):
    row = lax.broadcasted_iota(jnp.int32, (size, LANES), 0) + offset
    lane = lax.broadcasted_iota(jnp.int32, (size, LANES), 1)
    return jnp.sum(jnp.where(lane == row, line, 0.0), axis=1, keepdims=True)


def spread(column):
    return jnp.broadcast_to(column, (column.shape[0], LANES))


def exchange(message):
    return lax.all_to_all(message, ALL, split_axis=0, concat_axis=0, tiled=True)


def logits_kernel(
    clips, ranks, n_clip, came, proto, proto_t, unit_ref, norm_ref, exp_ref, assign_ref, message
):
    rows = []
    for g in range(clips):
        for p in range(n_clip):
            z = sum(came[(g * ranks + r) * n_clip + p] for r in range(ranks))
            rows.append(jnp.concatenate([z[i : i + 1] for i in range(z.shape[0])], axis=1))
    embed = jnp.concatenate(rows, axis=0)
    norm = jnp.sqrt(jnp.sum(embed * embed, axis=1, keepdims=True) + NORM_EPS)
    unit = embed / norm
    unit_ref[...] = unit
    norm_ref[...] = spread(norm)
    logits = jnp.dot(unit.astype(BF16), proto[...], preferred_element_type=F32)
    exponents = jnp.exp(logits / SOFTMAX_TEMP)
    assign = jnp.exp(logits / SINK_EPS)
    exp_ref[...] = exponents
    assign = assign / jnp.sum(assign, axis=0, keepdims=True)
    assign_ref[...] = assign
    part = jnp.dot(exponents.astype(BF16), proto_t[...], preferred_element_type=F32)
    batch = part.shape[0]
    line = to_lanes(jnp.sum(assign, axis=1, keepdims=True)) + to_lanes(
        jnp.sum(exponents, axis=1, keepdims=True), batch
    )
    halves = part.shape[1] // LANES
    for i in range(message.shape[0]):
        if i < halves * batch:
            h, b = divmod(i, batch)
            piece = part[b : b + 1, h * LANES : (h + 1) * LANES]
        else:
            piece = jnp.zeros((1, LANES), F32)
        message[i] = jnp.concatenate([piece, line], axis=0)


def second_kernel(came, assign_ref, assign_out, message, total_ref):
    batch = assign_ref.shape[0]
    came = jnp.sum(came[...], axis=0)
    total_ref[...] = spread(from_lanes(came[1:2], batch, batch))
    assign = assign_ref[...] / from_lanes(came[1:2], batch)
    assign = assign / jnp.sum(assign, axis=0, keepdims=True)
    assign_out[...] = assign
    line = to_lanes(jnp.sum(assign, axis=1, keepdims=True))
    out = jnp.concatenate([came[0:1], line], axis=0)
    for i in range(message.shape[0]):
        message[i] = out


def third_kernel(
    parity, came, assign_ref, proto_t, assign_out, keep_ref, send_ref, digits_ref, grad_ref
):
    batch = assign_ref.shape[0]
    halves = proto_t.shape[1] // LANES
    total = jnp.sum(came[...], axis=0)[1:2]
    assign = assign_ref[...] / from_lanes(total, batch)
    assign = assign / jnp.sum(assign, axis=0, keepdims=True)
    assign_out[...] = assign
    part = jnp.dot(assign.astype(BF16), proto_t[...], preferred_element_type=F32)
    half = part.shape[1] // 2
    odd = parity[0] == 1
    low, high = part[:, :half], part[:, half:]
    keep_ref[...] = jnp.where(odd, high, low)
    send_ref[...] = jnp.where(odd, low, high)
    rest = to_lanes(jnp.sum(assign, axis=1, keepdims=True))
    digits_ref[...] = jnp.zeros(digits_ref.shape, F32)
    for i in range(DIGITS):
        digit = rest.astype(BF16).astype(F32)
        digits_ref[i : i + 1, :] = digit
        rest = rest - digit
    for h in range(halves):
        for b in range(batch):
            grad_ref[b : b + 1, h * LANES : (h + 1) * LANES] = came[h * batch + b][0:1]


def message_kernel(keep, got, digits, side, message):
    part = (keep[...] + got[...]).astype(BF16)
    batch = part.shape[0]
    message[:, :batch, :] = jnp.broadcast_to(part[None], (message.shape[0],) + part.shape)
    message[:, batch:, :] = (side[...] + digits[...][None]).astype(BF16)


def output_kernel(
    protos,
    n_cam,
    pick,
    came,
    unit_ref,
    norm_ref,
    exp_ref,
    assign_ref,
    total_ref,
    prob_grad,
    proto,
    scale,
    wp,
    codes,
    proto_grad,
    grad_proj,
    grad_value,
    factor_s,
):
    clips, ranks, n_clip = came.shape[:3]
    batch = unit_ref.shape[0]
    share = grad_proj.shape[0]
    width = codes.shape[1]
    step = pl.program_id(0)

    @pl.when(step == 0)
    def _():
        sums = [jnp.zeros(came.shape[3:], F32) for _ in range(2)]
        for cam in range(n_cam):
            part = jnp.sum(came[cam // ranks, cam % ranks].astype(F32), axis=0)
            sums[cam % 2] = sums[cam % 2] + part
        line = jnp.sum((sums[0] + sums[1])[batch : batch + DIGITS], axis=0, keepdims=True)
        by_assign = protos / from_lanes(line, batch)
        by_prob = protos / total_ref[:, :1]
        factor_s[0] = spread(by_prob)
        factor_s[1] = spread(by_assign)
        assign_grad = jnp.concatenate([s[:batch] for s in sums], axis=1)
        grad_unit = prob_grad[...] * by_prob - assign_grad * by_assign
        unit = unit_ref[...]
        grad_embed = (
            grad_unit - unit * jnp.sum(unit * grad_unit, axis=1, keepdims=True)
        ) / norm_ref[:, :1]
        grad_embed = grad_embed.astype(BF16)

        def rows(rank, at):
            picked = [came[g, rank].astype(F32)[:, at, :] for g in range(clips)]
            return jnp.concatenate(picked, axis=0)[:, :share].astype(BF16)

        grad_proj[...] = lax.dot_general(
            rows(pick[0], batch + DIGITS), grad_embed, OUTER, preferred_element_type=F32
        )
        grad_pooled = lax.dot_general(
            grad_embed, wp[...], TRANSPOSED, preferred_element_type=F32
        ).astype(BF16)
        col_head = lax.broadcasted_iota(jnp.int32, grad_value.shape, 1) // HD
        value = jnp.zeros(grad_value.shape, F32)
        for head in range(grad_value.shape[1] // HD):
            mixed = rows(pick[1], batch + DIGITS + 1 + head)
            out = lax.dot_general(mixed, grad_pooled, OUTER, preferred_element_type=F32)
            value = jnp.where(col_head == head, out, value)
        grad_value[...] = value

    here = pl.ds(pl.multiple_of(step * width, width), width)
    assign = assign_ref[:, here] * factor_s[1][:, :1]
    grad_logits = (exp_ref[:, here] * factor_s[0][:, :1] - assign).astype(BF16)
    for g in range(clips):
        for p in range(n_clip):
            at = g * n_clip + p
            codes[p * clips + g : p * clips + g + 1, :] = assign[at : at + 1]
    grad = lax.dot_general(
        unit_ref[...].astype(BF16), grad_logits, OUTER, preferred_element_type=F32
    )
    inverse = scale[:, here]
    unit_proto = proto[:, here].astype(F32) * inverse
    along = jnp.sum(unit_proto * grad, axis=0, keepdims=True)
    proto_grad[...] = (grad - unit_proto * along) * inverse


def local(tokens, w_query, w_key, w_value, w_proj, prototypes):
    clips, _, tok, d = tokens.shape
    n_cam, n_clip = lax.axis_size("cam"), lax.axis_size("clip")
    devices = n_cam * n_clip
    ranks = n_cam // clips
    batch = clips * n_clip
    cols = d // ranks
    heads = cols // HD
    heads_here = heads // clips
    share = d // n_clip
    bottleneck, columns = prototypes.shape
    protos = columns * devices
    halves = bottleneck // LANES
    cam, clip = lax.axis_index("cam"), lax.axis_index("clip")
    rank = cam % ranks

    with jax.named_scope("tokens_of_a_clip"):
        stages = gather_clip(tokens.reshape(clips, tok, d), n_cam)

    with jax.named_scope("pooling"):
        weights = [
            lax.dynamic_slice_in_dim(w, rank * cols, cols, 1) for w in (w_query, w_key, w_value)
        ]
        wp = lax.dynamic_slice_in_dim(w_proj, rank * cols, cols, 0)
        parts = [project_blocks([b for _, b in stage], weights) for stage in stages[:-1]]
        key_weights, pooled, embed = pool(parts, [b for _, b in stages[-1]], weights, wp)

    with jax.named_scope("prototypes"):
        proto_f = prototypes.astype(F32)
        column_norm = jnp.sqrt(jnp.sum(proto_f * proto_f, axis=0, keepdims=True) + NORM_EPS)
        scale = 1.0 / column_norm
        proto_b = (proto_f / column_norm).astype(BF16)
        proto_t = proto_b.T

    with jax.named_scope("mixtures"):
        cameras, blocks, at = {}, [], 0
        for stage in stages:
            for camera, block in stage:
                cameras.setdefault(camera, []).append((len(blocks), at))
                blocks.append(block)
                at += block.shape[0]
        (mix,) = call(
            functools.partial(mixture_kernel, list(cameras.values())),
            [((heads, d), F32)],
            [key_weights, *blocks],
            2 * at * d * 32,
        )
        mix_to = mix.reshape(clips, heads_here, n_clip, share).transpose(0, 2, 1, 3)
        mix_to = jnp.tile(mix_to.reshape(batch, heads_here, share), (ranks, 1, 1))
        pooled_to = jnp.tile(pooled.reshape(cols // share, 1, share), (devices * share // cols, 1, 1))
        side = jnp.concatenate([pooled_to, mix_to], axis=1)
        side = jnp.pad(side, ((0, 0), (DIGITS, 0), (0, LANES - share)))

    with jax.named_scope("logits"):
        came = exchange(jnp.broadcast_to(embed[None], (devices,) + embed.shape))
        unit, norm, exponents, assign, message = call(
            functools.partial(logits_kernel, clips, ranks, n_clip),
            [
                ((batch, bottleneck), F32),
                ((batch, LANES), F32),
                ((batch, columns), F32),
                ((batch, columns), F32),
                ((devices, 2, LANES), F32),
            ],
            [came, proto_b, proto_t],
            4 * batch * bottleneck * columns,
            2 * batch * columns,
        )

    with jax.named_scope("row_total_1"):
        came = exchange(message)
        assign, message, total = call(
            second_kernel,
            [((batch, columns), F32), ((devices, 2, LANES), F32), ((batch, LANES), F32)],
            [came, assign],
            8 * batch * columns,
        )

    with jax.named_scope("row_total_2"):
        came = exchange(message)
        parity = (cam % 2).reshape(1)
        assign, keep, send, digits, prob_grad = call(
            third_kernel,
            [
                ((batch, columns), F32),
                ((batch, bottleneck // 2), F32),
                ((batch, bottleneck // 2), F32),
                (side.shape[1:], F32),
                ((batch, bottleneck), F32),
            ],
            [parity, came, assign, proto_t],
            2 * batch * bottleneck * columns,
            in_specs=[SCALARS] + [WHOLE] * 3,
        )

    with jax.named_scope("row_total_3"):
        got = lax.ppermute(send, "cam", [(i, i ^ 1) for i in range(n_cam)])
        (message,) = call(
            message_kernel,
            [((devices, batch + side.shape[1], LANES), BF16)],
            [keep, got, digits, side],
            devices * batch * LANES,
        )
        came = exchange(message)

    with jax.named_scope("outputs"):
        width = heads_here * HD
        pick = jnp.stack([clip * share // cols, cam // clips])
        proj_rows = lax.dynamic_slice_in_dim(w_proj, cam * width, width, 0)
        block = min(columns, 512)
        ins = [
            pick,
            came.reshape((clips, ranks, n_clip) + came.shape[1:]),
            unit,
            norm,
            exponents,
            assign,
            total,
            prob_grad,
            prototypes,
            scale,
            proj_rows,
        ]
        return call(
            functools.partial(output_kernel, protos, n_cam),
            [
                ((batch, columns), F32),
                ((bottleneck, columns), F32),
                ((share, bottleneck), F32),
                ((share, width), F32),
            ],
            ins,
            2 * batch * bottleneck * columns,
            scratch=[pltpu.VMEM((2, batch, LANES), F32)],
            grid=(columns // block,),
            in_specs=[SCALARS] + [WHOLE] * (len(ins) - 1),
            out_specs=[
                pl.BlockSpec((batch, block), lambda i: (0, i)),
                pl.BlockSpec((bottleneck, block), lambda i: (0, i)),
                pl.BlockSpec((share, bottleneck), lambda i: (0, 0)),
                pl.BlockSpec((share, width), lambda i: (0, 0)),
            ],
        )


def solution(mesh):
    in_specs = (P("clip", "cam", None, None), P(), P(), P(), P(), P(None, ALL))
    out_specs = (P(None, ALL), P(None, ALL), P("clip", None), P("clip", "cam"))
    return jax.shard_map(local, mesh=mesh, in_specs=in_specs, out_specs=out_specs, check_vma=False)
```

```python
import functools

import jax
import jax.numpy as jnp
from jax import lax
from jax.experimental import pallas as pl
from jax.experimental.pallas import tpu as pltpu
from jax.sharding import PartitionSpec as P

HD = 64
SINK_EPS = 0.05
SOFTMAX_TEMP = 0.1
NORM_EPS = 1e-06
LANES = 128
DIGITS = 3
CHUNKS = 1
ALL = ("cam", "clip")
F32 = jnp.float32
BF16 = jnp.bfloat16
TRANSPOSED = (((1,), (1,)), ((), ()))
OUTER = (((0,), (0,)), ((), ()))
WHOLE = pl.BlockSpec(memory_space=pltpu.VMEM)
SCALARS = pl.BlockSpec(memory_space=pltpu.SMEM)


def call(
    kernel, outs, ins, flops, extra=0, scratch=(), grid=None, out_specs=None, in_specs=None, mib=4
):
    moved = sum(a.size * a.dtype.itemsize for a in ins)
    return pl.pallas_call(
        kernel,
        out_shape=tuple(jax.ShapeDtypeStruct(*o) for o in outs),
        in_specs=in_specs or [WHOLE] * len(ins),
        out_specs=out_specs or [WHOLE] * len(outs),
        scratch_shapes=list(scratch),
        grid=grid or (),
        compiler_params=pltpu.CompilerParams(vmem_limit_bytes=mib * 2**20),
        cost_estimate=pl.CostEstimate(flops=1, bytes_accessed=1, transcendentals=0),
    )(*ins)


def project(x, wq, wk, wv):
    q = jnp.dot(x, wq, preferred_element_type=F32).astype(BF16) * BF16(HD**-0.5)
    kt = jnp.dot(x, wk, preferred_element_type=F32).astype(BF16).T
    v = jnp.dot(x, wv, preferred_element_type=F32).astype(BF16)
    return q, kt, v


def project_kernel(blocks, *refs):
    wq, wk, wv = refs[blocks : blocks + 3]
    q_ref, kt_ref, v_ref = refs[blocks + 3 :]
    at = 0
    for x_ref in refs[:blocks]:
        rows = slice(at, at + x_ref.shape[0])
        at += x_ref.shape[0]
        q_ref[rows, :], kt_ref[:, rows], v_ref[rows, :] = project(
            x_ref[...], wq[...], wk[...], wv[...]
        )


def project_blocks(blocks, weights):
    d, cols = weights[0].shape
    rows = sum(b.shape[0] for b in blocks)
    return call(
        functools.partial(project_kernel, len(blocks)),
        [((rows, cols), BF16), ((cols, rows), BF16), ((rows, cols), BF16)],
        [*blocks, *weights],
        2 * rows * d * cols * 3,
    )


def pool_kernel(parts, late, *refs):
    early = [refs[3 * i : 3 * i + 3] for i in range(parts)]
    refs = refs[3 * parts :]
    x_refs, (wq, wk, wv, wp) = refs[:late], refs[late : late + 4]
    weight_ref, pooled_ref, message, q_s, kt_s, v_s, w_s = refs[late + 4 :]
    project_kernel(late, *x_refs, wq, wk, wv, q_s, kt_s, v_s)
    pieces = early + [(q_s, kt_s, v_s)]
    heads, total = w_s.shape
    cols = heads * HD
    lane = lax.broadcasted_iota(jnp.int32, (total, LANES), 1)

    @pl.loop(0, cols // LANES)
    def _(p):
        here = pl.ds(pl.multiple_of(p * LANES, LANES), LANES)
        q_pair = jnp.concatenate([q[:, here] for q, _, _ in pieces], axis=0)
        k_pair = jnp.concatenate([kt[here, :] for _, kt, _ in pieces], axis=1)
        for e in range(LANES // HD):
            q_head = jnp.where(lane // HD == e, q_pair, BF16(0))
            a = jnp.exp(jnp.dot(q_head, k_pair, preferred_element_type=F32))
            a = a * (1.0 / jnp.sum(a, axis=1, keepdims=True))
            w = jnp.sum(a, axis=0, keepdims=True) * (1.0 / total)
            w_s[pl.ds(p * (LANES // HD) + e, 1), :] = w

    weights = w_s[...].astype(BF16)
    weight_ref[...] = weights
    out, at = jnp.zeros((heads, cols), F32), 0
    for _, _, v in pieces:
        rows = slice(at, at + v.shape[0])
        at += v.shape[0]
        out = out + jnp.dot(weights[:, rows], v[...], preferred_element_type=F32)
    row_head = lax.broadcasted_iota(jnp.int32, out.shape, 0)
    col_head = lax.broadcasted_iota(jnp.int32, out.shape, 1) // HD
    pooled = jnp.sum(jnp.where(row_head == col_head, out, 0.0), axis=0, keepdims=True)
    pooled_ref[...] = pooled
    pooled_b = jnp.broadcast_to(pooled, (8, cols)).astype(BF16)
    embed = jnp.dot(pooled_b, wp[...], preferred_element_type=F32)[:1]
    embed = jnp.concatenate(
        [embed[:, i * LANES : (i + 1) * LANES] for i in range(message.shape[1])], axis=0
    )
    for i in range(message.shape[0]):
        message[i] = embed


def pool(parts, late, weights, wp, devices):
    d, cols = weights[0].shape
    heads = cols // HD
    fresh = sum(b.shape[0] for b in late)
    total = fresh + sum(q.shape[0] for q, _, _ in parts)
    bottleneck = wp.shape[1]
    ins = [a for part in parts for a in part] + [*late, *weights, wp]
    return call(
        functools.partial(pool_kernel, len(parts), len(late)),
        [((heads, total), BF16), ((1, cols), F32), ((devices, bottleneck // LANES, LANES), F32)],
        ins,
        2 * fresh * d * cols * 3 + 2 * total * total * cols * 4,
        heads * total * total,
        scratch=[
            pltpu.VMEM((fresh, cols), BF16),
            pltpu.VMEM((cols, fresh), BF16),
            pltpu.VMEM((fresh, cols), BF16),
            pltpu.VMEM((heads, total), F32),
        ],
        mib=4 + 4 * total * total * 5 // 2**20,
    )


def mixture_kernel(cameras, clips, n_clip, w_ref, pooled_ref, *refs):
    x_refs, side = refs[:-1], refs[-1]
    heads, d = w_ref.shape[0], x_refs[0].shape[1]
    heads_here, share = heads // clips, d // n_clip
    mix = jnp.zeros((heads, d), F32)
    for camera in cameras:
        m = jnp.zeros((heads, d), F32)
        for block, at in camera:
            w = w_ref[:, at : at + x_refs[block].shape[0]]
            m = m + jnp.dot(w, x_refs[block][...], preferred_element_type=F32)
        mix = mix + m.astype(BF16).astype(F32)

    def lanes(x, i):
        x = x[:, i * share : (i + 1) * share]
        if share == LANES:
            return x
        return jnp.concatenate([x, jnp.zeros((x.shape[0], LANES - share), F32)], axis=1)

    for i in range(side.shape[0]):
        j, p = divmod(i % (clips * n_clip), n_clip)
        side[i] = jnp.concatenate(
            [
                jnp.zeros((DIGITS, LANES), F32),
                lanes(pooled_ref[...], i % (pooled_ref.shape[1] // share)),
                lanes(mix[j * heads_here : (j + 1) * heads_here], p),
            ],
            axis=0,
        )


FAR = pl.BlockSpec(memory_space=pltpu.HBM)


def slice_kernel(plan, at, *refs):
    ins = 1 + max(which for which, _ in plan)
    outs, sems = refs[ins:-1], refs[-1]
    copies = []
    for i, (which, where) in enumerate(plan):
        source = refs[which].at[where(at)]
        copies.append(pltpu.make_async_copy(source, outs[i], sems.at[i]))
        copies[-1].start()
    for copy in copies:
        copy.wait()


def slices(at, arrays, plan, shapes):
    return call(
        functools.partial(slice_kernel, plan),
        [(shape, BF16) for shape in shapes],
        [at, *(pltpu.with_memory_space_constraint(a, pltpu.HBM) for a in arrays)],
        0,
        scratch=[pltpu.SemaphoreType.DMA((len(plan),))],
        in_specs=[SCALARS] + [FAR] * len(arrays),
    )


def after(x, *others):
    return lax.optimization_barrier((x, others))[0]


def first_blocks(tokens, n_cam):
    clips, tok, d = tokens.shape
    ranks = n_cam // clips
    group = lax.axis_index("cam") // ranks
    size = tok // CHUNKS
    at = jnp.stack([(group + s) % clips for s in range(clips)]).astype(jnp.int32)
    pieces = [(s, c) for c in range(CHUNKS) for s in range(1, clips)]

    def piece(s, c):
        return 0, lambda at: (at[s], pl.ds(c * size, size), slice(None))

    *sent, mine = slices(
        at,
        [tokens],
        [piece(s, c) for s, c in pieces] + [(0, lambda at: (at[0], slice(None), slice(None)))],
        [(size, d)] * len(pieces) + [(tok, d)],
    )
    held = [[(0, mine)]] + [[] for _ in range(CHUNKS)]
    for (s, c), block in zip(pieces, sent):
        perm = [(i, ((i // ranks + s) % clips) * ranks + i % ranks) for i in range(n_cam)]
        held[c + 1].append((s * ranks, lax.ppermute(block, "cam", perm)))
    return held


def relay(blocks, n_cam, ranks):
    stage = list(blocks)
    for t in range(1, ranks):
        perm = [(i, (i // ranks) * ranks + (i % ranks + t) % ranks) for i in range(n_cam)]
        stage.extend((camera + t, lax.ppermute(b, "cam", perm)) for camera, b in blocks)
    return stage


def prototype_kernel(proto, scale, proto_b):
    proto_f = proto[...].astype(F32)
    norm = jnp.sqrt(jnp.sum(proto_f * proto_f, axis=0, keepdims=True) + NORM_EPS)
    scale[...] = 1.0 / norm
    proto_b[...] = (proto_f / norm).astype(BF16)


def to_lanes(column, offset=0):
    shape = (column.shape[0], LANES)
    row = lax.broadcasted_iota(jnp.int32, shape, 0) + offset
    lane = lax.broadcasted_iota(jnp.int32, shape, 1)
    return jnp.sum(jnp.where(lane == row, column, 0.0), axis=0, keepdims=True)


def from_lanes(line, size, offset=0):
    row = lax.broadcasted_iota(jnp.int32, (size, LANES), 0) + offset
    lane = lax.broadcasted_iota(jnp.int32, (size, LANES), 1)
    return jnp.sum(jnp.where(lane == row, line, 0.0), axis=1, keepdims=True)


def spread(column):
    return jnp.broadcast_to(column, (column.shape[0], LANES))


def exchange(message):
    return lax.all_to_all(message, ALL, split_axis=0, concat_axis=0, tiled=True)


def logits_kernel(
    clips, ranks, n_clip, came, proto, unit_ref, norm_ref, exp_ref, assign_ref, message
):
    rows = []
    for g in range(clips):
        for p in range(n_clip):
            z = sum(came[(g * ranks + r) * n_clip + p] for r in range(ranks))
            rows.append(jnp.concatenate([z[i : i + 1] for i in range(z.shape[0])], axis=1))
    embed = jnp.concatenate(rows, axis=0)
    norm = jnp.sqrt(jnp.sum(embed * embed, axis=1, keepdims=True) + NORM_EPS)
    unit = embed / norm
    unit_ref[...] = unit
    norm_ref[...] = spread(norm)
    logits = jnp.dot(unit.astype(BF16), proto[...], preferred_element_type=F32)
    exponents = jnp.exp(logits / SOFTMAX_TEMP)
    assign = jnp.exp(logits / SINK_EPS)
    exp_ref[...] = exponents
    assign = assign / jnp.sum(assign, axis=0, keepdims=True)
    assign_ref[...] = assign
    part = lax.dot_general(
        exponents.astype(BF16), proto[...], TRANSPOSED, preferred_element_type=F32
    )
    batch = part.shape[0]
    line = to_lanes(jnp.sum(assign, axis=1, keepdims=True)) + to_lanes(
        jnp.sum(exponents, axis=1, keepdims=True), batch
    )
    halves = part.shape[1] // LANES
    for i in range(message.shape[0]):
        if i < halves * batch:
            h, b = divmod(i, batch)
            piece = part[b : b + 1, h * LANES : (h + 1) * LANES]
        else:
            piece = jnp.zeros((1, LANES), F32)
        message[i] = jnp.concatenate([piece, line], axis=0)


def second_kernel(came, assign_ref, assign_out, message, total_ref):
    batch = assign_ref.shape[0]
    came = jnp.sum(came[...], axis=0)
    total_ref[...] = spread(from_lanes(came[1:2], batch, batch))
    assign = assign_ref[...] / from_lanes(came[1:2], batch)
    assign = assign / jnp.sum(assign, axis=0, keepdims=True)
    assign_out[...] = assign
    line = to_lanes(jnp.sum(assign, axis=1, keepdims=True))
    out = jnp.concatenate([came[0:1], line], axis=0)
    for i in range(message.shape[0]):
        message[i] = out


def third_kernel(
    parity, came, assign_ref, proto, assign_out, keep_ref, send_ref, digits_ref, grad_ref
):
    batch = assign_ref.shape[0]
    halves = proto.shape[0] // LANES
    total = jnp.sum(came[...], axis=0)[1:2]
    assign = assign_ref[...] / from_lanes(total, batch)
    assign = assign / jnp.sum(assign, axis=0, keepdims=True)
    assign_out[...] = assign
    part = lax.dot_general(
        assign.astype(BF16), proto[...], TRANSPOSED, preferred_element_type=F32
    )
    half = part.shape[1] // 2
    odd = parity[0] == 1
    low, high = part[:, :half], part[:, half:]
    keep_ref[...] = jnp.where(odd, high, low)
    send_ref[...] = jnp.where(odd, low, high)
    rest = to_lanes(jnp.sum(assign, axis=1, keepdims=True))
    digits_ref[...] = jnp.zeros(digits_ref.shape, F32)
    for i in range(DIGITS):
        digit = rest.astype(BF16).astype(F32)
        digits_ref[i : i + 1, :] = digit
        rest = rest - digit
    for h in range(halves):
        for b in range(batch):
            grad_ref[b : b + 1, h * LANES : (h + 1) * LANES] = came[h * batch + b][0:1]


def message_kernel(keep, got, digits, side, message):
    part = (keep[...] + got[...]).astype(BF16)
    batch = part.shape[0]
    message[:, :batch, :] = jnp.broadcast_to(part[None], (message.shape[0],) + part.shape)
    message[:, batch:, :] = (side[...] + digits[...][None]).astype(BF16)


def output_kernel(
    protos,
    n_cam,
    pick,
    came,
    unit_ref,
    norm_ref,
    exp_ref,
    assign_ref,
    total_ref,
    prob_grad,
    proto,
    scale,
    wp,
    codes,
    proto_grad,
    grad_proj,
    grad_value,
    factor_s,
):
    clips, ranks, n_clip = came.shape[:3]
    batch = unit_ref.shape[0]
    share = grad_proj.shape[0]
    width = codes.shape[1]
    step = pl.program_id(0)

    @pl.when(step == 0)
    def _():
        sums = [jnp.zeros(came.shape[3:], F32) for _ in range(2)]
        for cam in range(n_cam):
            part = jnp.sum(came[cam // ranks, cam % ranks].astype(F32), axis=0)
            sums[cam % 2] = sums[cam % 2] + part
        line = jnp.sum((sums[0] + sums[1])[batch : batch + DIGITS], axis=0, keepdims=True)
        by_assign = protos / from_lanes(line, batch)
        by_prob = protos / total_ref[:, :1]
        factor_s[0] = spread(by_prob)
        factor_s[1] = spread(by_assign)
        assign_grad = jnp.concatenate([s[:batch] for s in sums], axis=1)
        grad_unit = prob_grad[...] * by_prob - assign_grad * by_assign
        unit = unit_ref[...]
        grad_embed = (
            grad_unit - unit * jnp.sum(unit * grad_unit, axis=1, keepdims=True)
        ) / norm_ref[:, :1]
        grad_embed = grad_embed.astype(BF16)

        def rows(rank, at):
            picked = [came[g, rank].astype(F32)[:, at, :] for g in range(clips)]
            return jnp.concatenate(picked, axis=0)[:, :share].astype(BF16)

        grad_proj[...] = lax.dot_general(
            rows(pick[0], batch + DIGITS), grad_embed, OUTER, preferred_element_type=F32
        )
        grad_pooled = lax.dot_general(
            grad_embed, wp[...], TRANSPOSED, preferred_element_type=F32
        ).astype(BF16)
        col_head = lax.broadcasted_iota(jnp.int32, grad_value.shape, 1) // HD
        value = jnp.zeros(grad_value.shape, F32)
        for head in range(grad_value.shape[1] // HD):
            mixed = rows(pick[1], batch + DIGITS + 1 + head)
            out = lax.dot_general(mixed, grad_pooled, OUTER, preferred_element_type=F32)
            value = jnp.where(col_head == head, out, value)
        grad_value[...] = value

    here = pl.ds(pl.multiple_of(step * width, width), width)
    assign = assign_ref[:, here] * factor_s[1][:, :1]
    grad_logits = (exp_ref[:, here] * factor_s[0][:, :1] - assign).astype(BF16)
    for g in range(clips):
        for p in range(n_clip):
            at = g * n_clip + p
            codes[p * clips + g : p * clips + g + 1, :] = assign[at : at + 1]
    grad = lax.dot_general(
        unit_ref[...].astype(BF16), grad_logits, OUTER, preferred_element_type=F32
    )
    inverse = scale[:, here]
    unit_proto = proto[:, here].astype(F32) * inverse
    along = jnp.sum(unit_proto * grad, axis=0, keepdims=True)
    proto_grad[...] = (grad - unit_proto * along) * inverse


def local(tokens, w_query, w_key, w_value, w_proj, prototypes):
    clips, _, tok, d = tokens.shape
    n_cam, n_clip = lax.axis_size("cam"), lax.axis_size("clip")
    devices = n_cam * n_clip
    ranks = n_cam // clips
    batch = clips * n_clip
    cols = d // ranks
    heads = cols // HD
    heads_here = heads // clips
    share = d // n_clip
    bottleneck, columns = prototypes.shape
    protos = columns * devices
    cam, clip = lax.axis_index("cam"), lax.axis_index("clip")
    rank = cam % ranks

    with jax.named_scope("tokens_of_a_clip"):
        held = first_blocks(tokens.reshape(clips, tok, d), n_cam)

    with jax.named_scope("prototypes"):
        scale, proto_b = call(
            prototype_kernel,
            [((1, columns), F32), ((bottleneck, columns), BF16)],
            [prototypes],
            4 * bottleneck * columns,
            mib=8,
        )

    with jax.named_scope("pooling"):
        columns_of = [
            (i, lambda at: (slice(None), pl.ds(pl.multiple_of(at[0], cols), cols))) for i in range(3)
        ]
        rows_of = (3, lambda at: (pl.ds(pl.multiple_of(at[0], cols), cols), slice(None)))
        *weights, wp = slices(
            (rank * cols).reshape(1),
            [w_query, w_key, w_value, w_proj],
            columns_of + [rows_of],
            [(d, cols)] * 3 + [(cols, bottleneck)],
        )
        stages, parts = [], []
        for i, blocks in enumerate(held):
            if i:
                blocks = [(camera, after(b, proto_b, *parts)) for camera, b in blocks]
            stages.append(relay(blocks, n_cam, ranks))
            if i < CHUNKS:
                parts.append(project_blocks([b for _, b in stages[-1]], weights))
        late = [b for _, b in stages[-1]]
        key_weights, pooled, message = pool(parts, late, weights, wp, devices)

    with jax.named_scope("mixtures"):
        cameras, blocks, at = {}, [], 0
        for stage in stages:
            for camera, block in stage:
                cameras.setdefault(camera, []).append((len(blocks), at))
                blocks.append(block)
                at += block.shape[0]
        (side,) = call(
            functools.partial(mixture_kernel, list(cameras.values()), clips, n_clip),
            [((devices, DIGITS + 1 + heads_here, LANES), F32)],
            [key_weights, pooled, *blocks],
            2 * at * d * 32,
            mib=8,
        )

    with jax.named_scope("logits"):
        came = after(exchange(message), side)
        unit, norm, exponents, assign, message = call(
            functools.partial(logits_kernel, clips, ranks, n_clip),
            [
                ((batch, bottleneck), F32),
                ((batch, LANES), F32),
                ((batch, columns), F32),
                ((batch, columns), F32),
                ((devices, 2, LANES), F32),
            ],
            [came, proto_b],
            4 * batch * bottleneck * columns,
            2 * batch * columns,
        )

    with jax.named_scope("row_total_1"):
        came = exchange(message)
        assign, message, total = call(
            second_kernel,
            [((batch, columns), F32), ((devices, 2, LANES), F32), ((batch, LANES), F32)],
            [came, assign],
            8 * batch * columns,
        )

    with jax.named_scope("row_total_2"):
        came = exchange(message)
        parity = (cam % 2).reshape(1)
        assign, keep, send, digits, prob_grad = call(
            third_kernel,
            [
                ((batch, columns), F32),
                ((batch, bottleneck // 2), F32),
                ((batch, bottleneck // 2), F32),
                (side.shape[1:], F32),
                ((batch, bottleneck), F32),
            ],
            [parity, came, assign, proto_b],
            2 * batch * bottleneck * columns,
            in_specs=[SCALARS] + [WHOLE] * 3,
        )

    with jax.named_scope("row_total_3"):
        got = lax.ppermute(send, "cam", [(i, i ^ 1) for i in range(n_cam)])
        (message,) = call(
            message_kernel,
            [((devices, batch + side.shape[1], LANES), BF16)],
            [keep, got, digits, side],
            devices * batch * LANES,
        )
        came = exchange(message)

    with jax.named_scope("outputs"):
        width = heads_here * HD
        pick = jnp.stack([clip * share // cols, cam // clips])
        proj_rows = lax.dynamic_slice_in_dim(w_proj, cam * width, width, 0)
        block = min(columns, 512)
        ins = [
            pick,
            came.reshape((clips, ranks, n_clip) + came.shape[1:]),
            unit,
            norm,
            exponents,
            assign,
            total,
            prob_grad,
            prototypes,
            scale,
            proj_rows,
        ]
        return call(
            functools.partial(output_kernel, protos, n_cam),
            [
                ((batch, columns), F32),
                ((bottleneck, columns), F32),
                ((share, bottleneck), F32),
                ((share, width), F32),
            ],
            ins,
            2 * batch * bottleneck * columns,
            scratch=[pltpu.VMEM((2, batch, LANES), F32)],
            mib=8,
            grid=(columns // block,),
            in_specs=[SCALARS] + [WHOLE] * (len(ins) - 1),
            out_specs=[
                pl.BlockSpec((batch, block), lambda i: (0, i)),
                pl.BlockSpec((bottleneck, block), lambda i: (0, i)),
                pl.BlockSpec((share, bottleneck), lambda i: (0, 0)),
                pl.BlockSpec((share, width), lambda i: (0, 0)),
            ],
        )


def solution(mesh):
    in_specs = (P("clip", "cam", None, None), P(), P(), P(), P(), P(None, ALL))
    out_specs = (P(None, ALL), P(None, ALL), P("clip", None), P("clip", "cam"))
    return jax.shard_map(local, mesh=mesh, in_specs=in_specs, out_specs=out_specs, check_vma=False)
```

```python
import functools

import jax
import jax.numpy as jnp
from jax import lax
from jax.experimental import pallas as pl
from jax.experimental.pallas import tpu as pltpu
from jax.sharding import PartitionSpec as P

HD = 64
SINK_EPS = 0.05
SOFTMAX_TEMP = 0.1
NORM_EPS = 1e-06
LANES = 128
DIGITS = 3
CHUNKS = 1
ALL = ("cam", "clip")
F32 = jnp.float32
BF16 = jnp.bfloat16
TRANSPOSED = (((1,), (1,)), ((), ()))
OUTER = (((0,), (0,)), ((), ()))
WHOLE = pl.BlockSpec(memory_space=pltpu.VMEM)
SCALARS = pl.BlockSpec(memory_space=pltpu.SMEM)


def call(
    kernel, outs, ins, flops, extra=0, scratch=(), grid=None, out_specs=None, in_specs=None, mib=4
):
    moved = sum(a.size * a.dtype.itemsize for a in ins)
    return pl.pallas_call(
        kernel,
        out_shape=tuple(jax.ShapeDtypeStruct(*o) for o in outs),
        in_specs=in_specs or [WHOLE] * len(ins),
        out_specs=out_specs or [WHOLE] * len(outs),
        scratch_shapes=list(scratch),
        grid=grid or (),
        compiler_params=pltpu.CompilerParams(vmem_limit_bytes=mib * 2**20),
        cost_estimate=pl.CostEstimate(flops=1, bytes_accessed=1, transcendentals=0),
    )(*ins)


def project(x, wq, wk, wv):
    q = jnp.dot(x, wq, preferred_element_type=F32).astype(BF16) * BF16(HD**-0.5)
    kt = jnp.dot(x, wk, preferred_element_type=F32).astype(BF16).T
    v = jnp.dot(x, wv, preferred_element_type=F32).astype(BF16)
    return q, kt, v


def project_kernel(blocks, *refs):
    wq, wk, wv = refs[blocks : blocks + 3]
    q_ref, kt_ref, v_ref = refs[blocks + 3 :]
    at = 0
    for x_ref in refs[:blocks]:
        rows = slice(at, at + x_ref.shape[0])
        at += x_ref.shape[0]
        q_ref[rows, :], kt_ref[:, rows], v_ref[rows, :] = project(
            x_ref[...], wq[...], wk[...], wv[...]
        )


def project_blocks(blocks, weights):
    d, cols = weights[0].shape
    rows = sum(b.shape[0] for b in blocks)
    return call(
        functools.partial(project_kernel, len(blocks)),
        [((rows, cols), BF16), ((cols, rows), BF16), ((rows, cols), BF16)],
        [*blocks, *weights],
        2 * rows * d * cols * 3,
    )


def pool_kernel(parts, late, *refs):
    early = [refs[3 * i : 3 * i + 3] for i in range(parts)]
    refs = refs[3 * parts :]
    x_refs, (wq, wk, wv, wp) = refs[:late], refs[late : late + 4]
    weight_ref, pooled_ref, message, q_s, kt_s, v_s, w_s = refs[late + 4 :]
    project_kernel(late, *x_refs, wq, wk, wv, q_s, kt_s, v_s)
    pieces = early + [(q_s, kt_s, v_s)]
    heads, total = w_s.shape
    cols = heads * HD
    lane = lax.broadcasted_iota(jnp.int32, (total, LANES), 1)

    @pl.loop(0, cols // LANES)
    def _(p):
        here = pl.ds(pl.multiple_of(p * LANES, LANES), LANES)
        q_pair = jnp.concatenate([q[:, here] for q, _, _ in pieces], axis=0)
        k_pair = jnp.concatenate([kt[here, :] for _, kt, _ in pieces], axis=1)
        for e in range(LANES // HD):
            q_head = jnp.where(lane // HD == e, q_pair, BF16(0))
            a = jnp.exp(jnp.dot(q_head, k_pair, preferred_element_type=F32))
            a = a * (1.0 / jnp.sum(a, axis=1, keepdims=True))
            w = jnp.sum(a, axis=0, keepdims=True) * (1.0 / total)
            w_s[pl.ds(p * (LANES // HD) + e, 1), :] = w

    weights = w_s[...].astype(BF16)
    weight_ref[...] = weights
    out, at = jnp.zeros((heads, cols), F32), 0
    for _, _, v in pieces:
        rows = slice(at, at + v.shape[0])
        at += v.shape[0]
        out = out + jnp.dot(weights[:, rows], v[...], preferred_element_type=F32)
    row_head = lax.broadcasted_iota(jnp.int32, out.shape, 0)
    col_head = lax.broadcasted_iota(jnp.int32, out.shape, 1) // HD
    pooled = jnp.sum(jnp.where(row_head == col_head, out, 0.0), axis=0, keepdims=True)
    pooled_ref[...] = pooled
    pooled_b = jnp.broadcast_to(pooled, (8, cols)).astype(BF16)
    embed = jnp.dot(pooled_b, wp[...], preferred_element_type=F32)[:1]
    embed = jnp.concatenate(
        [embed[:, i * LANES : (i + 1) * LANES] for i in range(message.shape[1])], axis=0
    )
    for i in range(message.shape[0]):
        message[i] = embed


def pool(parts, late, weights, wp, devices):
    d, cols = weights[0].shape
    heads = cols // HD
    fresh = sum(b.shape[0] for b in late)
    total = fresh + sum(q.shape[0] for q, _, _ in parts)
    bottleneck = wp.shape[1]
    ins = [a for part in parts for a in part] + [*late, *weights, wp]
    return call(
        functools.partial(pool_kernel, len(parts), len(late)),
        [((heads, total), BF16), ((1, cols), F32), ((devices, bottleneck // LANES, LANES), F32)],
        ins,
        2 * fresh * d * cols * 3 + 2 * total * total * cols * 4,
        heads * total * total,
        scratch=[
            pltpu.VMEM((fresh, cols), BF16),
            pltpu.VMEM((cols, fresh), BF16),
            pltpu.VMEM((fresh, cols), BF16),
            pltpu.VMEM((heads, total), F32),
        ],
        mib=4 + 4 * total * total * 5 // 2**20,
    )


def mixture_kernel(cameras, clips, n_clip, w_ref, pooled_ref, *refs):
    x_refs, side = refs[:-1], refs[-1]
    heads, d = w_ref.shape[0], x_refs[0].shape[1]
    heads_here, share = heads // clips, d // n_clip
    mix = jnp.zeros((heads, d), F32)
    for camera in cameras:
        m = jnp.zeros((heads, d), F32)
        for block, at in camera:
            w = w_ref[:, at : at + x_refs[block].shape[0]]
            m = m + jnp.dot(w, x_refs[block][...], preferred_element_type=F32)
        mix = mix + m.astype(BF16).astype(F32)

    def lanes(x, i):
        x = x[:, i * share : (i + 1) * share]
        if share == LANES:
            return x
        return jnp.concatenate([x, jnp.zeros((x.shape[0], LANES - share), F32)], axis=1)

    for i in range(side.shape[0]):
        j, p = divmod(i % (clips * n_clip), n_clip)
        side[i] = jnp.concatenate(
            [
                jnp.zeros((DIGITS, LANES), F32),
                lanes(pooled_ref[...], i % (pooled_ref.shape[1] // share)),
                lanes(mix[j * heads_here : (j + 1) * heads_here], p),
            ],
            axis=0,
        )


FAR = pl.BlockSpec(memory_space=pltpu.HBM)


def slice_kernel(plan, at, *refs):
    ins = 1 + max(which for which, _ in plan)
    outs, sems = refs[ins:-1], refs[-1]
    copies = []
    for i, (which, where) in enumerate(plan):
        source = refs[which].at[where(at)]
        copies.append(pltpu.make_async_copy(source, outs[i], sems.at[i]))
        copies[-1].start()
    for copy in copies:
        copy.wait()


def slices(at, arrays, plan, shapes):
    return call(
        functools.partial(slice_kernel, plan),
        [(shape, BF16) for shape in shapes],
        [at, *(pltpu.with_memory_space_constraint(a, pltpu.HBM) for a in arrays)],
        0,
        scratch=[pltpu.SemaphoreType.DMA((len(plan),))],
        in_specs=[SCALARS] + [FAR] * len(arrays),
    )


def after(x, *others):
    return lax.optimization_barrier((x, others))[0]


def token_piece(s, c, size):
    return lambda at: (at[s], pl.ds(c * size, size), slice(None))


def from_other_groups(tokens, groups, n_cam):
    clips, tok, d = tokens.shape
    ranks = n_cam // clips
    size = tok // CHUNKS
    pieces = [(s, c) for c in range(CHUNKS) for s in range(1, clips)]
    *sent, mine = slices(
        groups,
        [tokens],
        [(0, token_piece(s, c, size)) for s, c in pieces] + [(0, token_piece(0, 0, tok))],
        [(size, d)] * len(pieces) + [(tok, d)],
    )
    held = [[] for _ in range(CHUNKS)]
    for (s, c), block in zip(pieces, sent):
        perm = [(i, ((i // ranks + s) % clips) * ranks + i % ranks) for i in range(n_cam)]
        held[c].append((s * ranks, lax.ppermute(block, "cam", perm)))
    return mine, held


def relay(blocks, n_cam, ranks):
    stage = list(blocks)
    for t in range(1, ranks):
        perm = [(i, (i // ranks) * ranks + (i % ranks + t) % ranks) for i in range(n_cam)]
        stage.extend((camera + t, lax.ppermute(b, "cam", perm)) for camera, b in blocks)
    return stage


def prototype_kernel(proto, scale, proto_b):
    proto_f = proto[...].astype(F32)
    norm = jnp.sqrt(jnp.sum(proto_f * proto_f, axis=0, keepdims=True) + NORM_EPS)
    scale[...] = 1.0 / norm
    proto_b[...] = (proto_f / norm).astype(BF16)


def to_lanes(column, offset=0):
    shape = (column.shape[0], LANES)
    row = lax.broadcasted_iota(jnp.int32, shape, 0) + offset
    lane = lax.broadcasted_iota(jnp.int32, shape, 1)
    return jnp.sum(jnp.where(lane == row, column, 0.0), axis=0, keepdims=True)


def from_lanes(line, size, offset=0):
    row = lax.broadcasted_iota(jnp.int32, (size, LANES), 0) + offset
    lane = lax.broadcasted_iota(jnp.int32, (size, LANES), 1)
    return jnp.sum(jnp.where(lane == row, line, 0.0), axis=1, keepdims=True)


def spread(column):
    return jnp.broadcast_to(column, (column.shape[0], LANES))


def exchange(message):
    return lax.all_to_all(message, ALL, split_axis=0, concat_axis=0, tiled=True)


def logits_kernel(
    clips, ranks, n_clip, came, proto, unit_ref, norm_ref, exp_ref, assign_ref, message
):
    rows = []
    for g in range(clips):
        for p in range(n_clip):
            z = sum(came[(g * ranks + r) * n_clip + p] for r in range(ranks))
            rows.append(jnp.concatenate([z[i : i + 1] for i in range(z.shape[0])], axis=1))
    embed = jnp.concatenate(rows, axis=0)
    norm = jnp.sqrt(jnp.sum(embed * embed, axis=1, keepdims=True) + NORM_EPS)
    unit = embed / norm
    unit_ref[...] = unit
    norm_ref[...] = spread(norm)
    logits = jnp.dot(unit.astype(BF16), proto[...], preferred_element_type=F32)
    exponents = jnp.exp(logits / SOFTMAX_TEMP)
    assign = jnp.exp(logits / SINK_EPS)
    exp_ref[...] = exponents
    assign = assign / jnp.sum(assign, axis=0, keepdims=True)
    assign_ref[...] = assign
    part = lax.dot_general(
        exponents.astype(BF16), proto[...], TRANSPOSED, preferred_element_type=F32
    )
    batch = part.shape[0]
    line = to_lanes(jnp.sum(assign, axis=1, keepdims=True)) + to_lanes(
        jnp.sum(exponents, axis=1, keepdims=True), batch
    )
    halves = part.shape[1] // LANES
    for i in range(message.shape[0]):
        if i < halves * batch:
            h, b = divmod(i, batch)
            piece = part[b : b + 1, h * LANES : (h + 1) * LANES]
        else:
            piece = jnp.zeros((1, LANES), F32)
        message[i] = jnp.concatenate([piece, line], axis=0)


def second_kernel(came, assign_ref, assign_out, message, total_ref):
    batch = assign_ref.shape[0]
    came = jnp.sum(came[...], axis=0)
    total_ref[...] = spread(from_lanes(came[1:2], batch, batch))
    assign = assign_ref[...] / from_lanes(came[1:2], batch)
    assign = assign / jnp.sum(assign, axis=0, keepdims=True)
    assign_out[...] = assign
    line = to_lanes(jnp.sum(assign, axis=1, keepdims=True))
    out = jnp.concatenate([came[0:1], line], axis=0)
    for i in range(message.shape[0]):
        message[i] = out


def third_kernel(
    parity, came, assign_ref, proto, assign_out, keep_ref, send_ref, digits_ref, grad_ref
):
    batch = assign_ref.shape[0]
    halves = proto.shape[0] // LANES
    total = jnp.sum(came[...], axis=0)[1:2]
    assign = assign_ref[...] / from_lanes(total, batch)
    assign = assign / jnp.sum(assign, axis=0, keepdims=True)
    assign_out[...] = assign
    part = lax.dot_general(
        assign.astype(BF16), proto[...], TRANSPOSED, preferred_element_type=F32
    )
    half = part.shape[1] // 2
    odd = parity[0] == 1
    low, high = part[:, :half], part[:, half:]
    keep_ref[...] = jnp.where(odd, high, low)
    send_ref[...] = jnp.where(odd, low, high)
    rest = to_lanes(jnp.sum(assign, axis=1, keepdims=True))
    digits_ref[...] = jnp.zeros(digits_ref.shape, F32)
    for i in range(DIGITS):
        digit = rest.astype(BF16).astype(F32)
        digits_ref[i : i + 1, :] = digit
        rest = rest - digit
    for h in range(halves):
        for b in range(batch):
            grad_ref[b : b + 1, h * LANES : (h + 1) * LANES] = came[h * batch + b][0:1]


def message_kernel(keep, got, digits, side, message):
    part = (keep[...] + got[...]).astype(BF16)
    batch = part.shape[0]
    message[:, :batch, :] = jnp.broadcast_to(part[None], (message.shape[0],) + part.shape)
    message[:, batch:, :] = (side[...] + digits[...][None]).astype(BF16)


def output_kernel(
    protos,
    n_cam,
    block,
    pick,
    came,
    unit_ref,
    norm_ref,
    exp_ref,
    assign_ref,
    total_ref,
    prob_grad,
    proto,
    scale,
    wp,
    codes_out,
    proto_grad_out,
    grad_proj_out,
    grad_value_out,
    codes,
    proto_grad,
    grad_proj,
    grad_value,
    sems,
):
    clips, ranks, n_clip = came.shape[:3]
    batch, columns = exp_ref.shape
    share = grad_proj.shape[0]
    copies = []

    def send(source, target):
        copies.append(pltpu.make_async_copy(source, target, sems.at[len(copies)]))
        copies[-1].start()

    sums = [jnp.zeros(came.shape[3:], F32) for _ in range(2)]
    for cam in range(n_cam):
        part = jnp.sum(came[cam // ranks, cam % ranks].astype(F32), axis=0)
        sums[cam % 2] = sums[cam % 2] + part
    line = jnp.sum((sums[0] + sums[1])[batch : batch + DIGITS], axis=0, keepdims=True)
    by_assign = protos / from_lanes(line, batch)
    by_prob = protos / total_ref[:, :1]
    unit = unit_ref[...]
    unit_b = unit.astype(BF16)

    for start in range(0, columns, block):
        here = slice(start, start + block)
        assign = assign_ref[:, here] * by_assign
        grad_logits = (exp_ref[:, here] * by_prob - assign).astype(BF16)
        for g in range(clips):
            for p in range(n_clip):
                at, to = g * n_clip + p, p * clips + g
                codes[to : to + 1, here] = assign[at : at + 1]
        grad = lax.dot_general(unit_b, grad_logits, OUTER, preferred_element_type=F32)
        inverse = scale[:, here]
        unit_proto = proto[:, here].astype(F32) * inverse
        along = jnp.sum(unit_proto * grad, axis=0, keepdims=True)
        proto_grad[:, here] = (grad - unit_proto * along) * inverse
        send(proto_grad.at[:, here], proto_grad_out.at[:, here])
    send(codes, codes_out)

    assign_grad = jnp.concatenate([s[:batch] for s in sums], axis=1)
    grad_unit = prob_grad[...] * by_prob - assign_grad * by_assign
    grad_embed = (
        grad_unit - unit * jnp.sum(unit * grad_unit, axis=1, keepdims=True)
    ) / norm_ref[:, :1]
    grad_embed = grad_embed.astype(BF16)

    def rows(rank, at):
        picked = [came[g, rank].astype(F32)[:, at, :] for g in range(clips)]
        return jnp.concatenate(picked, axis=0)[:, :share].astype(BF16)

    grad_proj[...] = lax.dot_general(
        rows(pick[0], batch + DIGITS), grad_embed, OUTER, preferred_element_type=F32
    )
    send(grad_proj, grad_proj_out)
    grad_pooled = lax.dot_general(
        grad_embed, wp[...], TRANSPOSED, preferred_element_type=F32
    ).astype(BF16)
    col_head = lax.broadcasted_iota(jnp.int32, grad_value.shape, 1) // HD
    value = jnp.zeros(grad_value.shape, F32)
    for head in range(grad_value.shape[1] // HD):
        mixed = rows(pick[1], batch + DIGITS + 1 + head)
        out = lax.dot_general(mixed, grad_pooled, OUTER, preferred_element_type=F32)
        value = jnp.where(col_head == head, out, value)
    grad_value[...] = value
    send(grad_value, grad_value_out)
    for copy in copies:
        copy.wait()


def local(tokens, w_query, w_key, w_value, w_proj, prototypes):
    clips, _, tok, d = tokens.shape
    n_cam, n_clip = lax.axis_size("cam"), lax.axis_size("clip")
    devices = n_cam * n_clip
    ranks = n_cam // clips
    batch = clips * n_clip
    cols = d // ranks
    heads = cols // HD
    heads_here = heads // clips
    share = d // n_clip
    bottleneck, columns = prototypes.shape
    protos = columns * devices
    cam, clip = lax.axis_index("cam"), lax.axis_index("clip")
    rank = cam % ranks

    with jax.named_scope("tokens_of_a_clip"):
        tokens = tokens.reshape(clips, tok, d)
        groups = [(cam // ranks + s) % clips for s in range(clips)]
        groups = jnp.stack(groups + [rank * cols]).astype(jnp.int32)
        mine, held = from_other_groups(tokens, groups, n_cam)

    with jax.named_scope("prototypes"):
        scale, proto_b = call(
            prototype_kernel,
            [((1, columns), F32), ((bottleneck, columns), BF16)],
            [prototypes],
            4 * bottleneck * columns,
            mib=8,
        )

    with jax.named_scope("pooling"):
        def columns_of(at):
            return slice(None), pl.ds(pl.multiple_of(at[clips], cols), cols)

        def rows_of(at):
            return pl.ds(pl.multiple_of(at[clips], cols), cols), slice(None)

        *weights, wp = slices(
            groups,
            [w_query, w_key, w_value, w_proj],
            [(i, columns_of) for i in range(3)] + [(3, rows_of)],
            [(d, cols)] * 3 + [(cols, bottleneck)],
        )
        stages, parts = [relay([(0, mine)], n_cam, ranks)], []
        parts.append(project_blocks([b for _, b in stages[0]], weights))
        for blocks in held:
            blocks = [(camera, after(b, proto_b, *parts)) for camera, b in blocks]
            stages.append(relay(blocks, n_cam, ranks))
            if blocks is not held[-1] and len(stages) <= CHUNKS:
                parts.append(project_blocks([b for _, b in stages[-1]], weights))
        own = len(held[-1])
        parts.append(project_blocks([b for _, b in stages[-1][:own]], weights))
        late = [b for _, b in stages[-1][own:]]
        key_weights, pooled, message = pool(parts, late, weights, wp, devices)

    with jax.named_scope("mixtures"):
        cameras, blocks, at = {}, [], 0
        for stage in stages:
            for camera, block in stage:
                cameras.setdefault(camera, []).append((len(blocks), at))
                blocks.append(block)
                at += block.shape[0]
        (side,) = call(
            functools.partial(mixture_kernel, list(cameras.values()), clips, n_clip),
            [((devices, DIGITS + 1 + heads_here, LANES), F32)],
            [key_weights, pooled, *blocks],
            2 * at * d * 32,
            mib=8,
        )

    with jax.named_scope("logits"):
        came = after(exchange(message), side)
        unit, norm, exponents, assign, message = call(
            functools.partial(logits_kernel, clips, ranks, n_clip),
            [
                ((batch, bottleneck), F32),
                ((batch, LANES), F32),
                ((batch, columns), F32),
                ((batch, columns), F32),
                ((devices, 2, LANES), F32),
            ],
            [came, proto_b],
            4 * batch * bottleneck * columns,
            2 * batch * columns,
        )

    with jax.named_scope("row_total_1"):
        came = exchange(message)
        assign, message, total = call(
            second_kernel,
            [((batch, columns), F32), ((devices, 2, LANES), F32), ((batch, LANES), F32)],
            [came, assign],
            8 * batch * columns,
        )

    with jax.named_scope("row_total_2"):
        came = exchange(message)
        parity = (cam % 2).reshape(1)
        assign, keep, send, digits, prob_grad = call(
            third_kernel,
            [
                ((batch, columns), F32),
                ((batch, bottleneck // 2), F32),
                ((batch, bottleneck // 2), F32),
                (side.shape[1:], F32),
                ((batch, bottleneck), F32),
            ],
            [parity, came, assign, proto_b],
            2 * batch * bottleneck * columns,
            in_specs=[SCALARS] + [WHOLE] * 3,
        )

    with jax.named_scope("row_total_3"):
        got = lax.ppermute(send, "cam", [(i, i ^ 1) for i in range(n_cam)])
        (message,) = call(
            message_kernel,
            [((devices, batch + side.shape[1], LANES), BF16)],
            [keep, got, digits, side],
            devices * batch * LANES,
        )
        came = exchange(message)

    with jax.named_scope("outputs"):
        width = heads_here * HD
        pick = jnp.stack([clip * share // cols, cam // clips])
        proj_rows = lax.dynamic_slice_in_dim(w_proj, cam * width, width, 0)
        block = min(columns, 512)
        ins = [
            pick,
            came.reshape((clips, ranks, n_clip) + came.shape[1:]),
            unit,
            norm,
            exponents,
            assign,
            total,
            prob_grad,
            prototypes,
            scale,
            proj_rows,
        ]
        outs = [
            ((batch, columns), F32),
            ((bottleneck, columns), F32),
            ((share, bottleneck), F32),
            ((share, width), F32),
        ]
        return call(
            functools.partial(output_kernel, protos, n_cam, block),
            outs,
            ins,
            2 * batch * bottleneck * columns,
            scratch=[pltpu.VMEM(*o) for o in outs]
            + [pltpu.SemaphoreType.DMA((columns // block + 3,))],
            in_specs=[SCALARS] + [WHOLE] * (len(ins) - 1),
            out_specs=[FAR] * len(outs),
            mib=8,
        )


def solution(mesh):
    in_specs = (P("clip", "cam", None, None), P(), P(), P(), P(), P(None, ALL))
    out_specs = (P(None, ALL), P(None, ALL), P("clip", None), P("clip", "cam"))
    return jax.shard_map(local, mesh=mesh, in_specs=in_specs, out_specs=out_specs, check_vma=False)
```

```python
import functools

import jax
import jax.numpy as jnp
from jax import lax
from jax.experimental import pallas as pl
from jax.experimental.pallas import tpu as pltpu
from jax.sharding import PartitionSpec as P

HD = 64
SINK_EPS = 0.05
SOFTMAX_TEMP = 0.1
NORM_EPS = 1e-06
LANES = 128
DIGITS = 3
ALL = ("cam", "clip")
F32 = jnp.float32
BF16 = jnp.bfloat16
TRANSPOSED = (((1,), (1,)), ((), ()))
OUTER = (((0,), (0,)), ((), ()))
WHOLE = pl.BlockSpec(memory_space=pltpu.VMEM)


def call(
    kernel, outs, ins, flops, extra=0, scratch=(), grid=None, out_specs=None, in_specs=None, mib=4
):
    moved = sum(a.size * a.dtype.itemsize for a in ins)
    return pl.pallas_call(
        kernel,
        out_shape=tuple(jax.ShapeDtypeStruct(*o) for o in outs),
        in_specs=in_specs or [WHOLE] * len(ins),
        out_specs=out_specs or [WHOLE] * len(outs),
        scratch_shapes=list(scratch),
        grid=grid or (),
        compiler_params=pltpu.CompilerParams(vmem_limit_bytes=mib * 2**20),
        cost_estimate=pl.CostEstimate(flops=1, bytes_accessed=1, transcendentals=0),
    )(*ins)


def project(x, wq, wk, wv):
    q = jnp.dot(x, wq, preferred_element_type=F32).astype(BF16) * BF16(HD**-0.5)
    kt = jnp.dot(x, wk, preferred_element_type=F32).astype(BF16).T
    v = jnp.dot(x, wv, preferred_element_type=F32).astype(BF16)
    return q, kt, v


def project_kernel(blocks, *refs):
    wq, wk, wv = refs[blocks : blocks + 3]
    q_ref, kt_ref, v_ref = refs[blocks + 3 :]
    at = 0
    for x_ref in refs[:blocks]:
        rows = slice(at, at + x_ref.shape[0])
        at += x_ref.shape[0]
        q_ref[rows, :], kt_ref[:, rows], v_ref[rows, :] = project(
            x_ref[...], wq[...], wk[...], wv[...]
        )


def project_blocks(blocks, weights):
    d, cols = weights[0].shape
    rows = sum(b.shape[0] for b in blocks)
    return call(
        functools.partial(project_kernel, len(blocks)),
        [((rows, cols), BF16), ((cols, rows), BF16), ((rows, cols), BF16)],
        [*blocks, *weights],
        2 * rows * d * cols * 3,
    )


def head_of(q, head, lane):
    tile, at = divmod(head * HD, LANES)
    here = slice(tile * LANES, (tile + 1) * LANES)
    return jnp.where(lane // HD == at // HD, q[:, here], BF16(0)), here


def scores(q_head, kt):
    e = jnp.exp(jnp.dot(q_head, kt, preferred_element_type=F32))
    return e, sum(e[:, i : i + LANES] for i in range(0, e.shape[1], LANES))


def first_kernel(blocks, *refs):
    ins, (q_ref, kt_ref, v_ref, exp_ref, sum_ref) = refs[: blocks + 3], refs[blocks + 3 :]
    project_kernel(blocks, *ins, q_ref, kt_ref, v_ref)
    rows, cols = q_ref.shape
    lane = lax.broadcasted_iota(jnp.int32, (rows, LANES), 1)
    sums = jnp.zeros((rows, LANES), F32)
    for head in range(cols // HD):
        q_head, here = head_of(q_ref, head, lane)
        e, part = scores(q_head, kt_ref[here, :])
        exp_ref[head * rows : (head + 1) * rows, :] = e.astype(BF16)
        sums = jnp.where(lane == head, jnp.sum(part, axis=1, keepdims=True), sums)
    sum_ref[...] = sums


def first_blocks(blocks, weights):
    d, cols = weights[0].shape
    rows = sum(b.shape[0] for b in blocks)
    heads = cols // HD
    return call(
        functools.partial(first_kernel, len(blocks)),
        [
            ((rows, cols), BF16),
            ((cols, rows), BF16),
            ((rows, cols), BF16),
            ((heads * rows, rows), BF16),
            ((rows, LANES), F32),
        ],
        [*blocks, *weights],
        2 * rows * d * cols * 3,
        mib=4 + 8 * rows * rows // 2**20,
    )


def pool_kernel(late, step, *refs):
    q_e, kt_e, v_e, exp_e, sum_e, q_a, kt_a, v_a = refs[:8]
    x_refs, (wq, wk, wv, wp) = refs[8 : 8 + late], refs[8 + late : 12 + late]
    weight_ref, pooled_ref, message, q_s, kt_s, v_s, w_s, *buffers = refs[12 + late :]
    here_already = q_a.shape[0]
    q_s[:here_already], kt_s[:, :here_already], v_s[:here_already] = q_a[...], kt_a[...], v_a[...]
    at = here_already
    for x_ref in x_refs:
        rows = slice(at, at + x_ref.shape[0])
        at += x_ref.shape[0]
        q_s[rows, :], kt_s[:, rows], v_s[rows, :] = project(x_ref[...], wq[...], wk[...], wv[...])
    heads, total = w_s.shape
    cols = heads * HD
    first, fresh = q_e.shape[0], q_s.shape[0]
    lane_e = lax.broadcasted_iota(jnp.int32, (first, LANES), 1)
    lane_s = lax.broadcasted_iota(jnp.int32, (fresh, LANES), 1)

    inverse = None
    for head in range(heads + 1):
        new, old = buffers[2 * (head % 2) :][:2], buffers[2 * ((head + 1) % 2) :][:2]
        if head < heads:
            queries_e, here = head_of(q_e, head, lane_e)
            queries_s, _ = head_of(q_s, head, lane_s)
            total_e = jnp.zeros((first, LANES), F32)
            total_s = jnp.zeros((fresh, LANES), F32)
        for at in range(0, total, step):
            keys = slice(at, at + step)
            at_s = slice(at - first, at - first + step)
            if head < heads:
                kt = kt_e[here, keys] if at < first else kt_s[here, at_s]
                new[0][:, keys], part = scores(queries_s, kt)
                total_s = total_s + part
                if at >= first:
                    new[1][:, at_s], part = scores(queries_e, kt)
                    total_e = total_e + part
            if head > 0:
                if at < first:
                    a = exp_e[(head - 1) * first : head * first, keys].astype(F32)
                else:
                    a = old[1][:, at_s]
                a = [a * inverse[1], old[0][:, keys] * inverse[0]]
                if first == fresh:
                    a = [a[0] + a[1]]
                w = sum(jnp.sum(part, axis=0, keepdims=True) for part in a)
                w_s[head - 1 : head, keys] = w * (1.0 / total)
        if head < heads:
            total_e = jnp.sum(total_e, axis=1, keepdims=True) + sum_e[:, head : head + 1]
            inverse = 1.0 / jnp.sum(total_s, axis=1, keepdims=True), 1.0 / total_e

    weights = w_s[...].astype(BF16)
    weight_ref[...] = weights
    out = jnp.dot(weights[:, :first], v_e[...], preferred_element_type=F32)
    out = out + jnp.dot(weights[:, first:], v_s[...], preferred_element_type=F32)
    row_head = lax.broadcasted_iota(jnp.int32, out.shape, 0)
    col_head = lax.broadcasted_iota(jnp.int32, out.shape, 1) // HD
    pooled = jnp.sum(jnp.where(row_head == col_head, out, 0.0), axis=0, keepdims=True)
    pooled_ref[...] = pooled
    pooled_b = jnp.broadcast_to(pooled, (8, cols)).astype(BF16)
    embed = jnp.dot(pooled_b, wp[...], preferred_element_type=F32)[:1]
    embed = jnp.concatenate(
        [embed[:, i * LANES : (i + 1) * LANES] for i in range(message.shape[1])], axis=0
    )
    for i in range(message.shape[0]):
        message[i] = embed


def pool(early, ready, late, weights, wp, devices):
    d, cols = weights[0].shape
    heads = cols // HD
    first = early[0].shape[0]
    fresh = ready[0].shape[0] + sum(b.shape[0] for b in late)
    total = first + fresh
    bottleneck = wp.shape[1]
    pair = [pltpu.VMEM((fresh, total), F32), pltpu.VMEM((first, fresh), F32)]
    return call(
        functools.partial(pool_kernel, len(late), min(first, fresh, 256)),
        [((heads, total), BF16), ((1, cols), F32), ((devices, bottleneck // LANES, LANES), F32)],
        [*early, *ready, *late, *weights, wp],
        2 * fresh * d * cols * 3 + 2 * total * total * cols * 4,
        heads * total * total,
        scratch=[
            pltpu.VMEM((fresh, cols), BF16),
            pltpu.VMEM((cols, fresh), BF16),
            pltpu.VMEM((fresh, cols), BF16),
            pltpu.VMEM((heads, total), F32),
            *pair,
            *pair,
        ],
        mib=12 + 12 * fresh * (total + first) // 2**20,
    )


def mixture_kernel(cameras, clips, n_clip, w_ref, pooled_ref, *refs):
    x_refs, side = refs[:-1], refs[-1]
    heads, d = w_ref.shape[0], x_refs[0].shape[1]
    heads_here, share = heads // clips, d // n_clip
    mix = jnp.zeros((heads, d), F32)
    for camera in cameras:
        m = jnp.zeros((heads, d), F32)
        for block, at in camera:
            w = w_ref[:, at : at + x_refs[block].shape[0]]
            m = m + jnp.dot(w, x_refs[block][...], preferred_element_type=F32)
        mix = mix + m.astype(BF16).astype(F32)

    def lanes(x, i):
        x = x[:, i * share : (i + 1) * share]
        if share == LANES:
            return x
        return jnp.concatenate([x, jnp.zeros((x.shape[0], LANES - share), F32)], axis=1)

    for i in range(side.shape[0]):
        j, p = divmod(i % (clips * n_clip), n_clip)
        side[i] = jnp.concatenate(
            [
                jnp.zeros((DIGITS, LANES), F32),
                lanes(pooled_ref[...], i % (pooled_ref.shape[1] // share)),
                lanes(mix[j * heads_here : (j + 1) * heads_here], p),
            ],
            axis=0,
        )


FAR = pl.BlockSpec(memory_space=pltpu.HBM)


def slice_kernel(plan, *refs):
    ins = 1 + max(which for which, _ in plan)
    outs, sems = refs[ins:-1], refs[-1]
    copies = []
    for i, (which, where) in enumerate(plan):
        source = refs[which].at[where()]
        copies.append(pltpu.make_async_copy(source, outs[i], sems.at[i]))
        copies[-1].start()
    for copy in copies:
        copy.wait()


def slices(arrays, plan, shapes):
    return call(
        functools.partial(slice_kernel, plan),
        [(shape, BF16) for shape in shapes],
        [pltpu.with_memory_space_constraint(a, pltpu.HBM) for a in arrays],
        0,
        scratch=[pltpu.SemaphoreType.DMA((len(plan),))],
        in_specs=[FAR] * len(arrays),
    )


def after(x, *others):
    return lax.optimization_barrier((x, others))[0]


def token_block(s, clips, ranks):
    return 0, lambda: ((lax.axis_index("cam") // ranks + s) % clips, slice(None), slice(None))


def from_other_groups(tokens, n_cam):
    clips, tok, d = tokens.shape
    ranks = n_cam // clips
    mine, *sent = slices(
        [tokens], [token_block(s, clips, ranks) for s in range(clips)], [(tok, d)] * clips
    )
    held = []
    for s, block in enumerate(sent, 1):
        perm = [(i, ((i // ranks + s) % clips) * ranks + i % ranks) for i in range(n_cam)]
        held.append((s * ranks, lax.ppermute(block, "cam", perm)))
    return mine, held


def relay(blocks, n_cam, ranks):
    stage = list(blocks)
    for t in range(1, ranks):
        perm = [(i, (i // ranks) * ranks + (i % ranks + t) % ranks) for i in range(n_cam)]
        stage.extend((camera + t, lax.ppermute(b, "cam", perm)) for camera, b in blocks)
    return stage


def prototype_kernel(proto, scale, proto_b):
    proto_f = proto[...].astype(F32)
    norm = jnp.sqrt(jnp.sum(proto_f * proto_f, axis=0, keepdims=True) + NORM_EPS)
    scale[...] = 1.0 / norm
    proto_b[...] = (proto_f / norm).astype(BF16)


def to_lanes(column, offset=0):
    shape = (column.shape[0], LANES)
    row = lax.broadcasted_iota(jnp.int32, shape, 0) + offset
    lane = lax.broadcasted_iota(jnp.int32, shape, 1)
    return jnp.sum(jnp.where(lane == row, column, 0.0), axis=0, keepdims=True)


def from_lanes(line, size, offset=0):
    row = lax.broadcasted_iota(jnp.int32, (size, LANES), 0) + offset
    lane = lax.broadcasted_iota(jnp.int32, (size, LANES), 1)
    return jnp.sum(jnp.where(lane == row, line, 0.0), axis=1, keepdims=True)


def spread(column):
    return jnp.broadcast_to(column, (column.shape[0], LANES))


def exchange(message):
    return lax.all_to_all(message, ALL, split_axis=0, concat_axis=0, tiled=True)


def logits_kernel(
    clips, ranks, n_clip, came, proto, unit_ref, norm_ref, exp_ref, assign_ref, message
):
    rows = []
    for g in range(clips):
        for p in range(n_clip):
            z = sum(came[(g * ranks + r) * n_clip + p] for r in range(ranks))
            rows.append(jnp.concatenate([z[i : i + 1] for i in range(z.shape[0])], axis=1))
    embed = jnp.concatenate(rows, axis=0)
    norm = jnp.sqrt(jnp.sum(embed * embed, axis=1, keepdims=True) + NORM_EPS)
    unit = embed / norm
    unit_ref[...] = unit
    norm_ref[...] = spread(norm)
    logits = jnp.dot(unit.astype(BF16), proto[...], preferred_element_type=F32)
    exponents = jnp.exp(logits / SOFTMAX_TEMP)
    assign = jnp.exp(logits / SINK_EPS)
    exp_ref[...] = exponents
    assign = assign / jnp.sum(assign, axis=0, keepdims=True)
    assign_ref[...] = assign
    part = lax.dot_general(
        exponents.astype(BF16), proto[...], TRANSPOSED, preferred_element_type=F32
    )
    batch = part.shape[0]
    line = to_lanes(jnp.sum(assign, axis=1, keepdims=True)) + to_lanes(
        jnp.sum(exponents, axis=1, keepdims=True), batch
    )
    halves = part.shape[1] // LANES
    for i in range(message.shape[0]):
        if i < halves * batch:
            h, b = divmod(i, batch)
            piece = part[b : b + 1, h * LANES : (h + 1) * LANES]
        else:
            piece = jnp.zeros((1, LANES), F32)
        message[i] = jnp.concatenate([piece, line], axis=0)


def second_kernel(came, assign_ref, assign_out, message, total_ref):
    batch = assign_ref.shape[0]
    came = jnp.sum(came[...], axis=0)
    total_ref[...] = spread(from_lanes(came[1:2], batch, batch))
    assign = assign_ref[...] / from_lanes(came[1:2], batch)
    assign = assign / jnp.sum(assign, axis=0, keepdims=True)
    assign_out[...] = assign
    line = to_lanes(jnp.sum(assign, axis=1, keepdims=True))
    out = jnp.concatenate([came[0:1], line], axis=0)
    for i in range(message.shape[0]):
        message[i] = out


def third_kernel(
    came, assign_ref, proto, assign_out, keep_ref, send_ref, digits_ref, grad_ref
):
    batch = assign_ref.shape[0]
    halves = proto.shape[0] // LANES
    total = jnp.sum(came[...], axis=0)[1:2]
    assign = assign_ref[...] / from_lanes(total, batch)
    assign = assign / jnp.sum(assign, axis=0, keepdims=True)
    assign_out[...] = assign
    part = lax.dot_general(
        assign.astype(BF16), proto[...], TRANSPOSED, preferred_element_type=F32
    )
    half = part.shape[1] // 2
    odd = lax.axis_index("cam") % 2 == 1
    low, high = part[:, :half], part[:, half:]
    keep_ref[...] = jnp.where(odd, high, low)
    send_ref[...] = jnp.where(odd, low, high)
    rest = to_lanes(jnp.sum(assign, axis=1, keepdims=True))
    digits_ref[...] = jnp.zeros(digits_ref.shape, F32)
    for i in range(DIGITS):
        digit = rest.astype(BF16).astype(F32)
        digits_ref[i : i + 1, :] = digit
        rest = rest - digit
    for h in range(halves):
        for b in range(batch):
            grad_ref[b : b + 1, h * LANES : (h + 1) * LANES] = came[h * batch + b][0:1]


def message_kernel(keep, got, digits, side, message):
    part = (keep[...] + got[...]).astype(BF16)
    batch = part.shape[0]
    message[:, :batch, :] = jnp.broadcast_to(part[None], (message.shape[0],) + part.shape)
    message[:, batch:, :] = (side[...] + digits[...][None]).astype(BF16)


def output_kernel(
    protos,
    n_cam,
    block,
    came,
    unit_ref,
    norm_ref,
    exp_ref,
    assign_ref,
    total_ref,
    prob_grad,
    proto,
    scale,
    wp,
    codes_out,
    proto_grad_out,
    grad_proj_out,
    grad_value_out,
    codes,
    proto_grad,
    grad_proj,
    grad_value,
    sems,
):
    clips, ranks, n_clip = came.shape[:3]
    batch, columns = exp_ref.shape
    share = grad_proj.shape[0]
    cols = clips * wp.shape[0]
    copies = []

    def send(source, target):
        copies.append(pltpu.make_async_copy(source, target, sems.at[len(copies)]))
        copies[-1].start()

    sums = [jnp.zeros(came.shape[3:], F32) for _ in range(2)]
    for cam in range(n_cam):
        part = jnp.sum(came[cam // ranks, cam % ranks].astype(F32), axis=0)
        sums[cam % 2] = sums[cam % 2] + part
    line = jnp.sum((sums[0] + sums[1])[batch : batch + DIGITS], axis=0, keepdims=True)
    by_assign = protos / from_lanes(line, batch)
    by_prob = protos / total_ref[:, :1]
    unit = unit_ref[...]
    unit_b = unit.astype(BF16)

    for start in range(0, columns, block):
        here = slice(start, start + block)
        assign = assign_ref[:, here] * by_assign
        grad_logits = (exp_ref[:, here] * by_prob - assign).astype(BF16)
        for g in range(clips):
            for p in range(n_clip):
                row, to = g * n_clip + p, p * clips + g
                codes[to : to + 1, here] = assign[row : row + 1]
        grad = lax.dot_general(unit_b, grad_logits, OUTER, preferred_element_type=F32)
        inverse = scale[:, here]
        unit_proto = proto[:, here].astype(F32) * inverse
        along = jnp.sum(unit_proto * grad, axis=0, keepdims=True)
        proto_grad[:, here] = (grad - unit_proto * along) * inverse
        send(proto_grad.at[:, here], proto_grad_out.at[:, here])
    send(codes, codes_out)

    assign_grad = jnp.concatenate([s[:batch] for s in sums], axis=1)
    grad_unit = prob_grad[...] * by_prob - assign_grad * by_assign
    grad_embed = (
        grad_unit - unit * jnp.sum(unit * grad_unit, axis=1, keepdims=True)
    ) / norm_ref[:, :1]
    grad_embed = grad_embed.astype(BF16)

    def rows(rank, row):
        picked = [came[g, rank].astype(F32)[:, row, :] for g in range(clips)]
        return jnp.concatenate(picked, axis=0)[:, :share].astype(BF16)

    grad_proj[...] = lax.dot_general(
        rows(lax.axis_index("clip") * share // cols, batch + DIGITS), grad_embed, OUTER, preferred_element_type=F32
    )
    send(grad_proj, grad_proj_out)
    grad_pooled = lax.dot_general(
        grad_embed, wp[...], TRANSPOSED, preferred_element_type=F32
    ).astype(BF16)
    col_head = lax.broadcasted_iota(jnp.int32, grad_value.shape, 1) // HD
    value = jnp.zeros(grad_value.shape, F32)
    for head in range(grad_value.shape[1] // HD):
        mixed = rows(lax.axis_index("cam") // clips, batch + DIGITS + 1 + head)
        out = lax.dot_general(mixed, grad_pooled, OUTER, preferred_element_type=F32)
        value = jnp.where(col_head == head, out, value)
    grad_value[...] = value
    send(grad_value, grad_value_out)
    for copy in copies:
        copy.wait()


def local(tokens, w_query, w_key, w_value, w_proj, prototypes):
    clips, _, tok, d = tokens.shape
    n_cam, n_clip = lax.axis_size("cam"), lax.axis_size("clip")
    devices = n_cam * n_clip
    ranks = n_cam // clips
    batch = clips * n_clip
    cols = d // ranks
    heads = cols // HD
    heads_here = heads // clips
    share = d // n_clip
    bottleneck, columns = prototypes.shape
    protos = columns * devices
    width = heads_here * HD

    with jax.named_scope("tokens_of_a_clip"):
        tokens = tokens.reshape(clips, tok, d)
        mine, held = from_other_groups(tokens, n_cam)

    with jax.named_scope("prototypes"):
        scale, proto_b = call(
            prototype_kernel,
            [((1, columns), F32), ((bottleneck, columns), BF16)],
            [prototypes],
            4 * bottleneck * columns,
            mib=8,
        )

    with jax.named_scope("pooling"):
        def columns_of():
            start = lax.axis_index("cam") % ranks * cols
            return slice(None), pl.ds(pl.multiple_of(start, cols), cols)

        def rows_of():
            start = lax.axis_index("cam") % ranks * cols
            return pl.ds(pl.multiple_of(start, cols), cols), slice(None)

        def heads_of():
            start = lax.axis_index("cam") * width
            return pl.ds(pl.multiple_of(start, width), width), slice(None)

        *weights, wp, proj_rows = slices(
            [w_query, w_key, w_value, w_proj],
            [(i, columns_of) for i in range(3)] + [(3, rows_of), (3, heads_of)],
            [(d, cols)] * 3 + [(cols, bottleneck), (width, bottleneck)],
        )
        stages = [relay([(0, mine)], n_cam, ranks)]
        early = first_blocks([b for _, b in stages[0]], weights)
        held = [(camera, after(b, proto_b, *early)) for camera, b in held]
        stages.append(relay(held, n_cam, ranks))
        ready = project_blocks([b for _, b in held], weights)
        late = [b for _, b in stages[1][len(held) :]]
        key_weights, pooled, message = pool(early, ready, late, weights, wp, devices)

    with jax.named_scope("mixtures"):
        cameras, blocks, at = {}, [], 0
        for stage in stages:
            for camera, block in stage:
                cameras.setdefault(camera, []).append((len(blocks), at))
                blocks.append(block)
                at += block.shape[0]
        (side,) = call(
            functools.partial(mixture_kernel, list(cameras.values()), clips, n_clip),
            [((devices, DIGITS + 1 + heads_here, LANES), F32)],
            [key_weights, pooled, *blocks],
            2 * at * d * 32,
            mib=8,
        )

    with jax.named_scope("logits"):
        came = after(exchange(message), side)
        unit, norm, exponents, assign, message = call(
            functools.partial(logits_kernel, clips, ranks, n_clip),
            [
                ((batch, bottleneck), F32),
                ((batch, LANES), F32),
                ((batch, columns), F32),
                ((batch, columns), F32),
                ((devices, 2, LANES), F32),
            ],
            [came, proto_b],
            4 * batch * bottleneck * columns,
            2 * batch * columns,
        )

    with jax.named_scope("row_total_1"):
        came = exchange(message)
        assign, message, total = call(
            second_kernel,
            [((batch, columns), F32), ((devices, 2, LANES), F32), ((batch, LANES), F32)],
            [came, assign],
            8 * batch * columns,
        )

    with jax.named_scope("row_total_2"):
        came = exchange(message)
        assign, keep, send, digits, prob_grad = call(
            third_kernel,
            [
                ((batch, columns), F32),
                ((batch, bottleneck // 2), F32),
                ((batch, bottleneck // 2), F32),
                (side.shape[1:], F32),
                ((batch, bottleneck), F32),
            ],
            [came, assign, proto_b],
            2 * batch * bottleneck * columns,
        )

    with jax.named_scope("row_total_3"):
        got = lax.ppermute(send, "cam", [(i, i ^ 1) for i in range(n_cam)])
        (message,) = call(
            message_kernel,
            [((devices, batch + side.shape[1], LANES), BF16)],
            [keep, got, digits, side],
            devices * batch * LANES,
        )
        came = exchange(after(message, proj_rows))

    with jax.named_scope("outputs"):
        block = min(columns, 512)
        ins = [
            came.reshape((clips, ranks, n_clip) + came.shape[1:]),
            unit,
            norm,
            exponents,
            assign,
            total,
            prob_grad,
            prototypes,
            scale,
            proj_rows,
        ]
        outs = [
            ((batch, columns), F32),
            ((bottleneck, columns), F32),
            ((share, bottleneck), F32),
            ((share, width), F32),
        ]
        return call(
            functools.partial(output_kernel, protos, n_cam, block),
            outs,
            ins,
            2 * batch * bottleneck * columns,
            scratch=[pltpu.VMEM(*o) for o in outs]
            + [pltpu.SemaphoreType.DMA((columns // block + 3,))],
            out_specs=[FAR] * len(outs),
            mib=8,
        )


def solution(mesh):
    in_specs = (P("clip", "cam", None, None), P(), P(), P(), P(), P(None, ALL))
    out_specs = (P(None, ALL), P(None, ALL), P("clip", None), P("clip", "cam"))
    return jax.shard_map(local, mesh=mesh, in_specs=in_specs, out_specs=out_specs, check_vma=False)
```

```python
import functools

import jax
import jax.numpy as jnp
from jax import lax
from jax.experimental import pallas as pl
from jax.experimental.pallas import tpu as pltpu
from jax.sharding import PartitionSpec as P

HD = 64
SINK_EPS = 0.05
SOFTMAX_TEMP = 0.1
NORM_EPS = 1e-06
LANES = 128
DIGITS = 3
ALL = ("cam", "clip")
F32 = jnp.float32
BF16 = jnp.bfloat16
TRANSPOSED = (((1,), (1,)), ((), ()))
OUTER = (((0,), (0,)), ((), ()))
WHOLE = pl.BlockSpec(memory_space=pltpu.VMEM)


def call(
    kernel, outs, ins, flops, extra=0, scratch=(), grid=None, out_specs=None, in_specs=None, mib=4
):
    moved = sum(a.size * a.dtype.itemsize for a in ins)
    return pl.pallas_call(
        kernel,
        out_shape=tuple(jax.ShapeDtypeStruct(*o) for o in outs),
        in_specs=in_specs or [WHOLE] * len(ins),
        out_specs=out_specs or [WHOLE] * len(outs),
        scratch_shapes=list(scratch),
        grid=grid or (),
        compiler_params=pltpu.CompilerParams(vmem_limit_bytes=mib * 2**20),
        cost_estimate=pl.CostEstimate(flops=1, bytes_accessed=1, transcendentals=0),
    )(*ins)


def project(x, wq, wk, wv):
    q = jnp.dot(x, wq, preferred_element_type=F32).astype(BF16) * BF16(HD**-0.5)
    kt = jnp.dot(x, wk, preferred_element_type=F32).astype(BF16).T
    v = jnp.dot(x, wv, preferred_element_type=F32).astype(BF16)
    return q, kt, v


def project_kernel(blocks, *refs):
    wq, wk, wv = refs[blocks : blocks + 3]
    q_ref, kt_ref, v_ref = refs[blocks + 3 :]
    x = jnp.concatenate([x_ref[...] for x_ref in refs[:blocks]], axis=0)
    q_ref[...], kt_ref[...], v_ref[...] = project(x, wq[...], wk[...], wv[...])


def project_blocks(blocks, weights):
    d, cols = weights[0].shape
    rows = sum(b.shape[0] for b in blocks)
    return call(
        functools.partial(project_kernel, len(blocks)),
        [((rows, cols), BF16), ((cols, rows), BF16), ((rows, cols), BF16)],
        [*blocks, *weights],
        2 * rows * d * cols * 3,
    )


def head_of(q, head, lane):
    tile, at = divmod(head * HD, LANES)
    here = slice(tile * LANES, (tile + 1) * LANES)
    return jnp.where(lane // HD == at // HD, q[:, here], BF16(0)), here


def scores(q_head, kt):
    e = jnp.exp(jnp.dot(q_head, kt, preferred_element_type=F32))
    return e, sum(e[:, i : i + LANES] for i in range(0, e.shape[1], LANES))


def first_kernel(blocks, *refs):
    ins, (q_ref, kt_ref, v_ref, exp_ref, sum_ref) = refs[: blocks + 3], refs[blocks + 3 :]
    project_kernel(blocks, *ins, q_ref, kt_ref, v_ref)
    rows, cols = q_ref.shape
    lane = lax.broadcasted_iota(jnp.int32, (rows, LANES), 1)
    sums = jnp.zeros((rows, LANES), F32)
    for head in range(cols // HD):
        q_head, here = head_of(q_ref, head, lane)
        e, part = scores(q_head, kt_ref[here, :])
        exp_ref[head * rows : (head + 1) * rows, :] = e.astype(BF16)
        sums = jnp.where(lane == head, jnp.sum(part, axis=1, keepdims=True), sums)
    sum_ref[...] = sums


def first_blocks(blocks, weights):
    d, cols = weights[0].shape
    rows = sum(b.shape[0] for b in blocks)
    heads = cols // HD
    return call(
        functools.partial(first_kernel, len(blocks)),
        [
            ((rows, cols), BF16),
            ((cols, rows), BF16),
            ((rows, cols), BF16),
            ((heads * rows, rows), BF16),
            ((rows, LANES), F32),
        ],
        [*blocks, *weights],
        2 * rows * d * cols * 3,
        mib=4 + 8 * rows * rows // 2**20,
    )


def next_kernel(blocks, q_e, kt_e, sum_e, *refs):
    ins, outs = refs[: blocks + 3], refs[blocks + 3 :]
    q_n, kt_n, v_n, exp_n, exp_x, sum_n, sum_ref = outs
    project_kernel(blocks, *ins, q_n, kt_n, v_n)
    rows, cols = q_n.shape
    first = q_e.shape[0]
    lane_n = lax.broadcasted_iota(jnp.int32, (rows, LANES), 1)
    lane_e = lax.broadcasted_iota(jnp.int32, (first, LANES), 1)
    sums_n, sums_e = jnp.zeros((rows, LANES), F32), sum_e[...]
    for head in range(cols // HD):
        queries_n, here = head_of(q_n, head, lane_n)
        queries_e, _ = head_of(q_e, head, lane_e)
        a, part_a = scores(queries_n, kt_e[here, :])
        b, part_b = scores(queries_n, kt_n[here, :])
        x, part_x = scores(queries_e, kt_n[here, :])
        exp_n[head * rows : (head + 1) * rows, :first] = a.astype(BF16)
        exp_n[head * rows : (head + 1) * rows, first:] = b.astype(BF16)
        exp_x[head * first : (head + 1) * first, :] = x.astype(BF16)
        part = jnp.sum(part_a + part_b, axis=1, keepdims=True)
        sums_n = jnp.where(lane_n == head, part, sums_n)
        part = jnp.sum(part_x, axis=1, keepdims=True)
        sums_e = sums_e + jnp.where(lane_e == head, part, 0.0)
    sum_n[...] = sums_n
    sum_ref[...] = sums_e


def next_blocks(blocks, early, weights):
    q_e, kt_e, _, _, sum_e = early
    d, cols = weights[0].shape
    first = q_e.shape[0]
    rows = sum(b.shape[0] for b in blocks)
    heads = cols // HD
    return call(
        functools.partial(next_kernel, len(blocks)),
        [
            ((rows, cols), BF16),
            ((cols, rows), BF16),
            ((rows, cols), BF16),
            ((heads * rows, first + rows), BF16),
            ((heads * first, rows), BF16),
            ((rows, LANES), F32),
            ((first, LANES), F32),
        ],
        [q_e, kt_e, sum_e, *blocks, *weights],
        2 * rows * d * cols * 3,
        mib=4 + 24 * first * rows // 2**20,
    )


def pool_kernel(late, *refs):
    (q_e, kt_e, v_e, exp_e), refs = refs[:4], refs[4:]
    (q_n, kt_n, v_n, exp_n, exp_x, sum_n, sum_e), refs = refs[:7], refs[7:]
    (q_a, kt_a, v_a), refs = refs[:3], refs[3:]
    x_refs, (wq, wk, wv, wp) = refs[:late], refs[late : 4 + late]
    weight_ref, pooled_ref, message, q_s, kt_s, v_s, w_s = refs[4 + late :]
    at = q_a.shape[0]
    q_s[:at], kt_s[:, :at], v_s[:at] = q_a[...], kt_a[...], v_a[...]
    for x_ref in x_refs:
        rows = slice(at, at + x_ref.shape[0])
        at += x_ref.shape[0]
        q_s[rows, :], kt_s[:, rows], v_s[rows, :] = project(x_ref[...], wq[...], wk[...], wv[...])
    heads, total = w_s.shape
    cols = heads * HD
    first, then, fresh = q_e.shape[0], q_n.shape[0], q_s.shape[0]
    bounds = [0, first, first + then, total]

    def lanes(rows):
        return lax.broadcasted_iota(jnp.int32, (rows, LANES), 1)

    @pl.loop(0, cols // LANES)
    def _(tile):
        here = pl.ds(pl.multiple_of(tile * LANES, LANES), LANES)
        for e in range(LANES // HD):
            head = tile * (LANES // HD) + e

            def exps(q, kt):
                q_head = jnp.where(lanes(q.shape[0]) // HD == e, q[:, here], BF16(0))
                return jnp.exp(jnp.dot(q_head, kt[here, :], preferred_element_type=F32))

            def row_sum(a):
                return jnp.sum(a, axis=1, keepdims=True)

            def known(sums):
                return row_sum(jnp.where(lanes(sums.shape[0]) == head, sums[...], 0.0))

            def kept(a, rows, keys):
                return a[pl.ds(pl.multiple_of(head * rows, rows), rows), keys].astype(F32)

            new = [exps(q_s, kt) for kt in (kt_e, kt_n, kt_s)]
            e_s, n_s = exps(q_e, kt_s), exps(q_n, kt_s)
            by_s = 1.0 / sum(row_sum(a) for a in new)
            by_e = 1.0 / (known(sum_e) + row_sum(e_s))
            by_n = 1.0 / (known(sum_n) + row_sum(n_s))
            columns = [
                (new[0], kept(exp_e, first, slice(None)), kept(exp_n, then, slice(0, first))),
                (new[1], kept(exp_x, first, slice(None)), kept(exp_n, then, slice(first, None))),
                (new[2], e_s, n_s),
            ]
            for i, parts in enumerate(columns):
                w = sum(
                    jnp.sum(a * by, axis=0, keepdims=True)
                    for a, by in zip(parts, (by_s, by_e, by_n))
                )
                w_s[pl.ds(head, 1), bounds[i] : bounds[i + 1]] = w * (1.0 / total)

    weights = w_s[...].astype(BF16)
    weight_ref[...] = weights
    out = sum(
        jnp.dot(weights[:, bounds[i] : bounds[i + 1]], v[...], preferred_element_type=F32)
        for i, v in enumerate((v_e, v_n, v_s))
    )
    row_head = lax.broadcasted_iota(jnp.int32, out.shape, 0)
    col_head = lax.broadcasted_iota(jnp.int32, out.shape, 1) // HD
    pooled = jnp.sum(jnp.where(row_head == col_head, out, 0.0), axis=0, keepdims=True)
    pooled_ref[...] = pooled
    pooled_b = jnp.broadcast_to(pooled, (8, cols)).astype(BF16)
    embed = jnp.dot(pooled_b, wp[...], preferred_element_type=F32)[:1]
    embed = jnp.concatenate(
        [embed[:, i * LANES : (i + 1) * LANES] for i in range(message.shape[1])], axis=0
    )
    for i in range(message.shape[0]):
        message[i] = embed


def pool(early, after_early, ready, late, weights, wp, devices):
    d, cols = weights[0].shape
    heads = cols // HD
    first, then = early[0].shape[0], after_early[0].shape[0]
    fresh = ready[0].shape[0] + sum(b.shape[0] for b in late)
    total = first + then + fresh
    bottleneck = wp.shape[1]
    return call(
        functools.partial(pool_kernel, len(late)),
        [((heads, total), BF16), ((1, cols), F32), ((devices, bottleneck // LANES, LANES), F32)],
        [*early[:4], *after_early, *ready, *late, *weights, wp],
        2 * fresh * d * cols * 3 + 2 * total * total * cols * 4,
        heads * total * total,
        scratch=[
            pltpu.VMEM((fresh, cols), BF16),
            pltpu.VMEM((cols, fresh), BF16),
            pltpu.VMEM((fresh, cols), BF16),
            pltpu.VMEM((heads, total), F32),
        ],
        mib=6 + 40 * fresh * total // 2**20,
    )


def mixture_kernel(cameras, clips, n_clip, w_ref, pooled_ref, *refs):
    x_refs, side = refs[:-1], refs[-1]
    heads, d = w_ref.shape[0], x_refs[0].shape[1]
    heads_here, share = heads // clips, d // n_clip
    mix = jnp.zeros((heads, d), F32)
    for camera in cameras:
        m = jnp.zeros((heads, d), F32)
        for block, at in camera:
            w = w_ref[:, at : at + x_refs[block].shape[0]]
            m = m + jnp.dot(w, x_refs[block][...], preferred_element_type=F32)
        mix = mix + m.astype(BF16).astype(F32)

    def lanes(x, i):
        x = x[:, i * share : (i + 1) * share]
        if share == LANES:
            return x
        return jnp.concatenate([x, jnp.zeros((x.shape[0], LANES - share), F32)], axis=1)

    for i in range(side.shape[0]):
        j, p = divmod(i % (clips * n_clip), n_clip)
        side[i] = jnp.concatenate(
            [
                jnp.zeros((DIGITS, LANES), F32),
                lanes(pooled_ref[...], i % (pooled_ref.shape[1] // share)),
                lanes(mix[j * heads_here : (j + 1) * heads_here], p),
            ],
            axis=0,
        )


FAR = pl.BlockSpec(memory_space=pltpu.HBM)


def slice_kernel(plan, *refs):
    ins = 1 + max(which for which, _ in plan)
    outs, sems = refs[ins:-1], refs[-1]
    copies = []
    for i, (which, where) in enumerate(plan):
        source = refs[which].at[where()]
        copies.append(pltpu.make_async_copy(source, outs[i], sems.at[i]))
        copies[-1].start()
    for copy in copies:
        copy.wait()


def slices(arrays, plan, shapes):
    return call(
        functools.partial(slice_kernel, plan),
        [(shape, BF16) for shape in shapes],
        [pltpu.with_memory_space_constraint(a, pltpu.HBM) for a in arrays],
        0,
        scratch=[pltpu.SemaphoreType.DMA((len(plan),))],
        in_specs=[FAR] * len(arrays),
    )


def after(x, *others):
    return lax.optimization_barrier((x, others))[0]


def token_block(s, clips, ranks, start, size):
    rows = pl.ds(start, size)
    return 0, lambda: ((lax.axis_index("cam") // ranks + s) % clips, rows, slice(None))


def from_other_groups(tokens, n_cam):
    clips, tok, d = tokens.shape
    ranks = n_cam // clips
    half = tok // 2
    pieces = [(s, c) for c in range(2) for s in range(1, clips)]
    mine, *sent = slices(
        [tokens],
        [token_block(0, clips, ranks, 0, tok)]
        + [token_block(s, clips, ranks, c * half, half) for s, c in pieces],
        [(tok, d)] + [(half, d)] * len(pieces),
    )
    held = [[], []]
    for (s, c), block in zip(pieces, sent):
        perm = [
            (i, ((i // ranks + s) % clips) * ranks + (i % ranks + c) % ranks) for i in range(n_cam)
        ]
        held[c].append((s * ranks + c % ranks, lax.ppermute(block, "cam", perm)))
    return mine, *held


def relay(blocks, n_cam, ranks, cuts=1):
    stage = list(blocks)
    size = blocks[0][1].shape[0] // cuts
    blocks = [(camera, b[i * size : (i + 1) * size]) for camera, b in blocks for i in range(cuts)]
    for t in range(1, ranks):
        perm = [(i, (i // ranks) * ranks + (i % ranks + t) % ranks) for i in range(n_cam)]
        for camera, b in blocks:
            label = camera // ranks * ranks + (camera + t) % ranks
            stage.append((label, lax.ppermute(b, "cam", perm)))
    return stage


def prototype_kernel(proto, scale, proto_b):
    proto_f = proto[...].astype(F32)
    norm = jnp.sqrt(jnp.sum(proto_f * proto_f, axis=0, keepdims=True) + NORM_EPS)
    scale[...] = 1.0 / norm
    proto_b[...] = (proto_f / norm).astype(BF16)


def to_lanes(column, offset=0):
    shape = (column.shape[0], LANES)
    row = lax.broadcasted_iota(jnp.int32, shape, 0) + offset
    lane = lax.broadcasted_iota(jnp.int32, shape, 1)
    return jnp.sum(jnp.where(lane == row, column, 0.0), axis=0, keepdims=True)


def from_lanes(line, size, offset=0):
    row = lax.broadcasted_iota(jnp.int32, (size, LANES), 0) + offset
    lane = lax.broadcasted_iota(jnp.int32, (size, LANES), 1)
    return jnp.sum(jnp.where(lane == row, line, 0.0), axis=1, keepdims=True)


def spread(column):
    return jnp.broadcast_to(column, (column.shape[0], LANES))


def exchange(message):
    return lax.all_to_all(message, ALL, split_axis=0, concat_axis=0, tiled=True)


def logits_kernel(
    clips, ranks, n_clip, came, proto, unit_ref, norm_ref, exp_ref, assign_ref, message
):
    rows = []
    for g in range(clips):
        for p in range(n_clip):
            z = sum(came[(g * ranks + r) * n_clip + p] for r in range(ranks))
            rows.append(jnp.concatenate([z[i : i + 1] for i in range(z.shape[0])], axis=1))
    embed = jnp.concatenate(rows, axis=0)
    norm = jnp.sqrt(jnp.sum(embed * embed, axis=1, keepdims=True) + NORM_EPS)
    unit = embed / norm
    unit_ref[...] = unit
    norm_ref[...] = spread(norm)
    logits = jnp.dot(unit.astype(BF16), proto[...], preferred_element_type=F32)
    exponents = jnp.exp(logits / SOFTMAX_TEMP)
    assign = jnp.exp(logits / SINK_EPS)
    exp_ref[...] = exponents
    assign = assign / jnp.sum(assign, axis=0, keepdims=True)
    assign_ref[...] = assign
    part = lax.dot_general(
        exponents.astype(BF16), proto[...], TRANSPOSED, preferred_element_type=F32
    )
    batch = part.shape[0]
    line = to_lanes(jnp.sum(assign, axis=1, keepdims=True)) + to_lanes(
        jnp.sum(exponents, axis=1, keepdims=True), batch
    )
    halves = part.shape[1] // LANES
    for i in range(message.shape[0]):
        if i < halves * batch:
            h, b = divmod(i, batch)
            piece = part[b : b + 1, h * LANES : (h + 1) * LANES]
        else:
            piece = jnp.zeros((1, LANES), F32)
        message[i] = jnp.concatenate([piece, line], axis=0)


def second_kernel(came, assign_ref, assign_out, message, total_ref):
    batch = assign_ref.shape[0]
    came = jnp.sum(came[...], axis=0)
    total_ref[...] = spread(from_lanes(came[1:2], batch, batch))
    assign = assign_ref[...] / from_lanes(came[1:2], batch)
    assign = assign / jnp.sum(assign, axis=0, keepdims=True)
    assign_out[...] = assign
    line = to_lanes(jnp.sum(assign, axis=1, keepdims=True))
    out = jnp.concatenate([came[0:1], line], axis=0)
    for i in range(message.shape[0]):
        message[i] = out


def third_kernel(
    came, assign_ref, proto, assign_out, keep_ref, send_ref, digits_ref, grad_ref
):
    batch = assign_ref.shape[0]
    halves = proto.shape[0] // LANES
    total = jnp.sum(came[...], axis=0)[1:2]
    assign = assign_ref[...] / from_lanes(total, batch)
    assign = assign / jnp.sum(assign, axis=0, keepdims=True)
    assign_out[...] = assign
    part = lax.dot_general(
        assign.astype(BF16), proto[...], TRANSPOSED, preferred_element_type=F32
    )
    half = part.shape[1] // 2
    odd = lax.axis_index("cam") % 2 == 1
    low, high = part[:, :half], part[:, half:]
    keep_ref[...] = jnp.where(odd, high, low)
    send_ref[...] = jnp.where(odd, low, high)
    rest = to_lanes(jnp.sum(assign, axis=1, keepdims=True))
    digits_ref[...] = jnp.zeros(digits_ref.shape, F32)
    for i in range(DIGITS):
        digit = rest.astype(BF16).astype(F32)
        digits_ref[i : i + 1, :] = digit
        rest = rest - digit
    for h in range(halves):
        for b in range(batch):
            grad_ref[b : b + 1, h * LANES : (h + 1) * LANES] = came[h * batch + b][0:1]


def message_kernel(keep, got, digits, side, message):
    part = (keep[...] + got[...]).astype(BF16)
    batch = part.shape[0]
    message[:, :batch, :] = jnp.broadcast_to(part[None], (message.shape[0],) + part.shape)
    message[:, batch:, :] = (side[...] + digits[...][None]).astype(BF16)


def output_kernel(
    protos,
    n_cam,
    block,
    came,
    unit_ref,
    norm_ref,
    exp_ref,
    assign_ref,
    total_ref,
    prob_grad,
    proto,
    scale,
    wp,
    codes_out,
    proto_grad_out,
    grad_proj_out,
    grad_value_out,
    codes,
    proto_grad,
    grad_proj,
    grad_value,
    sems,
):
    clips, ranks, n_clip = came.shape[:3]
    batch, columns = exp_ref.shape
    share = grad_proj.shape[0]
    cols = clips * wp.shape[0]
    copies = []

    def send(source, target):
        copies.append(pltpu.make_async_copy(source, target, sems.at[len(copies)]))
        copies[-1].start()

    sums = [jnp.zeros(came.shape[3:], F32) for _ in range(2)]
    for cam in range(n_cam):
        part = jnp.sum(came[cam // ranks, cam % ranks].astype(F32), axis=0)
        sums[cam % 2] = sums[cam % 2] + part
    line = jnp.sum((sums[0] + sums[1])[batch : batch + DIGITS], axis=0, keepdims=True)
    by_assign = protos / from_lanes(line, batch)
    by_prob = protos / total_ref[:, :1]
    unit = unit_ref[...]
    unit_b = unit.astype(BF16)

    for start in range(0, columns, block):
        here = slice(start, start + block)
        assign = assign_ref[:, here] * by_assign
        grad_logits = (exp_ref[:, here] * by_prob - assign).astype(BF16)
        for g in range(clips):
            for p in range(n_clip):
                row, to = g * n_clip + p, p * clips + g
                codes[to : to + 1, here] = assign[row : row + 1]
        grad = lax.dot_general(unit_b, grad_logits, OUTER, preferred_element_type=F32)
        inverse = scale[:, here]
        unit_proto = proto[:, here].astype(F32) * inverse
        along = jnp.sum(unit_proto * grad, axis=0, keepdims=True)
        proto_grad[:, here] = (grad - unit_proto * along) * inverse
        send(proto_grad.at[:, here], proto_grad_out.at[:, here])
    send(codes, codes_out)

    assign_grad = jnp.concatenate([s[:batch] for s in sums], axis=1)
    grad_unit = prob_grad[...] * by_prob - assign_grad * by_assign
    grad_embed = (
        grad_unit - unit * jnp.sum(unit * grad_unit, axis=1, keepdims=True)
    ) / norm_ref[:, :1]
    grad_embed = grad_embed.astype(BF16)

    def rows(rank, row):
        picked = [came[g, rank].astype(F32)[:, row, :] for g in range(clips)]
        return jnp.concatenate(picked, axis=0)[:, :share].astype(BF16)

    grad_proj[...] = lax.dot_general(
        rows(lax.axis_index("clip") * share // cols, batch + DIGITS), grad_embed, OUTER, preferred_element_type=F32
    )
    send(grad_proj, grad_proj_out)
    grad_pooled = lax.dot_general(
        grad_embed, wp[...], TRANSPOSED, preferred_element_type=F32
    ).astype(BF16)
    col_head = lax.broadcasted_iota(jnp.int32, grad_value.shape, 1) // HD
    value = jnp.zeros(grad_value.shape, F32)
    for head in range(grad_value.shape[1] // HD):
        mixed = rows(lax.axis_index("cam") // clips, batch + DIGITS + 1 + head)
        out = lax.dot_general(mixed, grad_pooled, OUTER, preferred_element_type=F32)
        value = jnp.where(col_head == head, out, value)
    grad_value[...] = value
    send(grad_value, grad_value_out)
    for copy in copies:
        copy.wait()


def local(tokens, w_query, w_key, w_value, w_proj, prototypes):
    clips, _, tok, d = tokens.shape
    n_cam, n_clip = lax.axis_size("cam"), lax.axis_size("clip")
    devices = n_cam * n_clip
    ranks = n_cam // clips
    batch = clips * n_clip
    cols = d // ranks
    heads = cols // HD
    heads_here = heads // clips
    share = d // n_clip
    bottleneck, columns = prototypes.shape
    protos = columns * devices
    width = heads_here * HD

    with jax.named_scope("tokens_of_a_clip"):
        tokens = tokens.reshape(clips, tok, d)
        mine, half, rest = from_other_groups(tokens, n_cam)

    with jax.named_scope("prototypes"):
        scale, proto_b = call(
            prototype_kernel,
            [((1, columns), F32), ((bottleneck, columns), BF16)],
            [prototypes],
            4 * bottleneck * columns,
            mib=8,
        )

    with jax.named_scope("pooling"):
        def columns_of():
            start = lax.axis_index("cam") % ranks * cols
            return slice(None), pl.ds(pl.multiple_of(start, cols), cols)

        def rows_of():
            start = lax.axis_index("cam") % ranks * cols
            return pl.ds(pl.multiple_of(start, cols), cols), slice(None)

        def heads_of():
            start = lax.axis_index("cam") * width
            return pl.ds(pl.multiple_of(start, width), width), slice(None)

        *weights, wp, proj_rows = slices(
            [w_query, w_key, w_value, w_proj],
            [(i, columns_of) for i in range(3)] + [(3, rows_of), (3, heads_of)],
            [(d, cols)] * 3 + [(cols, bottleneck), (width, bottleneck)],
        )
        stages = [relay([(0, mine)], n_cam, ranks)]
        early = first_blocks([b for _, b in stages[0]], weights)
        half = [(camera, after(b, proto_b, *early)) for camera, b in half]
        stages.append(relay(half, n_cam, ranks, 2))
        then = next_blocks([b for _, b in stages[1]], early, weights)
        rest = [(camera, after(b, *then)) for camera, b in rest]
        stages.append(relay(rest, n_cam, ranks))
        ready = project_blocks([b for _, b in rest], weights)
        late = [b for _, b in stages[2][len(rest) :]]
        key_weights, pooled, message = pool(early, then, ready, late, weights, wp, devices)

    with jax.named_scope("mixtures"):
        cameras, blocks, at = {}, [], 0
        for stage in stages:
            for camera, block in stage:
                cameras.setdefault(camera, []).append((len(blocks), at))
                blocks.append(block)
                at += block.shape[0]
        (side,) = call(
            functools.partial(mixture_kernel, list(cameras.values()), clips, n_clip),
            [((devices, DIGITS + 1 + heads_here, LANES), F32)],
            [key_weights, pooled, *blocks],
            2 * at * d * 32,
            mib=8,
        )

    with jax.named_scope("logits"):
        came = after(exchange(message), side)
        unit, norm, exponents, assign, message = call(
            functools.partial(logits_kernel, clips, ranks, n_clip),
            [
                ((batch, bottleneck), F32),
                ((batch, LANES), F32),
                ((batch, columns), F32),
                ((batch, columns), F32),
                ((devices, 2, LANES), F32),
            ],
            [came, proto_b],
            4 * batch * bottleneck * columns,
            2 * batch * columns,
        )

    with jax.named_scope("row_total_1"):
        came = exchange(message)
        assign, message, total = call(
            second_kernel,
            [((batch, columns), F32), ((devices, 2, LANES), F32), ((batch, LANES), F32)],
            [came, assign],
            8 * batch * columns,
        )

    with jax.named_scope("row_total_2"):
        came = exchange(message)
        assign, keep, send, digits, prob_grad = call(
            third_kernel,
            [
                ((batch, columns), F32),
                ((batch, bottleneck // 2), F32),
                ((batch, bottleneck // 2), F32),
                (side.shape[1:], F32),
                ((batch, bottleneck), F32),
            ],
            [came, assign, proto_b],
            2 * batch * bottleneck * columns,
        )

    with jax.named_scope("row_total_3"):
        got = lax.ppermute(send, "cam", [(i, i ^ 1) for i in range(n_cam)])
        (message,) = call(
            message_kernel,
            [((devices, batch + side.shape[1], LANES), BF16)],
            [keep, got, digits, side],
            devices * batch * LANES,
        )
        came = exchange(after(message, proj_rows))

    with jax.named_scope("outputs"):
        block = min(columns, 512)
        ins = [
            came.reshape((clips, ranks, n_clip) + came.shape[1:]),
            unit,
            norm,
            exponents,
            assign,
            total,
            prob_grad,
            prototypes,
            scale,
            proj_rows,
        ]
        outs = [
            ((batch, columns), F32),
            ((bottleneck, columns), F32),
            ((share, bottleneck), F32),
            ((share, width), F32),
        ]
        return call(
            functools.partial(output_kernel, protos, n_cam, block),
            outs,
            ins,
            2 * batch * bottleneck * columns,
            scratch=[pltpu.VMEM(*o) for o in outs]
            + [pltpu.SemaphoreType.DMA((columns // block + 3,))],
            out_specs=[FAR] * len(outs),
            mib=8,
        )


def solution(mesh):
    in_specs = (P("clip", "cam", None, None), P(), P(), P(), P(), P(None, ALL))
    out_specs = (P(None, ALL), P(None, ALL), P("clip", None), P("clip", "cam"))
    return jax.shard_map(local, mesh=mesh, in_specs=in_specs, out_specs=out_specs, check_vma=False)
```

```python
import functools

import jax
import jax.numpy as jnp
from jax import lax
from jax.experimental import pallas as pl
from jax.experimental.pallas import tpu as pltpu
from jax.sharding import PartitionSpec as P

HD = 64
SINK_EPS = 0.05
SOFTMAX_TEMP = 0.1
NORM_EPS = 1e-06
LANES = 128
DIGITS = 3
ALL = ("cam", "clip")
F32 = jnp.float32
BF16 = jnp.bfloat16
TRANSPOSED = (((1,), (1,)), ((), ()))
OUTER = (((0,), (0,)), ((), ()))
WHOLE = pl.BlockSpec(memory_space=pltpu.VMEM)


def call(
    kernel, outs, ins, flops, extra=0, scratch=(), grid=None, out_specs=None, in_specs=None, mib=4
):
    moved = sum(a.size * a.dtype.itemsize for a in ins)
    return pl.pallas_call(
        kernel,
        out_shape=tuple(jax.ShapeDtypeStruct(*o) for o in outs),
        in_specs=in_specs or [WHOLE] * len(ins),
        out_specs=out_specs or [WHOLE] * len(outs),
        scratch_shapes=list(scratch),
        grid=grid or (),
        compiler_params=pltpu.CompilerParams(vmem_limit_bytes=mib * 2**20),
        cost_estimate=pl.CostEstimate(flops=1, bytes_accessed=1, transcendentals=0),
    )(*ins)


def project(x, wq, wk, wv):
    q = jnp.dot(x, wq, preferred_element_type=F32).astype(BF16) * BF16(HD**-0.5)
    kt = jnp.dot(x, wk, preferred_element_type=F32).astype(BF16).T
    v = jnp.dot(x, wv, preferred_element_type=F32).astype(BF16)
    return q, kt, v


def project_kernel(blocks, *refs):
    wq, wk, wv = refs[blocks : blocks + 3]
    q_ref, kt_ref, v_ref = refs[blocks + 3 :]
    x = jnp.concatenate([x_ref[...] for x_ref in refs[:blocks]], axis=0)
    q_ref[...], kt_ref[...], v_ref[...] = project(x, wq[...], wk[...], wv[...])


def project_blocks(blocks, weights):
    d, cols = weights[0].shape
    rows = sum(b.shape[0] for b in blocks)
    return call(
        functools.partial(project_kernel, len(blocks)),
        [((rows, cols), BF16), ((cols, rows), BF16), ((rows, cols), BF16)],
        [*blocks, *weights],
        2 * rows * d * cols * 3,
    )


def head_of(q, head, lane):
    tile, at = divmod(head * HD, LANES)
    here = slice(tile * LANES, (tile + 1) * LANES)
    return jnp.where(lane // HD == at // HD, q[:, here], BF16(0)), here


def scores(q_head, kt):
    e = jnp.exp(jnp.dot(q_head, kt, preferred_element_type=F32))
    return e, sum(e[:, i : i + LANES] for i in range(0, e.shape[1], LANES))


def first_kernel(blocks, *refs):
    ins, (q_ref, kt_ref, v_ref, exp_ref, sum_ref) = refs[: blocks + 3], refs[blocks + 3 :]
    project_kernel(blocks, *ins, q_ref, kt_ref, v_ref)
    rows, cols = q_ref.shape
    lane = lax.broadcasted_iota(jnp.int32, (rows, LANES), 1)
    sums = jnp.zeros((rows, LANES), F32)
    for head in range(cols // HD):
        q_head, here = head_of(q_ref, head, lane)
        e, part = scores(q_head, kt_ref[here, :])
        exp_ref[head * rows : (head + 1) * rows, :] = e.astype(exp_ref.dtype)
        sums = jnp.where(lane == head, jnp.sum(part, axis=1, keepdims=True), sums)
    sum_ref[...] = sums


def kept_type(heads, rows):
    return F32 if 4 * heads * rows * rows <= 20 * 2**20 else BF16


def first_blocks(blocks, weights, kept):
    d, cols = weights[0].shape
    rows = sum(b.shape[0] for b in blocks)
    heads = cols // HD
    return call(
        functools.partial(first_kernel, len(blocks)),
        [
            ((rows, cols), BF16),
            ((cols, rows), BF16),
            ((rows, cols), BF16),
            ((heads * rows, rows), kept),
            ((rows, LANES), F32),
        ],
        [*blocks, *weights],
        2 * rows * d * cols * 3,
        mib=4 + 8 * rows * rows // 2**20,
    )


def next_kernel(blocks, q_e, kt_e, sum_e, *refs):
    ins, outs = refs[: blocks + 3], refs[blocks + 3 :]
    q_n, kt_n, v_n, exp_n, exp_x, sum_n, sum_ref = outs
    project_kernel(blocks, *ins, q_n, kt_n, v_n)
    rows, cols = q_n.shape
    first = q_e.shape[0]
    lane_n = lax.broadcasted_iota(jnp.int32, (rows, LANES), 1)
    lane_e = lax.broadcasted_iota(jnp.int32, (first, LANES), 1)
    sums_n, sums_e = jnp.zeros((rows, LANES), F32), sum_e[...]
    for head in range(cols // HD):
        queries_n, here = head_of(q_n, head, lane_n)
        queries_e, _ = head_of(q_e, head, lane_e)
        a, part_a = scores(queries_n, kt_e[here, :])
        b, part_b = scores(queries_n, kt_n[here, :])
        x, part_x = scores(queries_e, kt_n[here, :])
        exp_n[head * rows : (head + 1) * rows, :first] = a.astype(exp_n.dtype)
        exp_n[head * rows : (head + 1) * rows, first:] = b.astype(exp_n.dtype)
        exp_x[head * first : (head + 1) * first, :] = x.astype(exp_x.dtype)
        part = jnp.sum(part_a + part_b, axis=1, keepdims=True)
        sums_n = jnp.where(lane_n == head, part, sums_n)
        part = jnp.sum(part_x, axis=1, keepdims=True)
        sums_e = sums_e + jnp.where(lane_e == head, part, 0.0)
    sum_n[...] = sums_n
    sum_ref[...] = sums_e


def next_blocks(blocks, early, weights):
    q_e, kt_e, _, _, sum_e = early
    d, cols = weights[0].shape
    first = q_e.shape[0]
    rows = sum(b.shape[0] for b in blocks)
    heads = cols // HD
    return call(
        functools.partial(next_kernel, len(blocks)),
        [
            ((rows, cols), BF16),
            ((cols, rows), BF16),
            ((rows, cols), BF16),
            ((heads * rows, first + rows), early[3].dtype),
            ((heads * first, rows), early[3].dtype),
            ((rows, LANES), F32),
            ((first, LANES), F32),
        ],
        [q_e, kt_e, sum_e, *blocks, *weights],
        2 * rows * d * cols * 3,
        mib=4 + 24 * first * rows // 2**20,
    )


def pool_kernel(late, *refs):
    (q_e, kt_e, v_e, exp_e), refs = refs[:4], refs[4:]
    (q_n, kt_n, v_n, exp_n, exp_x, sum_n, sum_e), refs = refs[:7], refs[7:]
    (q_a, kt_a, v_a), refs = refs[:3], refs[3:]
    x_refs, (wq, wk, wv, wp) = refs[:late], refs[late : 4 + late]
    weight_ref, pooled_ref, message, q_s, kt_s, v_s, w_s = refs[4 + late :]
    at = q_a.shape[0]
    q_s[:at], kt_s[:, :at], v_s[:at] = q_a[...], kt_a[...], v_a[...]
    for x_ref in x_refs:
        rows = slice(at, at + x_ref.shape[0])
        at += x_ref.shape[0]
        q_s[rows, :], kt_s[:, rows], v_s[rows, :] = project(x_ref[...], wq[...], wk[...], wv[...])
    heads, total = w_s.shape
    cols = heads * HD
    first, then, fresh = q_e.shape[0], q_n.shape[0], q_s.shape[0]
    bounds = [0, first, first + then, total]

    def lanes(rows):
        return lax.broadcasted_iota(jnp.int32, (rows, LANES), 1)

    @pl.loop(0, cols // LANES)
    def _(tile):
        here = pl.ds(pl.multiple_of(tile * LANES, LANES), LANES)
        for e in range(LANES // HD):
            head = tile * (LANES // HD) + e

            def exps(q, kt):
                q_head = jnp.where(lanes(q.shape[0]) // HD == e, q[:, here], BF16(0))
                return jnp.exp(jnp.dot(q_head, kt[here, :], preferred_element_type=F32))

            def row_sum(a):
                return jnp.sum(a, axis=1, keepdims=True)

            def known(sums):
                return row_sum(jnp.where(lanes(sums.shape[0]) == head, sums[...], 0.0))

            def kept(a, rows, keys):
                return a[pl.ds(pl.multiple_of(head * rows, rows), rows), keys].astype(F32)

            new = [exps(q_s, kt) for kt in (kt_e, kt_n, kt_s)]
            e_s, n_s = exps(q_e, kt_s), exps(q_n, kt_s)
            by_s = 1.0 / sum(row_sum(a) for a in new)
            by_e = 1.0 / (known(sum_e) + row_sum(e_s))
            by_n = 1.0 / (known(sum_n) + row_sum(n_s))
            columns = [
                (new[0], kept(exp_e, first, slice(None)), kept(exp_n, then, slice(0, first))),
                (new[1], kept(exp_x, first, slice(None)), kept(exp_n, then, slice(first, None))),
                (new[2], e_s, n_s),
            ]
            for i, parts in enumerate(columns):
                w = sum(
                    jnp.sum(a * by, axis=0, keepdims=True)
                    for a, by in zip(parts, (by_s, by_e, by_n))
                )
                w_s[pl.ds(head, 1), bounds[i] : bounds[i + 1]] = w * (1.0 / total)

    weights = w_s[...].astype(BF16)
    weight_ref[...] = weights
    out = sum(
        jnp.dot(weights[:, bounds[i] : bounds[i + 1]], v[...], preferred_element_type=F32)
        for i, v in enumerate((v_e, v_n, v_s))
    )
    row_head = lax.broadcasted_iota(jnp.int32, out.shape, 0)
    col_head = lax.broadcasted_iota(jnp.int32, out.shape, 1) // HD
    pooled = jnp.sum(jnp.where(row_head == col_head, out, 0.0), axis=0, keepdims=True)
    pooled_ref[...] = pooled
    pooled_b = jnp.broadcast_to(pooled, (8, cols)).astype(BF16)
    embed = jnp.dot(pooled_b, wp[...], preferred_element_type=F32)[:1]
    embed = jnp.concatenate(
        [embed[:, i * LANES : (i + 1) * LANES] for i in range(message.shape[1])], axis=0
    )
    for i in range(message.shape[0]):
        message[i] = embed


def pool(early, after_early, ready, late, weights, wp, devices):
    d, cols = weights[0].shape
    heads = cols // HD
    first, then = early[0].shape[0], after_early[0].shape[0]
    fresh = ready[0].shape[0] + sum(b.shape[0] for b in late)
    total = first + then + fresh
    bottleneck = wp.shape[1]
    return call(
        functools.partial(pool_kernel, len(late)),
        [((heads, total), BF16), ((1, cols), F32), ((devices, bottleneck // LANES, LANES), F32)],
        [*early[:4], *after_early, *ready, *late, *weights, wp],
        2 * fresh * d * cols * 3 + 2 * total * total * cols * 4,
        heads * total * total,
        scratch=[
            pltpu.VMEM((fresh, cols), BF16),
            pltpu.VMEM((cols, fresh), BF16),
            pltpu.VMEM((fresh, cols), BF16),
            pltpu.VMEM((heads, total), F32),
        ],
        mib=6 + 40 * fresh * total // 2**20,
    )


def mixture_kernel(cameras, clips, n_clip, w_ref, pooled_ref, *refs):
    x_refs, side = refs[:-1], refs[-1]
    heads, d = w_ref.shape[0], x_refs[0].shape[1]
    heads_here, share = heads // clips, d // n_clip
    mix = jnp.zeros((heads, d), F32)
    for camera in cameras:
        m = jnp.zeros((heads, d), F32)
        for block, at in camera:
            w = w_ref[:, at : at + x_refs[block].shape[0]]
            m = m + jnp.dot(w, x_refs[block][...], preferred_element_type=F32)
        mix = mix + m.astype(BF16).astype(F32)

    def lanes(x, i):
        x = x[:, i * share : (i + 1) * share]
        if share == LANES:
            return x
        return jnp.concatenate([x, jnp.zeros((x.shape[0], LANES - share), F32)], axis=1)

    for i in range(side.shape[0]):
        j, p = divmod(i % (clips * n_clip), n_clip)
        side[i] = jnp.concatenate(
            [
                lanes(pooled_ref[...], i % (pooled_ref.shape[1] // share)),
                lanes(mix[j * heads_here : (j + 1) * heads_here], p),
            ],
            axis=0,
        )


FAR = pl.BlockSpec(memory_space=pltpu.HBM)


def slice_kernel(plan, *refs):
    ins = 1 + max(which for which, _ in plan)
    outs, sems = refs[ins:-1], refs[-1]
    copies = []
    for i, (which, where) in enumerate(plan):
        source = refs[which].at[where()]
        copies.append(pltpu.make_async_copy(source, outs[i], sems.at[i]))
        copies[-1].start()
    for copy in copies:
        copy.wait()


def slices(arrays, plan, shapes):
    return call(
        functools.partial(slice_kernel, plan),
        [(shape, BF16) for shape in shapes],
        [pltpu.with_memory_space_constraint(a, pltpu.HBM) for a in arrays],
        0,
        scratch=[pltpu.SemaphoreType.DMA((len(plan),))],
        in_specs=[FAR] * len(arrays),
    )


def after(x, *others):
    return lax.optimization_barrier((x, others))[0]


def token_block(s, clips, ranks, start, size):
    rows = pl.ds(start, size)
    return 0, lambda: ((lax.axis_index("cam") // ranks + s) % clips, rows, slice(None))


def from_other_groups(tokens, n_cam):
    clips, tok, d = tokens.shape
    ranks = n_cam // clips
    half = tok // 2
    pieces = [(s, c) for c in range(2) for s in range(1, clips)]
    mine, *sent = slices(
        [tokens],
        [token_block(0, clips, ranks, 0, tok)]
        + [token_block(s, clips, ranks, c * half, half) for s, c in pieces],
        [(tok, d)] + [(half, d)] * len(pieces),
    )
    held = [[], []]
    for (s, c), block in zip(pieces, sent):
        perm = [
            (i, ((i // ranks + s) % clips) * ranks + (i % ranks + c) % ranks) for i in range(n_cam)
        ]
        held[c].append((s * ranks + c % ranks, lax.ppermute(block, "cam", perm)))
    return mine, *held


def relay(blocks, n_cam, ranks, cuts=1):
    stage = list(blocks)
    size = blocks[0][1].shape[0] // cuts
    blocks = [(camera, b[i * size : (i + 1) * size]) for camera, b in blocks for i in range(cuts)]
    for t in range(1, ranks):
        perm = [(i, (i // ranks) * ranks + (i % ranks + t) % ranks) for i in range(n_cam)]
        for camera, b in blocks:
            label = camera // ranks * ranks + (camera + t) % ranks
            stage.append((label, lax.ppermute(b, "cam", perm)))
    return stage


def prototype_kernel(proto, scale, proto_b):
    proto_f = proto[...].astype(F32)
    norm = jnp.sqrt(jnp.sum(proto_f * proto_f, axis=0, keepdims=True) + NORM_EPS)
    scale[...] = 1.0 / norm
    proto_b[...] = (proto_f / norm).astype(BF16)


def to_lanes(column, offset=0):
    shape = (column.shape[0], LANES)
    row = lax.broadcasted_iota(jnp.int32, shape, 0) + offset
    lane = lax.broadcasted_iota(jnp.int32, shape, 1)
    return jnp.sum(jnp.where(lane == row, column, 0.0), axis=0, keepdims=True)


def from_lanes(line, size, offset=0):
    row = lax.broadcasted_iota(jnp.int32, (size, LANES), 0) + offset
    lane = lax.broadcasted_iota(jnp.int32, (size, LANES), 1)
    return jnp.sum(jnp.where(lane == row, line, 0.0), axis=1, keepdims=True)


def digit_rows(batch, columns):
    return -(-columns * DIGITS // (LANES // batch))


def pack(*columns):
    batch = columns[0].shape[0]
    slots = LANES // batch
    lines = [jnp.zeros((1, LANES), F32)] * digit_rows(batch, len(columns))
    for i, rest in enumerate(columns):
        for slot in range(i * DIGITS, (i + 1) * DIGITS):
            digit = rest.astype(BF16).astype(F32)
            rest = rest - digit
            row, at = divmod(slot, slots)
            lines[row] = lines[row] + to_lanes(digit, at * batch)
    return jnp.concatenate(lines, axis=0)


def unpack(lines, batch, i):
    slots = LANES // batch
    column = jnp.zeros((batch, 1), F32)
    for slot in range(i * DIGITS, (i + 1) * DIGITS):
        row, at = divmod(slot, slots)
        column = column + from_lanes(lines[row : row + 1], batch, at * batch)
    return column


def spread(column):
    return jnp.broadcast_to(column, (column.shape[0], LANES))


def exchange(message):
    return lax.all_to_all(message, ALL, split_axis=0, concat_axis=0, tiled=True)


def logits_kernel(
    clips, ranks, n_clip, came, proto, side, unit_ref, norm_ref, exp_ref, assign_ref, message
):
    rows = []
    for g in range(clips):
        for p in range(n_clip):
            z = sum(came[(g * ranks + r) * n_clip + p] for r in range(ranks))
            rows.append(jnp.concatenate([z[i : i + 1] for i in range(z.shape[0])], axis=1))
    embed = jnp.concatenate(rows, axis=0)
    norm = jnp.sqrt(jnp.sum(embed * embed, axis=1, keepdims=True) + NORM_EPS)
    unit = embed / norm
    unit_ref[...] = unit
    norm_ref[...] = spread(norm)
    logits = jnp.dot(unit.astype(BF16), proto[...], preferred_element_type=F32)
    exponents = jnp.exp(logits / SOFTMAX_TEMP)
    assign = jnp.exp(logits / SINK_EPS)
    exp_ref[...] = exponents
    assign = assign / jnp.sum(assign, axis=0, keepdims=True)
    assign_ref[...] = assign
    part = lax.dot_general(
        exponents.astype(BF16), proto[...], TRANSPOSED, preferred_element_type=F32
    )
    batch = part.shape[0]
    lines = pack(
        jnp.sum(assign, axis=1, keepdims=True), jnp.sum(exponents, axis=1, keepdims=True)
    )
    halves = part.shape[1] // LANES
    high = part.astype(BF16).astype(F32)
    low = part - high
    for i in range(message.shape[0]):
        if i < halves * batch:
            h, b = divmod(i, batch)
            here = slice(h * LANES, (h + 1) * LANES)
            piece = [high[b : b + 1, here], low[b : b + 1, here]]
        else:
            piece = [jnp.zeros((2, LANES), F32)]
        message[i] = jnp.concatenate([*piece, lines, side[i]], axis=0).astype(BF16)


def second_kernel(came, assign_ref, assign_out, message, total_ref):
    batch = assign_ref.shape[0]
    came = jnp.sum(came[...].astype(F32), axis=0)
    lines = came[2 : 2 + digit_rows(batch, 2)]
    total_ref[...] = spread(unpack(lines, batch, 1))
    assign = assign_ref[...] / unpack(lines, batch, 0)
    assign = assign / jnp.sum(assign, axis=0, keepdims=True)
    assign_out[...] = assign
    line = to_lanes(jnp.sum(assign, axis=1, keepdims=True))
    out = jnp.concatenate([came[0:1] + came[1:2], line], axis=0)
    for i in range(message.shape[0]):
        message[i] = out


def third_kernel(
    came, assign_ref, proto, assign_out, keep_ref, send_ref, digits_ref, grad_ref
):
    batch = assign_ref.shape[0]
    halves = proto.shape[0] // LANES
    total = jnp.sum(came[...], axis=0)[1:2]
    assign = assign_ref[...] / from_lanes(total, batch)
    assign = assign / jnp.sum(assign, axis=0, keepdims=True)
    assign_out[...] = assign
    part = lax.dot_general(
        assign.astype(BF16), proto[...], TRANSPOSED, preferred_element_type=F32
    )
    half = part.shape[1] // 2
    odd = lax.axis_index("cam") % 2 == 1
    low, high = part[:, :half], part[:, half:]
    keep_ref[...] = jnp.where(odd, high, low)
    send_ref[...] = jnp.where(odd, low, high)
    digits_ref[...] = pack(jnp.sum(assign, axis=1, keepdims=True))
    for h in range(halves):
        for b in range(batch):
            grad_ref[b : b + 1, h * LANES : (h + 1) * LANES] = came[h * batch + b][0:1]


def message_kernel(keep, got, digits, message):
    rows = jnp.concatenate([keep[...] + got[...], digits[...]], axis=0)
    width = message.shape[2] // LANES
    rows = [rows[i : i + 1] for i in range(rows.shape[0])]
    rows += [jnp.zeros((1, LANES), F32)] * (2 * width - len(rows))
    long = [jnp.concatenate(rows[i * width : (i + 1) * width], axis=1) for i in range(2)]
    out = jnp.concatenate(long, axis=0).astype(BF16)
    for i in range(message.shape[0]):
        message[i] = out


def output_kernel(
    protos,
    n_cam,
    block,
    came,
    came_side,
    unit_ref,
    norm_ref,
    exp_ref,
    assign_ref,
    total_ref,
    prob_grad,
    proto,
    scale,
    wp,
    codes_out,
    proto_grad_out,
    grad_proj_out,
    grad_value_out,
    codes,
    proto_grad,
    grad_proj,
    grad_value,
    sems,
):
    clips, ranks, n_clip = came.shape[:3]
    batch, columns = exp_ref.shape
    share = grad_proj.shape[0]
    cols = clips * wp.shape[0]
    copies = []

    def send(source, target):
        copies.append(pltpu.make_async_copy(source, target, sems.at[len(copies)]))
        copies[-1].start()

    sums = [jnp.zeros(came.shape[3:], F32) for _ in range(2)]
    for cam in range(n_cam):
        part = jnp.sum(came[cam // ranks, cam % ranks].astype(F32), axis=0)
        sums[cam % 2] = sums[cam % 2] + part
    long = came.shape[4] // LANES

    def short(x, start, stop):
        places = [divmod(i, long) for i in range(start, stop)]
        return jnp.concatenate(
            [x[r : r + 1, i * LANES : (i + 1) * LANES] for r, i in places], axis=0
        )

    lines = short(sums[0] + sums[1], batch, batch + digit_rows(batch, 1))
    by_assign = protos / unpack(lines, batch, 0)
    by_prob = protos / total_ref[:, :1]
    unit = unit_ref[...]
    unit_b = unit.astype(BF16)

    for start in range(0, columns, block):
        here = slice(start, start + block)
        assign = assign_ref[:, here] * by_assign
        grad_logits = (exp_ref[:, here] * by_prob - assign).astype(BF16)
        for g in range(clips):
            for p in range(n_clip):
                row, to = g * n_clip + p, p * clips + g
                codes[to : to + 1, here] = assign[row : row + 1]
        grad = lax.dot_general(unit_b, grad_logits, OUTER, preferred_element_type=F32)
        inverse = scale[:, here]
        unit_proto = proto[:, here].astype(F32) * inverse
        along = jnp.sum(unit_proto * grad, axis=0, keepdims=True)
        proto_grad[:, here] = (grad - unit_proto * along) * inverse
        send(proto_grad.at[:, here], proto_grad_out.at[:, here])
    send(codes, codes_out)

    assign_grad = jnp.concatenate([short(s, 0, batch) for s in sums], axis=1)
    grad_unit = prob_grad[...] * by_prob - assign_grad * by_assign
    grad_embed = (
        grad_unit - unit * jnp.sum(unit * grad_unit, axis=1, keepdims=True)
    ) / norm_ref[:, :1]
    grad_embed = grad_embed.astype(BF16)

    side = 2 + digit_rows(batch, 2)

    def rows(rank, row):
        picked = [came_side[g, rank].astype(F32)[:, row, :] for g in range(clips)]
        return jnp.concatenate(picked, axis=0)[:, :share].astype(BF16)

    grad_proj[...] = lax.dot_general(
        rows(lax.axis_index("clip") * share // cols, side), grad_embed, OUTER, preferred_element_type=F32
    )
    send(grad_proj, grad_proj_out)
    grad_pooled = lax.dot_general(
        grad_embed, wp[...], TRANSPOSED, preferred_element_type=F32
    ).astype(BF16)
    col_head = lax.broadcasted_iota(jnp.int32, grad_value.shape, 1) // HD
    value = jnp.zeros(grad_value.shape, F32)
    for head in range(grad_value.shape[1] // HD):
        mixed = rows(lax.axis_index("cam") // clips, side + 1 + head)
        out = lax.dot_general(mixed, grad_pooled, OUTER, preferred_element_type=F32)
        value = jnp.where(col_head == head, out, value)
    grad_value[...] = value
    send(grad_value, grad_value_out)
    for copy in copies:
        copy.wait()


def local(tokens, w_query, w_key, w_value, w_proj, prototypes):
    clips, _, tok, d = tokens.shape
    n_cam, n_clip = lax.axis_size("cam"), lax.axis_size("clip")
    devices = n_cam * n_clip
    ranks = n_cam // clips
    batch = clips * n_clip
    cols = d // ranks
    heads = cols // HD
    heads_here = heads // clips
    share = d // n_clip
    bottleneck, columns = prototypes.shape
    protos = columns * devices
    width = heads_here * HD

    with jax.named_scope("tokens_of_a_clip"):
        tokens = tokens.reshape(clips, tok, d)
        mine, half, rest = from_other_groups(tokens, n_cam)

    with jax.named_scope("prototypes"):
        scale, proto_b = call(
            prototype_kernel,
            [((1, columns), F32), ((bottleneck, columns), BF16)],
            [prototypes],
            4 * bottleneck * columns,
            mib=8,
        )

    with jax.named_scope("pooling"):
        def columns_of():
            start = lax.axis_index("cam") % ranks * cols
            return slice(None), pl.ds(pl.multiple_of(start, cols), cols)

        def rows_of():
            start = lax.axis_index("cam") % ranks * cols
            return pl.ds(pl.multiple_of(start, cols), cols), slice(None)

        def heads_of():
            start = lax.axis_index("cam") * width
            return pl.ds(pl.multiple_of(start, width), width), slice(None)

        *weights, wp, proj_rows = slices(
            [w_query, w_key, w_value, w_proj],
            [(i, columns_of) for i in range(3)] + [(3, rows_of), (3, heads_of)],
            [(d, cols)] * 3 + [(cols, bottleneck), (width, bottleneck)],
        )
        stages = [relay([(0, mine)], n_cam, ranks)]
        kept = kept_type(heads, n_cam * tok - (n_cam - ranks) * tok // 2)
        early = first_blocks([b for _, b in stages[0]], weights, kept)
        half = [(camera, after(b, proto_b, *early)) for camera, b in half]
        stages.append(relay(half, n_cam, ranks, 2))
        then = next_blocks([b for _, b in stages[1]], early, weights)
        rest = [(camera, after(b, *then)) for camera, b in rest]
        stages.append(relay(rest, n_cam, ranks))
        ready = project_blocks([b for _, b in rest], weights)
        late = [b for _, b in stages[2][len(rest) :]]
        key_weights, pooled, message = pool(early, then, ready, late, weights, wp, devices)

    with jax.named_scope("mixtures"):
        cameras, blocks, at = {}, [], 0
        for stage in stages:
            for camera, block in stage:
                cameras.setdefault(camera, []).append((len(blocks), at))
                blocks.append(block)
                at += block.shape[0]
        (side,) = call(
            functools.partial(mixture_kernel, list(cameras.values()), clips, n_clip),
            [((devices, 1 + heads_here, LANES), F32)],
            [key_weights, pooled, *blocks],
            2 * at * d * 32,
            mib=8,
        )

    with jax.named_scope("logits"):
        came = after(exchange(message), side)
        unit, norm, exponents, assign, message = call(
            functools.partial(logits_kernel, clips, ranks, n_clip),
            [
                ((batch, bottleneck), F32),
                ((batch, LANES), F32),
                ((batch, columns), F32),
                ((batch, columns), F32),
                ((devices, 2 + digit_rows(batch, 2) + side.shape[1], LANES), BF16),
            ],
            [came, proto_b, side],
            4 * batch * bottleneck * columns,
            2 * batch * columns,
        )

    with jax.named_scope("row_total_1"):
        came_side = came = exchange(message)
        assign, message, total = call(
            second_kernel,
            [((batch, columns), F32), ((devices, 2, LANES), F32), ((batch, LANES), F32)],
            [came, assign],
            8 * batch * columns,
        )

    with jax.named_scope("row_total_2"):
        came = exchange(message)
        assign, keep, send, digits, prob_grad = call(
            third_kernel,
            [
                ((batch, columns), F32),
                ((batch, bottleneck // 2), F32),
                ((batch, bottleneck // 2), F32),
                ((digit_rows(batch, 1), LANES), F32),
                ((batch, bottleneck), F32),
            ],
            [came, assign, proto_b],
            2 * batch * bottleneck * columns,
        )

    with jax.named_scope("row_total_3"):
        got = lax.ppermute(send, "cam", [(i, i ^ 1) for i in range(n_cam)])
        (message,) = call(
            message_kernel,
            [((devices, 2, -(-(batch + digits.shape[0]) // 2) * LANES), BF16)],
            [keep, got, digits],
            devices * batch * LANES,
        )
        came = exchange(after(message, proj_rows))

    with jax.named_scope("outputs"):
        block = min(columns, 512)
        ins = [
            came.reshape((clips, ranks, n_clip) + came.shape[1:]),
            came_side.reshape((clips, ranks, n_clip) + came_side.shape[1:]),
            unit,
            norm,
            exponents,
            assign,
            total,
            prob_grad,
            prototypes,
            scale,
            proj_rows,
        ]
        outs = [
            ((batch, columns), F32),
            ((bottleneck, columns), F32),
            ((share, bottleneck), F32),
            ((share, width), F32),
        ]
        return call(
            functools.partial(output_kernel, protos, n_cam, block),
            outs,
            ins,
            2 * batch * bottleneck * columns,
            scratch=[pltpu.VMEM(*o) for o in outs]
            + [pltpu.SemaphoreType.DMA((columns // block + 3,))],
            out_specs=[FAR] * len(outs),
            mib=8,
        )


def solution(mesh):
    in_specs = (P("clip", "cam", None, None), P(), P(), P(), P(), P(None, ALL))
    out_specs = (P(None, ALL), P(None, ALL), P("clip", None), P("clip", "cam"))
    return jax.shard_map(local, mesh=mesh, in_specs=in_specs, out_specs=out_specs, check_vma=False)
```

```python
import functools

import jax
import jax.numpy as jnp
from jax import lax
from jax.experimental import pallas as pl
from jax.experimental.pallas import tpu as pltpu
from jax.sharding import PartitionSpec as P

HD = 64
SINK_EPS = 0.05
SOFTMAX_TEMP = 0.1
NORM_EPS = 1e-06
LANES = 128
DIGITS = 3
ALL = ("cam", "clip")
F32 = jnp.float32
BF16 = jnp.bfloat16
TRANSPOSED = (((1,), (1,)), ((), ()))
OUTER = (((0,), (0,)), ((), ()))
WHOLE = pl.BlockSpec(memory_space=pltpu.VMEM)


def call(
    kernel, outs, ins, flops, extra=0, scratch=(), grid=None, out_specs=None, in_specs=None, mib=4
):
    moved = sum(a.size * a.dtype.itemsize for a in ins)
    return pl.pallas_call(
        kernel,
        out_shape=tuple(jax.ShapeDtypeStruct(*o) for o in outs),
        in_specs=in_specs or [WHOLE] * len(ins),
        out_specs=out_specs or [WHOLE] * len(outs),
        scratch_shapes=list(scratch),
        grid=grid or (),
        compiler_params=pltpu.CompilerParams(vmem_limit_bytes=mib * 2**20),
        cost_estimate=pl.CostEstimate(flops=1, bytes_accessed=1, transcendentals=0),
    )(*ins)


def project(x, wq, wk, wv):
    q = jnp.dot(x, wq, preferred_element_type=F32).astype(BF16) * BF16(HD**-0.5)
    kt = jnp.dot(x, wk, preferred_element_type=F32).astype(BF16).T
    v = jnp.dot(x, wv, preferred_element_type=F32).astype(BF16)
    return q, kt, v


def project_kernel(blocks, *refs):
    wq, wk, wv = refs[blocks : blocks + 3]
    q_ref, kt_ref, v_ref = refs[blocks + 3 :]
    x = jnp.concatenate([x_ref[...] for x_ref in refs[:blocks]], axis=0)
    q_ref[...], kt_ref[...], v_ref[...] = project(x, wq[...], wk[...], wv[...])


def project_blocks(blocks, weights):
    d, cols = weights[0].shape
    rows = sum(b.shape[0] for b in blocks)
    return call(
        functools.partial(project_kernel, len(blocks)),
        [((rows, cols), BF16), ((cols, rows), BF16), ((rows, cols), BF16)],
        [*blocks, *weights],
        2 * rows * d * cols * 3,
    )


def head_of(q, head, lane):
    tile, at = divmod(head * HD, LANES)
    here = slice(tile * LANES, (tile + 1) * LANES)
    return jnp.where(lane // HD == at // HD, q[:, here], BF16(0)), here


def scores(q_head, kt):
    e = jnp.exp(jnp.dot(q_head, kt, preferred_element_type=F32))
    return e, sum(e[:, i : i + LANES] for i in range(0, e.shape[1], LANES))


def first_kernel(blocks, *refs):
    ins, (q_ref, kt_ref, v_ref, exp_ref, sum_ref) = refs[: blocks + 3], refs[blocks + 3 :]
    project_kernel(blocks, *ins, q_ref, kt_ref, v_ref)
    rows, cols = q_ref.shape
    lane = lax.broadcasted_iota(jnp.int32, (rows, LANES), 1)
    sums = jnp.zeros((rows, LANES), F32)
    for head in range(cols // HD):
        q_head, here = head_of(q_ref, head, lane)
        e, part = scores(q_head, kt_ref[here, :])
        exp_ref[head * rows : (head + 1) * rows, :] = e.astype(exp_ref.dtype)
        sums = jnp.where(lane == head, jnp.sum(part, axis=1, keepdims=True), sums)
    sum_ref[...] = sums


def kept_type(heads, rows):
    return F32 if 4 * heads * rows * rows <= 20 * 2**20 else BF16


def first_blocks(blocks, weights, kept):
    d, cols = weights[0].shape
    rows = sum(b.shape[0] for b in blocks)
    heads = cols // HD
    return call(
        functools.partial(first_kernel, len(blocks)),
        [
            ((rows, cols), BF16),
            ((cols, rows), BF16),
            ((rows, cols), BF16),
            ((heads * rows, rows), kept),
            ((rows, LANES), F32),
        ],
        [*blocks, *weights],
        2 * rows * d * cols * 3,
        mib=4 + 8 * rows * rows // 2**20,
    )


def next_kernel(blocks, q_e, kt_e, sum_e, *refs):
    ins, outs = refs[: blocks + 3], refs[blocks + 3 :]
    q_n, kt_n, v_n, exp_n, exp_x, sum_n, sum_ref = outs
    project_kernel(blocks, *ins, q_n, kt_n, v_n)
    rows, cols = q_n.shape
    first = q_e.shape[0]
    lane_n = lax.broadcasted_iota(jnp.int32, (rows, LANES), 1)
    lane_e = lax.broadcasted_iota(jnp.int32, (first, LANES), 1)
    sums_n, sums_e = jnp.zeros((rows, LANES), F32), sum_e[...]
    for head in range(cols // HD):
        queries_n, here = head_of(q_n, head, lane_n)
        queries_e, _ = head_of(q_e, head, lane_e)
        a, part_a = scores(queries_n, kt_e[here, :])
        b, part_b = scores(queries_n, kt_n[here, :])
        x, part_x = scores(queries_e, kt_n[here, :])
        exp_n[head * rows : (head + 1) * rows, :first] = a.astype(exp_n.dtype)
        exp_n[head * rows : (head + 1) * rows, first:] = b.astype(exp_n.dtype)
        exp_x[head * first : (head + 1) * first, :] = x.astype(exp_x.dtype)
        part = jnp.sum(part_a + part_b, axis=1, keepdims=True)
        sums_n = jnp.where(lane_n == head, part, sums_n)
        part = jnp.sum(part_x, axis=1, keepdims=True)
        sums_e = sums_e + jnp.where(lane_e == head, part, 0.0)
    sum_n[...] = sums_n
    sum_ref[...] = sums_e


def next_blocks(blocks, early, weights):
    q_e, kt_e, _, _, sum_e = early
    d, cols = weights[0].shape
    first = q_e.shape[0]
    rows = sum(b.shape[0] for b in blocks)
    heads = cols // HD
    return call(
        functools.partial(next_kernel, len(blocks)),
        [
            ((rows, cols), BF16),
            ((cols, rows), BF16),
            ((rows, cols), BF16),
            ((heads * rows, first + rows), early[3].dtype),
            ((heads * first, rows), early[3].dtype),
            ((rows, LANES), F32),
            ((first, LANES), F32),
        ],
        [q_e, kt_e, sum_e, *blocks, *weights],
        2 * rows * d * cols * 3,
        mib=4 + 24 * first * rows // 2**20,
    )


def pool_kernel(late, *refs):
    (q_e, kt_e, v_e, exp_e), refs = refs[:4], refs[4:]
    (q_n, kt_n, v_n, exp_n, exp_x, sum_n, sum_e), refs = refs[:7], refs[7:]
    (q_a, kt_a, v_a), refs = refs[:3], refs[3:]
    x_refs, (wq, wk, wv, wp) = refs[:late], refs[late : 4 + late]
    weight_ref, pooled_ref, message, q_s, kt_s, v_s, w_s = refs[4 + late :]
    at = q_a.shape[0]
    q_s[:at], kt_s[:, :at], v_s[:at] = q_a[...], kt_a[...], v_a[...]
    for x_ref in x_refs:
        rows = slice(at, at + x_ref.shape[0])
        at += x_ref.shape[0]
        q_s[rows, :], kt_s[:, rows], v_s[rows, :] = project(x_ref[...], wq[...], wk[...], wv[...])
    heads, total = w_s.shape
    cols = heads * HD
    first, then, fresh = q_e.shape[0], q_n.shape[0], q_s.shape[0]
    bounds = [0, first, first + then, total]

    def lanes(rows):
        return lax.broadcasted_iota(jnp.int32, (rows, LANES), 1)

    @pl.loop(0, cols // LANES)
    def _(tile):
        here = pl.ds(pl.multiple_of(tile * LANES, LANES), LANES)
        for e in range(LANES // HD):
            head = tile * (LANES // HD) + e

            def exps(q, kt):
                q_head = jnp.where(lanes(q.shape[0]) // HD == e, q[:, here], BF16(0))
                return jnp.exp(jnp.dot(q_head, kt[here, :], preferred_element_type=F32))

            def row_sum(a):
                return jnp.sum(a, axis=1, keepdims=True)

            def known(sums):
                return jnp.where(lanes(sums.shape[0]) == head, sums[...], 0.0)

            def lane_sums(a):
                return sum(a[:, i : i + LANES] for i in range(0, a.shape[1], LANES))

            def kept(a, rows, keys):
                return a[pl.ds(pl.multiple_of(head * rows, rows), rows), keys].astype(F32)

            new = [exps(q_s, kt) for kt in (kt_e, kt_n, kt_s)]
            e_s, n_s = exps(q_e, kt_s), exps(q_n, kt_s)
            by_s = 1.0 / row_sum(sum(lane_sums(a) for a in new))
            by_e = 1.0 / row_sum(known(sum_e) + lane_sums(e_s))
            by_n = 1.0 / row_sum(known(sum_n) + lane_sums(n_s))
            columns = [
                (new[0], kept(exp_e, first, slice(None)), kept(exp_n, then, slice(0, first))),
                (new[1], kept(exp_x, first, slice(None)), kept(exp_n, then, slice(first, None))),
                (new[2], e_s, n_s),
            ]
            for i, parts in enumerate(columns):
                w = sum(
                    jnp.sum(a * by, axis=0, keepdims=True)
                    for a, by in zip(parts, (by_s, by_e, by_n))
                )
                w_s[pl.ds(head, 1), bounds[i] : bounds[i + 1]] = w * (1.0 / total)

    weights = w_s[...].astype(BF16)
    weight_ref[...] = weights
    out = sum(
        jnp.dot(weights[:, bounds[i] : bounds[i + 1]], v[...], preferred_element_type=F32)
        for i, v in enumerate((v_e, v_n, v_s))
    )
    row_head = lax.broadcasted_iota(jnp.int32, out.shape, 0)
    col_head = lax.broadcasted_iota(jnp.int32, out.shape, 1) // HD
    pooled = jnp.sum(jnp.where(row_head == col_head, out, 0.0), axis=0, keepdims=True)
    pooled_ref[...] = pooled
    pooled_b = jnp.broadcast_to(pooled, (8, cols)).astype(BF16)
    embed = jnp.dot(pooled_b, wp[...], preferred_element_type=F32)[:1]
    embed = jnp.concatenate(
        [embed[:, i * LANES : (i + 1) * LANES] for i in range(message.shape[1])], axis=0
    )
    for i in range(message.shape[0]):
        message[i] = embed


def pool(early, after_early, ready, late, weights, wp, devices):
    d, cols = weights[0].shape
    heads = cols // HD
    first, then = early[0].shape[0], after_early[0].shape[0]
    fresh = ready[0].shape[0] + sum(b.shape[0] for b in late)
    total = first + then + fresh
    bottleneck = wp.shape[1]
    return call(
        functools.partial(pool_kernel, len(late)),
        [((heads, total), BF16), ((1, cols), F32), ((devices, bottleneck // LANES, LANES), F32)],
        [*early[:4], *after_early, *ready, *late, *weights, wp],
        2 * fresh * d * cols * 3 + 2 * total * total * cols * 4,
        heads * total * total,
        scratch=[
            pltpu.VMEM((fresh, cols), BF16),
            pltpu.VMEM((cols, fresh), BF16),
            pltpu.VMEM((fresh, cols), BF16),
            pltpu.VMEM((heads, total), F32),
        ],
        mib=6 + 40 * fresh * total // 2**20,
    )


def mixture_kernel(cameras, clips, n_clip, w_ref, pooled_ref, *refs):
    x_refs, side = refs[:-1], refs[-1]
    heads, d = w_ref.shape[0], x_refs[0].shape[1]
    heads_here, share = heads // clips, d // n_clip
    mix = jnp.zeros((heads, d), F32)
    for camera in cameras:
        m = jnp.zeros((heads, d), F32)
        for block, at in camera:
            w = w_ref[:, at : at + x_refs[block].shape[0]]
            m = m + jnp.dot(w, x_refs[block][...], preferred_element_type=F32)
        mix = mix + m.astype(BF16).astype(F32)

    def lanes(x, i):
        x = x[:, i * share : (i + 1) * share]
        if share == LANES:
            return x
        return jnp.concatenate([x, jnp.zeros((x.shape[0], LANES - share), F32)], axis=1)

    for i in range(side.shape[0]):
        j, p = divmod(i % (clips * n_clip), n_clip)
        side[i] = jnp.concatenate(
            [
                lanes(pooled_ref[...], i % (pooled_ref.shape[1] // share)),
                lanes(mix[j * heads_here : (j + 1) * heads_here], p),
            ],
            axis=0,
        )


FAR = pl.BlockSpec(memory_space=pltpu.HBM)


def slice_kernel(plan, *refs):
    ins = 1 + max(which for which, _ in plan)
    outs, sems = refs[ins:-1], refs[-1]
    copies = []
    for i, (which, where) in enumerate(plan):
        source = refs[which].at[where()]
        copies.append(pltpu.make_async_copy(source, outs[i], sems.at[i]))
        copies[-1].start()
    for copy in copies:
        copy.wait()


def slices(arrays, plan, shapes):
    return call(
        functools.partial(slice_kernel, plan),
        [(shape, BF16) for shape in shapes],
        [pltpu.with_memory_space_constraint(a, pltpu.HBM) for a in arrays],
        0,
        scratch=[pltpu.SemaphoreType.DMA((len(plan),))],
        in_specs=[FAR] * len(arrays),
    )


def after(x, *others):
    return lax.optimization_barrier((x, others))[0]


def token_block(s, clips, ranks, start, size):
    rows = pl.ds(start, size)
    return 0, lambda: ((lax.axis_index("cam") // ranks + s) % clips, rows, slice(None))


def from_other_groups(tokens, n_cam):
    clips, tok, d = tokens.shape
    ranks = n_cam // clips
    half = tok // 2
    pieces = [(s, c) for c in range(2) for s in range(1, clips)]
    mine, *sent = slices(
        [tokens],
        [token_block(0, clips, ranks, 0, tok)]
        + [token_block(s, clips, ranks, c * half, half) for s, c in pieces],
        [(tok, d)] + [(half, d)] * len(pieces),
    )
    held = [[], []]
    for (s, c), block in zip(pieces, sent):
        perm = [
            (i, ((i // ranks + s) % clips) * ranks + (i % ranks + c) % ranks) for i in range(n_cam)
        ]
        held[c].append((s * ranks + c % ranks, lax.ppermute(block, "cam", perm)))
    return mine, *held


def relay(blocks, n_cam, ranks, cuts=1):
    stage = list(blocks)
    size = blocks[0][1].shape[0] // cuts
    blocks = [(camera, b[i * size : (i + 1) * size]) for camera, b in blocks for i in range(cuts)]
    for t in range(1, ranks):
        perm = [(i, (i // ranks) * ranks + (i % ranks + t) % ranks) for i in range(n_cam)]
        for camera, b in blocks:
            label = camera // ranks * ranks + (camera + t) % ranks
            stage.append((label, lax.ppermute(b, "cam", perm)))
    return stage


def prototype_kernel(proto, scale, proto_b):
    proto_f = proto[...].astype(F32)
    norm = jnp.sqrt(jnp.sum(proto_f * proto_f, axis=0, keepdims=True) + NORM_EPS)
    scale[...] = 1.0 / norm
    proto_b[...] = (proto_f / norm).astype(BF16)


def to_lanes(column, offset=0):
    shape = (column.shape[0], LANES)
    row = lax.broadcasted_iota(jnp.int32, shape, 0) + offset
    lane = lax.broadcasted_iota(jnp.int32, shape, 1)
    return jnp.sum(jnp.where(lane == row, column, 0.0), axis=0, keepdims=True)


def from_lanes(line, size, offset=0):
    row = lax.broadcasted_iota(jnp.int32, (size, LANES), 0) + offset
    lane = lax.broadcasted_iota(jnp.int32, (size, LANES), 1)
    return jnp.sum(jnp.where(lane == row, line, 0.0), axis=1, keepdims=True)


def digit_rows(batch, columns):
    return -(-columns * DIGITS // (LANES // batch))


def pack(*columns):
    batch = columns[0].shape[0]
    slots = LANES // batch
    lines = [jnp.zeros((1, LANES), F32)] * digit_rows(batch, len(columns))
    for i, rest in enumerate(columns):
        for slot in range(i * DIGITS, (i + 1) * DIGITS):
            digit = rest.astype(BF16).astype(F32)
            rest = rest - digit
            row, at = divmod(slot, slots)
            lines[row] = lines[row] + to_lanes(digit, at * batch)
    return jnp.concatenate(lines, axis=0)


def unpack(lines, batch, i):
    slots = LANES // batch
    column = jnp.zeros((batch, 1), F32)
    for slot in range(i * DIGITS, (i + 1) * DIGITS):
        row, at = divmod(slot, slots)
        column = column + from_lanes(lines[row : row + 1], batch, at * batch)
    return column


def spread(column):
    return jnp.broadcast_to(column, (column.shape[0], LANES))


def exchange(message):
    return lax.all_to_all(message, ALL, split_axis=0, concat_axis=0, tiled=True)


def logits_kernel(
    clips, ranks, n_clip, came, proto, side, unit_ref, norm_ref, exp_ref, assign_ref, message
):
    rows = []
    for g in range(clips):
        for p in range(n_clip):
            z = sum(came[(g * ranks + r) * n_clip + p] for r in range(ranks))
            rows.append(jnp.concatenate([z[i : i + 1] for i in range(z.shape[0])], axis=1))
    embed = jnp.concatenate(rows, axis=0)
    norm = jnp.sqrt(jnp.sum(embed * embed, axis=1, keepdims=True) + NORM_EPS)
    unit = embed / norm
    unit_ref[...] = unit
    norm_ref[...] = spread(norm)
    logits = jnp.dot(unit.astype(BF16), proto[...], preferred_element_type=F32)
    exponents = jnp.exp(logits / SOFTMAX_TEMP)
    assign = jnp.exp(logits / SINK_EPS)
    exp_ref[...] = exponents
    assign = assign / jnp.sum(assign, axis=0, keepdims=True)
    assign_ref[...] = assign
    part = lax.dot_general(
        exponents.astype(BF16), proto[...], TRANSPOSED, preferred_element_type=F32
    )
    batch = part.shape[0]
    lines = pack(
        jnp.sum(assign, axis=1, keepdims=True), jnp.sum(exponents, axis=1, keepdims=True)
    )
    halves = part.shape[1] // LANES
    high = part.astype(BF16).astype(F32)
    low = part - high
    for i in range(message.shape[0]):
        if i < halves * batch:
            h, b = divmod(i, batch)
            here = slice(h * LANES, (h + 1) * LANES)
            piece = [high[b : b + 1, here], low[b : b + 1, here]]
        else:
            piece = [jnp.zeros((2, LANES), F32)]
        message[i] = jnp.concatenate([*piece, lines, side[i]], axis=0).astype(BF16)


def second_kernel(came, assign_ref, assign_out, message, total_ref):
    batch = assign_ref.shape[0]
    came = jnp.sum(came[...].astype(F32), axis=0)
    lines = came[2 : 2 + digit_rows(batch, 2)]
    total_ref[...] = spread(unpack(lines, batch, 1))
    assign = assign_ref[...] / unpack(lines, batch, 0)
    assign = assign / jnp.sum(assign, axis=0, keepdims=True)
    assign_out[...] = assign
    line = to_lanes(jnp.sum(assign, axis=1, keepdims=True))
    out = jnp.concatenate([came[0:1] + came[1:2], line], axis=0)
    for i in range(message.shape[0]):
        message[i] = out


def third_kernel(
    came, assign_ref, proto, assign_out, keep_ref, send_ref, digits_ref, grad_ref
):
    batch = assign_ref.shape[0]
    halves = proto.shape[0] // LANES
    total = jnp.sum(came[...], axis=0)[1:2]
    assign = assign_ref[...] / from_lanes(total, batch)
    assign = assign / jnp.sum(assign, axis=0, keepdims=True)
    assign_out[...] = assign
    part = lax.dot_general(
        assign.astype(BF16), proto[...], TRANSPOSED, preferred_element_type=F32
    )
    half = part.shape[1] // 2
    odd = lax.axis_index("cam") % 2 == 1
    low, high = part[:, :half], part[:, half:]
    keep_ref[...] = jnp.where(odd, high, low)
    send_ref[...] = jnp.where(odd, low, high)
    digits_ref[...] = pack(jnp.sum(assign, axis=1, keepdims=True))
    for h in range(halves):
        for b in range(batch):
            grad_ref[b : b + 1, h * LANES : (h + 1) * LANES] = came[h * batch + b][0:1]


def message_kernel(keep, got, digits, message):
    rows = jnp.concatenate([keep[...] + got[...], digits[...]], axis=0)
    width = message.shape[2] // LANES
    rows = [rows[i : i + 1] for i in range(rows.shape[0])]
    rows += [jnp.zeros((1, LANES), F32)] * (2 * width - len(rows))
    long = [jnp.concatenate(rows[i * width : (i + 1) * width], axis=1) for i in range(2)]
    out = jnp.concatenate(long, axis=0).astype(BF16)
    for i in range(message.shape[0]):
        message[i] = out


def output_kernel(
    protos,
    n_cam,
    block,
    came,
    came_side,
    unit_ref,
    norm_ref,
    exp_ref,
    assign_ref,
    total_ref,
    prob_grad,
    proto,
    scale,
    wp,
    codes_out,
    proto_grad_out,
    grad_proj_out,
    grad_value_out,
    codes,
    proto_grad,
    grad_proj,
    grad_value,
    sems,
):
    clips, ranks, n_clip = came.shape[:3]
    batch, columns = exp_ref.shape
    share = grad_proj.shape[0]
    cols = clips * wp.shape[0]
    copies = []

    def send(source, target):
        copies.append(pltpu.make_async_copy(source, target, sems.at[len(copies)]))
        copies[-1].start()

    sums = [jnp.zeros(came.shape[3:], F32) for _ in range(2)]
    for cam in range(n_cam):
        part = jnp.sum(came[cam // ranks, cam % ranks].astype(F32), axis=0)
        sums[cam % 2] = sums[cam % 2] + part
    long = came.shape[4] // LANES

    def short(x, start, stop):
        places = [divmod(i, long) for i in range(start, stop)]
        return jnp.concatenate(
            [x[r : r + 1, i * LANES : (i + 1) * LANES] for r, i in places], axis=0
        )

    lines = short(sums[0] + sums[1], batch, batch + digit_rows(batch, 1))
    by_assign = protos / unpack(lines, batch, 0)
    by_prob = protos / total_ref[:, :1]
    unit = unit_ref[...]
    unit_b = unit.astype(BF16)

    for start in range(0, columns, block):
        here = slice(start, start + block)
        assign = assign_ref[:, here] * by_assign
        grad_logits = (exp_ref[:, here] * by_prob - assign).astype(BF16)
        for g in range(clips):
            for p in range(n_clip):
                row, to = g * n_clip + p, p * clips + g
                codes[to : to + 1, here] = assign[row : row + 1]
        grad = lax.dot_general(unit_b, grad_logits, OUTER, preferred_element_type=F32)
        inverse = scale[:, here]
        unit_proto = proto[:, here].astype(F32) * inverse
        along = jnp.sum(unit_proto * grad, axis=0, keepdims=True)
        proto_grad[:, here] = (grad - unit_proto * along) * inverse
        send(proto_grad.at[:, here], proto_grad_out.at[:, here])
    send(codes, codes_out)

    assign_grad = jnp.concatenate([short(s, 0, batch) for s in sums], axis=1)
    grad_unit = prob_grad[...] * by_prob - assign_grad * by_assign
    grad_embed = (
        grad_unit - unit * jnp.sum(unit * grad_unit, axis=1, keepdims=True)
    ) / norm_ref[:, :1]
    grad_embed = grad_embed.astype(BF16)

    side = 2 + digit_rows(batch, 2)

    def rows(rank, row):
        picked = [came_side[g, rank].astype(F32)[:, row, :] for g in range(clips)]
        return jnp.concatenate(picked, axis=0)[:, :share].astype(BF16)

    grad_proj[...] = lax.dot_general(
        rows(lax.axis_index("clip") * share // cols, side), grad_embed, OUTER, preferred_element_type=F32
    )
    send(grad_proj, grad_proj_out)
    grad_pooled = lax.dot_general(
        grad_embed, wp[...], TRANSPOSED, preferred_element_type=F32
    ).astype(BF16)
    col_head = lax.broadcasted_iota(jnp.int32, grad_value.shape, 1) // HD
    value = jnp.zeros(grad_value.shape, F32)
    for head in range(grad_value.shape[1] // HD):
        mixed = rows(lax.axis_index("cam") // clips, side + 1 + head)
        out = lax.dot_general(mixed, grad_pooled, OUTER, preferred_element_type=F32)
        value = jnp.where(col_head == head, out, value)
    grad_value[...] = value
    send(grad_value, grad_value_out)
    for copy in copies:
        copy.wait()


def local(tokens, w_query, w_key, w_value, w_proj, prototypes):
    clips, _, tok, d = tokens.shape
    n_cam, n_clip = lax.axis_size("cam"), lax.axis_size("clip")
    devices = n_cam * n_clip
    ranks = n_cam // clips
    batch = clips * n_clip
    cols = d // ranks
    heads = cols // HD
    heads_here = heads // clips
    share = d // n_clip
    bottleneck, columns = prototypes.shape
    protos = columns * devices
    width = heads_here * HD

    with jax.named_scope("tokens_of_a_clip"):
        tokens = tokens.reshape(clips, tok, d)
        mine, half, rest = from_other_groups(tokens, n_cam)

    with jax.named_scope("prototypes"):
        scale, proto_b = call(
            prototype_kernel,
            [((1, columns), F32), ((bottleneck, columns), BF16)],
            [prototypes],
            4 * bottleneck * columns,
            mib=8,
        )

    with jax.named_scope("pooling"):
        def columns_of():
            start = lax.axis_index("cam") % ranks * cols
            return slice(None), pl.ds(pl.multiple_of(start, cols), cols)

        def rows_of():
            start = lax.axis_index("cam") % ranks * cols
            return pl.ds(pl.multiple_of(start, cols), cols), slice(None)

        def heads_of():
            start = lax.axis_index("cam") * width
            return pl.ds(pl.multiple_of(start, width), width), slice(None)

        *weights, wp, proj_rows = slices(
            [w_query, w_key, w_value, w_proj],
            [(i, columns_of) for i in range(3)] + [(3, rows_of), (3, heads_of)],
            [(d, cols)] * 3 + [(cols, bottleneck), (width, bottleneck)],
        )
        stages = [relay([(0, mine)], n_cam, ranks)]
        kept = kept_type(heads, n_cam * tok - (n_cam - ranks) * tok // 2)
        early = first_blocks([b for _, b in stages[0]], weights, kept)
        half = [(camera, after(b, proto_b, *early)) for camera, b in half]
        stages.append(relay(half, n_cam, ranks, 2))
        then = next_blocks([b for _, b in stages[1]], early, weights)
        rest = [(camera, after(b, *then)) for camera, b in rest]
        stages.append(relay(rest, n_cam, ranks))
        ready = project_blocks([b for _, b in rest], weights)
        late = [b for _, b in stages[2][len(rest) :]]
        key_weights, pooled, message = pool(early, then, ready, late, weights, wp, devices)

    with jax.named_scope("mixtures"):
        cameras, blocks, at = {}, [], 0
        for stage in stages:
            for camera, block in stage:
                cameras.setdefault(camera, []).append((len(blocks), at))
                blocks.append(block)
                at += block.shape[0]
        (side,) = call(
            functools.partial(mixture_kernel, list(cameras.values()), clips, n_clip),
            [((devices, 1 + heads_here, LANES), F32)],
            [key_weights, pooled, *blocks],
            2 * at * d * 32,
            mib=8,
        )

    with jax.named_scope("logits"):
        came = after(exchange(message), side)
        unit, norm, exponents, assign, message = call(
            functools.partial(logits_kernel, clips, ranks, n_clip),
            [
                ((batch, bottleneck), F32),
                ((batch, LANES), F32),
                ((batch, columns), F32),
                ((batch, columns), F32),
                ((devices, 2 + digit_rows(batch, 2) + side.shape[1], LANES), BF16),
            ],
            [came, proto_b, side],
            4 * batch * bottleneck * columns,
            2 * batch * columns,
        )

    with jax.named_scope("row_total_1"):
        came_side = came = exchange(message)
        assign, message, total = call(
            second_kernel,
            [((batch, columns), F32), ((devices, 2, LANES), F32), ((batch, LANES), F32)],
            [came, assign],
            8 * batch * columns,
        )

    with jax.named_scope("row_total_2"):
        came = exchange(message)
        assign, keep, send, digits, prob_grad = call(
            third_kernel,
            [
                ((batch, columns), F32),
                ((batch, bottleneck // 2), F32),
                ((batch, bottleneck // 2), F32),
                ((digit_rows(batch, 1), LANES), F32),
                ((batch, bottleneck), F32),
            ],
            [came, assign, proto_b],
            2 * batch * bottleneck * columns,
        )

    with jax.named_scope("row_total_3"):
        got = lax.ppermute(send, "cam", [(i, i ^ 1) for i in range(n_cam)])
        (message,) = call(
            message_kernel,
            [((devices, 2, -(-(batch + digits.shape[0]) // 2) * LANES), BF16)],
            [keep, got, digits],
            devices * batch * LANES,
        )
        came = exchange(after(message, proj_rows))

    with jax.named_scope("outputs"):
        block = min(columns, 512)
        ins = [
            came.reshape((clips, ranks, n_clip) + came.shape[1:]),
            came_side.reshape((clips, ranks, n_clip) + came_side.shape[1:]),
            unit,
            norm,
            exponents,
            assign,
            total,
            prob_grad,
            prototypes,
            scale,
            proj_rows,
        ]
        outs = [
            ((batch, columns), F32),
            ((bottleneck, columns), F32),
            ((share, bottleneck), F32),
            ((share, width), F32),
        ]
        return call(
            functools.partial(output_kernel, protos, n_cam, block),
            outs,
            ins,
            2 * batch * bottleneck * columns,
            scratch=[pltpu.VMEM(*o) for o in outs]
            + [pltpu.SemaphoreType.DMA((columns // block + 3,))],
            out_specs=[FAR] * len(outs),
            mib=8,
        )


def solution(mesh):
    in_specs = (P("clip", "cam", None, None), P(), P(), P(), P(), P(None, ALL))
    out_specs = (P(None, ALL), P(None, ALL), P("clip", None), P("clip", "cam"))
    return jax.shard_map(local, mesh=mesh, in_specs=in_specs, out_specs=out_specs, check_vma=False)
```

```python
import functools

import jax
import jax.numpy as jnp
from jax import lax
from jax.experimental import pallas as pl
from jax.experimental.pallas import tpu as pltpu
from jax.sharding import PartitionSpec as P

HD = 64
SINK_EPS = 0.05
SOFTMAX_TEMP = 0.1
NORM_EPS = 1e-06
LANES = 128
DIGITS = 3
ALL = ("cam", "clip")
F32 = jnp.float32
BF16 = jnp.bfloat16
TRANSPOSED = (((1,), (1,)), ((), ()))
OUTER = (((0,), (0,)), ((), ()))
WHOLE = pl.BlockSpec(memory_space=pltpu.VMEM)


def call(
    kernel, outs, ins, flops, extra=0, scratch=(), grid=None, out_specs=None, in_specs=None, mib=4
):
    moved = sum(a.size * a.dtype.itemsize for a in ins)
    return pl.pallas_call(
        kernel,
        out_shape=tuple(jax.ShapeDtypeStruct(*o) for o in outs),
        in_specs=in_specs or [WHOLE] * len(ins),
        out_specs=out_specs or [WHOLE] * len(outs),
        scratch_shapes=list(scratch),
        grid=grid or (),
        compiler_params=pltpu.CompilerParams(vmem_limit_bytes=mib * 2**20),
        cost_estimate=pl.CostEstimate(flops=1, bytes_accessed=1, transcendentals=0),
    )(*ins)


def project(x, wq, wk, wv):
    q = jnp.dot(x, wq, preferred_element_type=F32).astype(BF16) * BF16(HD**-0.5)
    kt = jnp.dot(x, wk, preferred_element_type=F32).astype(BF16).T
    v = jnp.dot(x, wv, preferred_element_type=F32).astype(BF16)
    return q, kt, v


def project_kernel(blocks, *refs):
    wq, wk, wv = refs[blocks : blocks + 3]
    q_ref, kt_ref, v_ref = refs[blocks + 3 :]
    x = jnp.concatenate([x_ref[...] for x_ref in refs[:blocks]], axis=0)
    q_ref[...], kt_ref[...], v_ref[...] = project(x, wq[...], wk[...], wv[...])


def project_blocks(blocks, weights):
    d, cols = weights[0].shape
    rows = sum(b.shape[0] for b in blocks)
    return call(
        functools.partial(project_kernel, len(blocks)),
        [((rows, cols), BF16), ((cols, rows), BF16), ((rows, cols), BF16)],
        [*blocks, *weights],
        2 * rows * d * cols * 3,
    )


def head_of(q, head, lane):
    tile, at = divmod(head * HD, LANES)
    here = slice(tile * LANES, (tile + 1) * LANES)
    return jnp.where(lane // HD == at // HD, q[:, here], BF16(0)), here


def scores(q_head, kt):
    e = jnp.exp(jnp.dot(q_head, kt, preferred_element_type=F32))
    return e, sum(e[:, i : i + LANES] for i in range(0, e.shape[1], LANES))


def first_kernel(blocks, *refs):
    ins, (q_ref, kt_ref, v_ref, exp_ref, sum_ref) = refs[: blocks + 3], refs[blocks + 3 :]
    project_kernel(blocks, *ins, q_ref, kt_ref, v_ref)
    rows, cols = q_ref.shape
    lane = lax.broadcasted_iota(jnp.int32, (rows, LANES), 1)
    sums = jnp.zeros((rows, LANES), F32)
    for head in range(cols // HD):
        q_head, here = head_of(q_ref, head, lane)
        e, part = scores(q_head, kt_ref[here, :])
        exp_ref[head * rows : (head + 1) * rows, :] = e.astype(exp_ref.dtype)
        sums = jnp.where(lane == head, jnp.sum(part, axis=1, keepdims=True), sums)
    sum_ref[...] = sums


def kept_type(heads, rows):
    return F32 if 4 * heads * rows * rows <= 20 * 2**20 else BF16


def first_blocks(blocks, weights, kept):
    d, cols = weights[0].shape
    rows = sum(b.shape[0] for b in blocks)
    heads = cols // HD
    return call(
        functools.partial(first_kernel, len(blocks)),
        [
            ((rows, cols), BF16),
            ((cols, rows), BF16),
            ((rows, cols), BF16),
            ((heads * rows, rows), kept),
            ((rows, LANES), F32),
        ],
        [*blocks, *weights],
        2 * rows * d * cols * 3,
        mib=4 + 8 * rows * rows // 2**20,
    )


def next_kernel(blocks, q_e, kt_e, sum_e, *refs):
    ins, outs = refs[: blocks + 3], refs[blocks + 3 :]
    q_n, kt_n, v_n, exp_n, exp_x, sum_n, sum_ref = outs
    project_kernel(blocks, *ins, q_n, kt_n, v_n)
    rows, cols = q_n.shape
    first = q_e.shape[0]
    lane_n = lax.broadcasted_iota(jnp.int32, (rows, LANES), 1)
    lane_e = lax.broadcasted_iota(jnp.int32, (first, LANES), 1)
    sums_n, sums_e = jnp.zeros((rows, LANES), F32), sum_e[...]
    for head in range(cols // HD):
        queries_n, here = head_of(q_n, head, lane_n)
        queries_e, _ = head_of(q_e, head, lane_e)
        a, part_a = scores(queries_n, kt_e[here, :])
        b, part_b = scores(queries_n, kt_n[here, :])
        x, part_x = scores(queries_e, kt_n[here, :])
        exp_n[head * rows : (head + 1) * rows, :first] = a.astype(exp_n.dtype)
        exp_n[head * rows : (head + 1) * rows, first:] = b.astype(exp_n.dtype)
        exp_x[head * first : (head + 1) * first, :] = x.astype(exp_x.dtype)
        part = jnp.sum(part_a + part_b, axis=1, keepdims=True)
        sums_n = jnp.where(lane_n == head, part, sums_n)
        part = jnp.sum(part_x, axis=1, keepdims=True)
        sums_e = sums_e + jnp.where(lane_e == head, part, 0.0)
    sum_n[...] = sums_n
    sum_ref[...] = sums_e


def next_blocks(blocks, early, weights):
    q_e, kt_e, _, _, sum_e = early
    d, cols = weights[0].shape
    first = q_e.shape[0]
    rows = sum(b.shape[0] for b in blocks)
    heads = cols // HD
    return call(
        functools.partial(next_kernel, len(blocks)),
        [
            ((rows, cols), BF16),
            ((cols, rows), BF16),
            ((rows, cols), BF16),
            ((heads * rows, first + rows), early[3].dtype),
            ((heads * first, rows), early[3].dtype),
            ((rows, LANES), F32),
            ((first, LANES), F32),
        ],
        [q_e, kt_e, sum_e, *blocks, *weights],
        2 * rows * d * cols * 3,
        mib=4 + 24 * first * rows // 2**20,
    )


def pool_kernel(late, *refs):
    (q_e, kt_e, v_e, exp_e), refs = refs[:4], refs[4:]
    (q_n, kt_n, v_n, exp_n, exp_x, sum_n, sum_e), refs = refs[:7], refs[7:]
    (q_a, kt_a, v_a), refs = refs[:3], refs[3:]
    x_refs, (wq, wk, wv, wp) = refs[:late], refs[late : 4 + late]
    weight_ref, pooled_ref, message, q_s, kt_s, v_s, w_s = refs[4 + late :]
    at = q_a.shape[0]
    q_s[:at], kt_s[:, :at], v_s[:at] = q_a[...], kt_a[...], v_a[...]
    for x_ref in x_refs:
        rows = slice(at, at + x_ref.shape[0])
        at += x_ref.shape[0]
        q_s[rows, :], kt_s[:, rows], v_s[rows, :] = project(x_ref[...], wq[...], wk[...], wv[...])
    heads, total = w_s.shape
    cols = heads * HD
    first, then, fresh = q_e.shape[0], q_n.shape[0], q_s.shape[0]
    bounds = [0, first, first + then, total]

    def lanes(rows):
        return lax.broadcasted_iota(jnp.int32, (rows, LANES), 1)

    @pl.loop(0, cols // LANES, unroll=2 if exp_e.dtype == F32 else 1)
    def _(tile):
        here = pl.ds(pl.multiple_of(tile * LANES, LANES), LANES)
        for e in range(LANES // HD):
            head = tile * (LANES // HD) + e

            def exps(q, kt):
                q_head = jnp.where(lanes(q.shape[0]) // HD == e, q[:, here], BF16(0))
                return jnp.exp(jnp.dot(q_head, kt[here, :], preferred_element_type=F32))

            def row_sum(a):
                return jnp.sum(a, axis=1, keepdims=True)

            def known(sums):
                return jnp.where(lanes(sums.shape[0]) == head, sums[...], 0.0)

            def lane_sums(a):
                return sum(a[:, i : i + LANES] for i in range(0, a.shape[1], LANES))

            def kept(a, rows, keys):
                return a[pl.ds(pl.multiple_of(head * rows, rows), rows), keys].astype(F32)

            new = [exps(q_s, kt) for kt in (kt_e, kt_n, kt_s)]
            e_s, n_s = exps(q_e, kt_s), exps(q_n, kt_s)
            by_s = 1.0 / row_sum(sum(lane_sums(a) for a in new))
            by_e = 1.0 / row_sum(known(sum_e) + lane_sums(e_s))
            by_n = 1.0 / row_sum(known(sum_n) + lane_sums(n_s))
            columns = [
                (new[0], kept(exp_e, first, slice(None)), kept(exp_n, then, slice(0, first))),
                (new[1], kept(exp_x, first, slice(None)), kept(exp_n, then, slice(first, None))),
                (new[2], e_s, n_s),
            ]
            for i, parts in enumerate(columns):
                w = sum(
                    jnp.sum(a * by, axis=0, keepdims=True)
                    for a, by in zip(parts, (by_s, by_e, by_n))
                )
                w_s[pl.ds(head, 1), bounds[i] : bounds[i + 1]] = w * (1.0 / total)

    weights = w_s[...].astype(BF16)
    weight_ref[...] = weights
    out = sum(
        jnp.dot(weights[:, bounds[i] : bounds[i + 1]], v[...], preferred_element_type=F32)
        for i, v in enumerate((v_e, v_n, v_s))
    )
    row_head = lax.broadcasted_iota(jnp.int32, out.shape, 0)
    col_head = lax.broadcasted_iota(jnp.int32, out.shape, 1) // HD
    pooled = jnp.sum(jnp.where(row_head == col_head, out, 0.0), axis=0, keepdims=True)
    pooled_ref[...] = pooled
    pooled_b = jnp.broadcast_to(pooled, (8, cols)).astype(BF16)
    embed = jnp.dot(pooled_b, wp[...], preferred_element_type=F32)[:1]
    embed = jnp.concatenate(
        [embed[:, i * LANES : (i + 1) * LANES] for i in range(message.shape[1])], axis=0
    )
    for i in range(message.shape[0]):
        message[i] = embed


def pool(early, after_early, ready, late, weights, wp, devices):
    d, cols = weights[0].shape
    heads = cols // HD
    first, then = early[0].shape[0], after_early[0].shape[0]
    fresh = ready[0].shape[0] + sum(b.shape[0] for b in late)
    total = first + then + fresh
    bottleneck = wp.shape[1]
    return call(
        functools.partial(pool_kernel, len(late)),
        [((heads, total), BF16), ((1, cols), F32), ((devices, bottleneck // LANES, LANES), F32)],
        [*early[:4], *after_early, *ready, *late, *weights, wp],
        2 * fresh * d * cols * 3 + 2 * total * total * cols * 4,
        heads * total * total,
        scratch=[
            pltpu.VMEM((fresh, cols), BF16),
            pltpu.VMEM((cols, fresh), BF16),
            pltpu.VMEM((fresh, cols), BF16),
            pltpu.VMEM((heads, total), F32),
        ],
        mib=6 + 40 * fresh * total // 2**20,
    )


def mixture_kernel(cameras, clips, n_clip, w_ref, pooled_ref, *refs):
    x_refs, side = refs[:-1], refs[-1]
    heads, d = w_ref.shape[0], x_refs[0].shape[1]
    heads_here, share = heads // clips, d // n_clip
    mix = jnp.zeros((heads, d), F32)
    for camera in cameras:
        m = jnp.zeros((heads, d), F32)
        for block, at in camera:
            w = w_ref[:, at : at + x_refs[block].shape[0]]
            m = m + jnp.dot(w, x_refs[block][...], preferred_element_type=F32)
        mix = mix + m.astype(BF16).astype(F32)

    def lanes(x, i):
        x = x[:, i * share : (i + 1) * share]
        if share == LANES:
            return x
        return jnp.concatenate([x, jnp.zeros((x.shape[0], LANES - share), F32)], axis=1)

    for i in range(side.shape[0]):
        j, p = divmod(i % (clips * n_clip), n_clip)
        side[i] = jnp.concatenate(
            [
                lanes(pooled_ref[...], i % (pooled_ref.shape[1] // share)),
                lanes(mix[j * heads_here : (j + 1) * heads_here], p),
            ],
            axis=0,
        )


FAR = pl.BlockSpec(memory_space=pltpu.HBM)


def slice_kernel(plan, *refs):
    ins = 1 + max(which for which, _ in plan)
    outs, sems = refs[ins:-1], refs[-1]
    copies = []
    for i, (which, where) in enumerate(plan):
        source = refs[which].at[where()]
        copies.append(pltpu.make_async_copy(source, outs[i], sems.at[i]))
        copies[-1].start()
    for copy in copies:
        copy.wait()


def slices(arrays, plan, shapes):
    return call(
        functools.partial(slice_kernel, plan),
        [(shape, BF16) for shape in shapes],
        [pltpu.with_memory_space_constraint(a, pltpu.HBM) for a in arrays],
        0,
        scratch=[pltpu.SemaphoreType.DMA((len(plan),))],
        in_specs=[FAR] * len(arrays),
    )


def after(x, *others):
    return lax.optimization_barrier((x, others))[0]


def token_block(s, clips, ranks, start, size):
    rows = pl.ds(start, size)
    return 0, lambda: ((lax.axis_index("cam") // ranks + s) % clips, rows, slice(None))


def from_other_groups(tokens, n_cam):
    clips, tok, d = tokens.shape
    ranks = n_cam // clips
    half = tok // 2
    pieces = [(s, c) for c in range(2) for s in range(1, clips)]
    mine, *sent = slices(
        [tokens],
        [token_block(0, clips, ranks, 0, tok)]
        + [token_block(s, clips, ranks, c * half, half) for s, c in pieces],
        [(tok, d)] + [(half, d)] * len(pieces),
    )
    held = [[], []]
    for (s, c), block in zip(pieces, sent):
        perm = [
            (i, ((i // ranks + s) % clips) * ranks + (i % ranks + c) % ranks) for i in range(n_cam)
        ]
        held[c].append((s * ranks + c % ranks, lax.ppermute(block, "cam", perm)))
    return mine, *held


def relay(blocks, n_cam, ranks, cuts=1):
    stage = list(blocks)
    size = blocks[0][1].shape[0] // cuts
    blocks = [(camera, b[i * size : (i + 1) * size]) for camera, b in blocks for i in range(cuts)]
    for t in range(1, ranks):
        perm = [(i, (i // ranks) * ranks + (i % ranks + t) % ranks) for i in range(n_cam)]
        for camera, b in blocks:
            label = camera // ranks * ranks + (camera + t) % ranks
            stage.append((label, lax.ppermute(b, "cam", perm)))
    return stage


def prototype_kernel(proto, scale, proto_b):
    proto_f = proto[...].astype(F32)
    norm = jnp.sqrt(jnp.sum(proto_f * proto_f, axis=0, keepdims=True) + NORM_EPS)
    scale[...] = 1.0 / norm
    proto_b[...] = (proto_f / norm).astype(BF16)


def to_lanes(column, offset=0):
    shape = (column.shape[0], LANES)
    row = lax.broadcasted_iota(jnp.int32, shape, 0) + offset
    lane = lax.broadcasted_iota(jnp.int32, shape, 1)
    return jnp.sum(jnp.where(lane == row, column, 0.0), axis=0, keepdims=True)


def from_lanes(line, size, offset=0):
    row = lax.broadcasted_iota(jnp.int32, (size, LANES), 0) + offset
    lane = lax.broadcasted_iota(jnp.int32, (size, LANES), 1)
    return jnp.sum(jnp.where(lane == row, line, 0.0), axis=1, keepdims=True)


def digit_rows(batch, columns):
    return -(-columns * DIGITS // (LANES // batch))


def pack(*columns):
    batch = columns[0].shape[0]
    slots = LANES // batch
    lines = [jnp.zeros((1, LANES), F32)] * digit_rows(batch, len(columns))
    for i, rest in enumerate(columns):
        for slot in range(i * DIGITS, (i + 1) * DIGITS):
            digit = rest.astype(BF16).astype(F32)
            rest = rest - digit
            row, at = divmod(slot, slots)
            lines[row] = lines[row] + to_lanes(digit, at * batch)
    return jnp.concatenate(lines, axis=0)


def unpack(lines, batch, i):
    slots = LANES // batch
    column = jnp.zeros((batch, 1), F32)
    for slot in range(i * DIGITS, (i + 1) * DIGITS):
        row, at = divmod(slot, slots)
        column = column + from_lanes(lines[row : row + 1], batch, at * batch)
    return column


def spread(column):
    return jnp.broadcast_to(column, (column.shape[0], LANES))


def exchange(message):
    return lax.all_to_all(message, ALL, split_axis=0, concat_axis=0, tiled=True)


def logits_kernel(
    clips, ranks, n_clip, came, proto, side, unit_ref, norm_ref, exp_ref, assign_ref, message
):
    rows = []
    for g in range(clips):
        for p in range(n_clip):
            z = sum(came[(g * ranks + r) * n_clip + p] for r in range(ranks))
            rows.append(jnp.concatenate([z[i : i + 1] for i in range(z.shape[0])], axis=1))
    embed = jnp.concatenate(rows, axis=0)
    norm = jnp.sqrt(jnp.sum(embed * embed, axis=1, keepdims=True) + NORM_EPS)
    unit = embed / norm
    unit_ref[...] = unit
    norm_ref[...] = spread(norm)
    logits = jnp.dot(unit.astype(BF16), proto[...], preferred_element_type=F32)
    exponents = jnp.exp(logits / SOFTMAX_TEMP)
    assign = jnp.exp(logits / SINK_EPS)
    exp_ref[...] = exponents
    assign = assign / jnp.sum(assign, axis=0, keepdims=True)
    assign_ref[...] = assign
    part = lax.dot_general(
        exponents.astype(BF16), proto[...], TRANSPOSED, preferred_element_type=F32
    )
    batch = part.shape[0]
    lines = pack(
        jnp.sum(assign, axis=1, keepdims=True), jnp.sum(exponents, axis=1, keepdims=True)
    )
    halves = part.shape[1] // LANES
    high = part.astype(BF16).astype(F32)
    low = part - high
    for i in range(message.shape[0]):
        if i < halves * batch:
            h, b = divmod(i, batch)
            here = slice(h * LANES, (h + 1) * LANES)
            piece = [high[b : b + 1, here], low[b : b + 1, here]]
        else:
            piece = [jnp.zeros((2, LANES), F32)]
        message[i] = jnp.concatenate([*piece, lines, side[i]], axis=0).astype(BF16)


def second_kernel(came, assign_ref, assign_out, message, total_ref):
    batch = assign_ref.shape[0]
    came = jnp.sum(came[...].astype(F32), axis=0)
    lines = came[2 : 2 + digit_rows(batch, 2)]
    total_ref[...] = spread(unpack(lines, batch, 1))
    assign = assign_ref[...] / unpack(lines, batch, 0)
    assign = assign / jnp.sum(assign, axis=0, keepdims=True)
    assign_out[...] = assign
    line = to_lanes(jnp.sum(assign, axis=1, keepdims=True))
    out = jnp.concatenate([came[0:1] + came[1:2], line], axis=0)
    for i in range(message.shape[0]):
        message[i] = out


def third_kernel(
    came, assign_ref, proto, assign_out, keep_ref, send_ref, digits_ref, grad_ref
):
    batch = assign_ref.shape[0]
    halves = proto.shape[0] // LANES
    total = jnp.sum(came[...], axis=0)[1:2]
    assign = assign_ref[...] / from_lanes(total, batch)
    assign = assign / jnp.sum(assign, axis=0, keepdims=True)
    assign_out[...] = assign
    part = lax.dot_general(
        assign.astype(BF16), proto[...], TRANSPOSED, preferred_element_type=F32
    )
    half = part.shape[1] // 2
    odd = lax.axis_index("cam") % 2 == 1
    low, high = part[:, :half], part[:, half:]
    keep_ref[...] = jnp.where(odd, high, low)
    send_ref[...] = jnp.where(odd, low, high)
    digits_ref[...] = pack(jnp.sum(assign, axis=1, keepdims=True))
    for h in range(halves):
        for b in range(batch):
            grad_ref[b : b + 1, h * LANES : (h + 1) * LANES] = came[h * batch + b][0:1]


def message_kernel(keep, got, digits, message):
    rows = jnp.concatenate([keep[...] + got[...], digits[...]], axis=0)
    width = message.shape[2] // LANES
    rows = [rows[i : i + 1] for i in range(rows.shape[0])]
    rows += [jnp.zeros((1, LANES), F32)] * (2 * width - len(rows))
    long = [jnp.concatenate(rows[i * width : (i + 1) * width], axis=1) for i in range(2)]
    out = jnp.concatenate(long, axis=0).astype(BF16)
    for i in range(message.shape[0]):
        message[i] = out


def output_kernel(
    protos,
    n_cam,
    block,
    came,
    came_side,
    unit_ref,
    norm_ref,
    exp_ref,
    assign_ref,
    total_ref,
    prob_grad,
    proto,
    scale,
    wp,
    codes_out,
    proto_grad_out,
    grad_proj_out,
    grad_value_out,
    codes,
    proto_grad,
    grad_proj,
    grad_value,
    sems,
):
    clips, ranks, n_clip = came.shape[:3]
    batch, columns = exp_ref.shape
    share = grad_proj.shape[0]
    cols = clips * wp.shape[0]
    copies = []

    def send(source, target):
        copies.append(pltpu.make_async_copy(source, target, sems.at[len(copies)]))
        copies[-1].start()

    sums = [jnp.zeros(came.shape[3:], F32) for _ in range(2)]
    for cam in range(n_cam):
        part = jnp.sum(came[cam // ranks, cam % ranks].astype(F32), axis=0)
        sums[cam % 2] = sums[cam % 2] + part
    long = came.shape[4] // LANES

    def short(x, start, stop):
        places = [divmod(i, long) for i in range(start, stop)]
        return jnp.concatenate(
            [x[r : r + 1, i * LANES : (i + 1) * LANES] for r, i in places], axis=0
        )

    lines = short(sums[0] + sums[1], batch, batch + digit_rows(batch, 1))
    by_assign = protos / unpack(lines, batch, 0)
    by_prob = protos / total_ref[:, :1]
    unit = unit_ref[...]
    unit_b = unit.astype(BF16)

    for start in range(0, columns, block):
        here = slice(start, start + block)
        assign = assign_ref[:, here] * by_assign
        grad_logits = (exp_ref[:, here] * by_prob - assign).astype(BF16)
        for g in range(clips):
            for p in range(n_clip):
                row, to = g * n_clip + p, p * clips + g
                codes[to : to + 1, here] = assign[row : row + 1]
        grad = lax.dot_general(unit_b, grad_logits, OUTER, preferred_element_type=F32)
        inverse = scale[:, here]
        unit_proto = proto[:, here].astype(F32) * inverse
        along = jnp.sum(unit_proto * grad, axis=0, keepdims=True)
        proto_grad[:, here] = (grad - unit_proto * along) * inverse
        send(proto_grad.at[:, here], proto_grad_out.at[:, here])
    send(codes, codes_out)

    assign_grad = jnp.concatenate([short(s, 0, batch) for s in sums], axis=1)
    grad_unit = prob_grad[...] * by_prob - assign_grad * by_assign
    grad_embed = (
        grad_unit - unit * jnp.sum(unit * grad_unit, axis=1, keepdims=True)
    ) / norm_ref[:, :1]
    grad_embed = grad_embed.astype(BF16)

    side = 2 + digit_rows(batch, 2)

    def rows(rank, row):
        picked = [came_side[g, rank].astype(F32)[:, row, :] for g in range(clips)]
        return jnp.concatenate(picked, axis=0)[:, :share].astype(BF16)

    grad_proj[...] = lax.dot_general(
        rows(lax.axis_index("clip") * share // cols, side), grad_embed, OUTER, preferred_element_type=F32
    )
    send(grad_proj, grad_proj_out)
    grad_pooled = lax.dot_general(
        grad_embed, wp[...], TRANSPOSED, preferred_element_type=F32
    ).astype(BF16)
    col_head = lax.broadcasted_iota(jnp.int32, grad_value.shape, 1) // HD
    value = jnp.zeros(grad_value.shape, F32)
    for head in range(grad_value.shape[1] // HD):
        mixed = rows(lax.axis_index("cam") // clips, side + 1 + head)
        out = lax.dot_general(mixed, grad_pooled, OUTER, preferred_element_type=F32)
        value = jnp.where(col_head == head, out, value)
    grad_value[...] = value
    send(grad_value, grad_value_out)
    for copy in copies:
        copy.wait()


def local(tokens, w_query, w_key, w_value, w_proj, prototypes):
    clips, _, tok, d = tokens.shape
    n_cam, n_clip = lax.axis_size("cam"), lax.axis_size("clip")
    devices = n_cam * n_clip
    ranks = n_cam // clips
    batch = clips * n_clip
    cols = d // ranks
    heads = cols // HD
    heads_here = heads // clips
    share = d // n_clip
    bottleneck, columns = prototypes.shape
    protos = columns * devices
    width = heads_here * HD

    with jax.named_scope("tokens_of_a_clip"):
        tokens = tokens.reshape(clips, tok, d)
        mine, half, rest = from_other_groups(tokens, n_cam)

    with jax.named_scope("prototypes"):
        scale, proto_b = call(
            prototype_kernel,
            [((1, columns), F32), ((bottleneck, columns), BF16)],
            [prototypes],
            4 * bottleneck * columns,
            mib=8,
        )

    with jax.named_scope("pooling"):
        def columns_of():
            start = lax.axis_index("cam") % ranks * cols
            return slice(None), pl.ds(pl.multiple_of(start, cols), cols)

        def rows_of():
            start = lax.axis_index("cam") % ranks * cols
            return pl.ds(pl.multiple_of(start, cols), cols), slice(None)

        def heads_of():
            start = lax.axis_index("cam") * width
            return pl.ds(pl.multiple_of(start, width), width), slice(None)

        *weights, wp, proj_rows = slices(
            [w_query, w_key, w_value, w_proj],
            [(i, columns_of) for i in range(3)] + [(3, rows_of), (3, heads_of)],
            [(d, cols)] * 3 + [(cols, bottleneck), (width, bottleneck)],
        )
        stages = [relay([(0, mine)], n_cam, ranks)]
        kept = kept_type(heads, n_cam * tok - (n_cam - ranks) * tok // 2)
        early = first_blocks([b for _, b in stages[0]], weights, kept)
        half = [(camera, after(b, proto_b, *early)) for camera, b in half]
        stages.append(relay(half, n_cam, ranks, 2))
        then = next_blocks([b for _, b in stages[1]], early, weights)
        rest = [(camera, after(b, *then)) for camera, b in rest]
        stages.append(relay(rest, n_cam, ranks))
        ready = project_blocks([b for _, b in rest], weights)
        late = [b for _, b in stages[2][len(rest) :]]
        key_weights, pooled, message = pool(early, then, ready, late, weights, wp, devices)

    with jax.named_scope("mixtures"):
        cameras, blocks, at = {}, [], 0
        for stage in stages:
            for camera, block in stage:
                cameras.setdefault(camera, []).append((len(blocks), at))
                blocks.append(block)
                at += block.shape[0]
        (side,) = call(
            functools.partial(mixture_kernel, list(cameras.values()), clips, n_clip),
            [((devices, 1 + heads_here, LANES), F32)],
            [key_weights, pooled, *blocks],
            2 * at * d * 32,
            mib=8,
        )

    with jax.named_scope("logits"):
        came = after(exchange(message), side)
        unit, norm, exponents, assign, message = call(
            functools.partial(logits_kernel, clips, ranks, n_clip),
            [
                ((batch, bottleneck), F32),
                ((batch, LANES), F32),
                ((batch, columns), F32),
                ((batch, columns), F32),
                ((devices, 2 + digit_rows(batch, 2) + side.shape[1], LANES), BF16),
            ],
            [came, proto_b, side],
            4 * batch * bottleneck * columns,
            2 * batch * columns,
        )

    with jax.named_scope("row_total_1"):
        came_side = came = exchange(message)
        assign, message, total = call(
            second_kernel,
            [((batch, columns), F32), ((devices, 2, LANES), F32), ((batch, LANES), F32)],
            [came, assign],
            8 * batch * columns,
        )

    with jax.named_scope("row_total_2"):
        came = exchange(message)
        assign, keep, send, digits, prob_grad = call(
            third_kernel,
            [
                ((batch, columns), F32),
                ((batch, bottleneck // 2), F32),
                ((batch, bottleneck // 2), F32),
                ((digit_rows(batch, 1), LANES), F32),
                ((batch, bottleneck), F32),
            ],
            [came, assign, proto_b],
            2 * batch * bottleneck * columns,
        )

    with jax.named_scope("row_total_3"):
        got = lax.ppermute(send, "cam", [(i, i ^ 1) for i in range(n_cam)])
        (message,) = call(
            message_kernel,
            [((devices, 2, -(-(batch + digits.shape[0]) // 2) * LANES), BF16)],
            [keep, got, digits],
            devices * batch * LANES,
        )
        came = exchange(after(message, proj_rows))

    with jax.named_scope("outputs"):
        block = min(columns, 256)
        ins = [
            came.reshape((clips, ranks, n_clip) + came.shape[1:]),
            came_side.reshape((clips, ranks, n_clip) + came_side.shape[1:]),
            unit,
            norm,
            exponents,
            assign,
            total,
            prob_grad,
            prototypes,
            scale,
            proj_rows,
        ]
        outs = [
            ((batch, columns), F32),
            ((bottleneck, columns), F32),
            ((share, bottleneck), F32),
            ((share, width), F32),
        ]
        return call(
            functools.partial(output_kernel, protos, n_cam, block),
            outs,
            ins,
            2 * batch * bottleneck * columns,
            scratch=[pltpu.VMEM(*o) for o in outs]
            + [pltpu.SemaphoreType.DMA((columns // block + 3,))],
            out_specs=[FAR] * len(outs),
            mib=8,
        )


def solution(mesh):
    in_specs = (P("clip", "cam", None, None), P(), P(), P(), P(), P(None, ALL))
    out_specs = (P(None, ALL), P(None, ALL), P("clip", None), P("clip", "cam"))
    return jax.shard_map(local, mesh=mesh, in_specs=in_specs, out_specs=out_specs, check_vma=False)
```
